32 devices in a mesh: dp: 2 (over core), dom: 16 (over z, y, x).
Axes of the slice: x: 2, y: 2, z: 4, core: 2. Of those that a mesh axis runs over, the one named last changes fastest.
Arguments:
- density: bfloat16 [2, 64, 128, 256], P('dp', None, 'dom'), may hold values from -6 to 6
- upstream: bfloat16 [2, 64, 128, 256], P('dp', None, 'dom'), may hold values from -6 to 6
- spectral_weight: float32 [2048, 64], P(('dp', 'dom')), may hold values from -0.5 to 0.5
- moment_one: float32 [2048, 64], P(('dp', 'dom')), may hold values from -64 to 64
- moment_two: float32 [2048, 64], P(('dp', 'dom')), may hold values from 64 to 1024
- skip_weight: bfloat16 [64, 64], replicated, may hold values from -0.75 to 0.75
- skip_bias: float32 [64], replicated, may hold values from -3 to 3
- mode_counts: int32 [2], replicated, may hold values from 8 to 16, as said below
Outputs:
- input_grad: bfloat16 [2, 64, 128, 256], P('dp', None, 'dom')
- new_weight: float32 [2048, 64], P(('dp', 'dom'))
- new_moment_one: float32 [2048, 64], P(('dp', 'dom'))
- new_moment_two: float32 [2048, 64], P(('dp', 'dom'))
The draws below stay inside these ranges and needn't reach their ends.
Inputs may be any that keep to these rules, and one draw needn't show every extreme that they name: `mode_counts`: some entry equals 16.
All inputs are finite; a program needn't handle non-finite values.
Results may differ from the reference program's by a relative error of at most 0.0053.
Values may be sent and summed in bfloat16 or wider, within the bound.
A program may use at most 64 MiB of HBM per device.

```python
import math
import jax
import jax.numpy as jnp
from jax import lax

C = 64
MODES = 16
LINES = 256
STEP = 10
SAMPLES = 2
NX = 128


def draw_mode_counts(key, part):
    first_key, second_key = jax.random.split(jax.random.fold_in(key, 17))
    counts = jax.random.randint(first_key, (SAMPLES,), MODES // 2, MODES + 1, dtype=jnp.int32)
    chosen = jax.random.randint(second_key, (), 0, SAMPLES, dtype=jnp.int32)
    return jnp.where(jnp.arange(SAMPLES, dtype=jnp.int32) == chosen, MODES, counts).astype(jnp.int32)


def block_levels(rng, extent, shards, least, top_value):
    loudness = 1.0
    for dim, shards_of in shards:
        steps = jax.random.uniform(jax.random.fold_in(jax.random.fold_in(rng, 6), dim), (shards_of,), jnp.float32, least / len(shards), top_value / len(shards))
        loudness = loudness * jnp.repeat(jnp.exp(steps), extent[dim] // shards_of).reshape((-1,) + (1,) * (len(extent) - 1 - dim))
    return loudness


def bell_draw(own_key, dims, spread, limit, shards=(), kind=jnp.bfloat16):
    factor_of = block_levels(own_key, dims, shards, -0.22, 0.18) if shards else 1.0
    drawn = jax.random.normal(own_key, dims, jnp.float32) * spread * factor_of
    return jnp.minimum(jnp.maximum(drawn, -limit), limit).astype(kind)


def setup_inputs(seed: int = 0) -> dict:
    key_list = jax.random.split(jax.random.key(seed), 9)
    density = bell_draw(key_list[0], (SAMPLES, C, NX, LINES), 1.0, 6.0, ((0, 2), (2, 16)))
    upstream = bell_draw(key_list[1], (SAMPLES, C, NX, LINES), 1.0, 6.0, ((0, 2), (2, 16)))
    spectral_weight = bell_draw(key_list[2], (2 * MODES * C, C), (2 * C) ** -0.5, 0.5, ((0, 32),), jnp.float32)
    moment_one = bell_draw(key_list[3], (2 * MODES * C, C), (0.5 * (SAMPLES * LINES) ** 0.5), 64.0, ((0, 32),), jnp.float32)
    moment_two = jnp.clip(jnp.exp(math.log(1024.0) - 2.7725887 * jax.random.uniform(key_list[4], (2 * MODES * C, C), jnp.float32) ** block_levels(key_list[4], (2 * MODES * C, C), ((0, 32),), -0.2, 0.2)), 64.0, 1024.0)
    skip_weight = bell_draw(key_list[5], (C, C), C ** -0.5, 0.75)
    skip_bias = bell_draw(key_list[6], (C,), 0.5, 3.0, (), jnp.float32)
    mode_counts = draw_mode_counts(jax.random.fold_in(key_list[8], 71), 0)
    return {"density": density, "upstream": upstream, "spectral_weight": spectral_weight, "moment_one": moment_one, "moment_two": moment_two, "skip_weight": skip_weight, "skip_bias": skip_bias, "mode_counts": mode_counts}


learn_rate = 0.01
beta_first = 0.9
beta_second = 0.95
decay_rate = 0.1
epsilon = 1e-08

def upcast(values):
    return values.astype(jnp.float32)

def axis_parts(count_xdim):
    freq_list = jnp.arange(MODES, dtype=jnp.int32)
    cell_list = jnp.arange(count_xdim, dtype=jnp.int32)
    phases = jnp.mod(freq_list[:, None] * cell_list[None, :], count_xdim).astype(jnp.float32) / count_xdim
    angles = 2.0 * math.pi * phases
    scaling = 1.0 / math.sqrt(count_xdim)
    return ((jnp.cos(angles) * scaling).astype(jnp.bfloat16), (jnp.sin(angles) * scaling).astype(jnp.bfloat16))

def doubling_table():
    return jnp.where(jnp.arange(MODES, dtype=jnp.int32) > 0, 2.0, 1.0).astype(jnp.float32)

def gelu_slope(values):
    cumulative = 0.5 * (1.0 + lax.erf(values * 0.7071067811865476))
    bell_curve = jnp.exp(-0.5 * values * values) * 0.3989422804014327
    return cumulative + values * bell_curve

def reference(density, upstream, spectral_weight, moment_one, moment_two, skip_weight, skip_bias, mode_counts):
    cosines, sines = axis_parts(NX)
    cos_wide = upcast(cosines)
    sin_wide = upcast(sines)
    doubling = doubling_table()
    keep_modes = (jnp.arange(MODES, dtype=jnp.int32)[None, :] < mode_counts[:, None]).astype(jnp.float32)
    weight_low = spectral_weight.astype(jnp.bfloat16).reshape(2, MODES, C, C)
    weight_real = upcast(weight_low[0])
    weight_imag = upcast(weight_low[1])
    skip_wide = upcast(skip_weight)

    def one_sample(grad_sum, inputs):
        sample, cotangent, keep = inputs
        values = upcast(sample)
        spec_real = upcast(jnp.einsum('cxl,fx->lcf', values, cos_wide).astype(jnp.bfloat16))
        spec_imag = upcast((-jnp.einsum('cxl,fx->lcf', values, sin_wide)).astype(jnp.bfloat16))
        form = 'lcf,fco->lof'
        mixed_real = (jnp.einsum(form, spec_real, weight_real) - jnp.einsum(form, spec_imag, weight_imag)) * keep
        mixed_imag = (jnp.einsum(form, spec_imag, weight_real) + jnp.einsum(form, spec_real, weight_imag)) * keep
        mixed_real = upcast(mixed_real.astype(jnp.bfloat16)) * doubling
        mixed_imag = upcast(mixed_imag.astype(jnp.bfloat16)) * doubling
        back_rows = jnp.einsum('lof,fx->oxl', mixed_real, cos_wide) - jnp.einsum('lof,fx->oxl', mixed_imag, sin_wide)
        back_rows = lax.optimization_barrier(back_rows.astype(jnp.bfloat16))
        skip_part = jnp.einsum('oc,cxl->oxl', skip_wide, values)
        before = upcast(back_rows) + skip_part + skip_bias[:, None, None]
        gate_grad = (upcast(cotangent) * gelu_slope(before)).astype(jnp.bfloat16)
        gate_wide = upcast(gate_grad)
        scale = keep * doubling
        grad_real = upcast((jnp.einsum('oxl,fx->lof', gate_wide, cos_wide) * scale).astype(jnp.bfloat16))
        grad_imag = upcast((-jnp.einsum('oxl,fx->lof', gate_wide, sin_wide) * scale).astype(jnp.bfloat16))
        outer = 'lof,lcf->fco'
        part_real = jnp.einsum(outer, grad_real, spec_real) + jnp.einsum(outer, grad_imag, spec_imag)
        part_imag = jnp.einsum(outer, grad_imag, spec_real) - jnp.einsum(outer, grad_real, spec_imag)
        grad_sum = grad_sum + jnp.stack([part_real, part_imag], 0)
        inner = 'fco,lof->lcf'
        input_real = jnp.einsum(inner, weight_real, grad_real) + jnp.einsum(inner, weight_imag, grad_imag)
        input_imag = jnp.einsum(inner, weight_real, grad_imag) - jnp.einsum(inner, weight_imag, grad_real)
        input_real = upcast(input_real.astype(jnp.bfloat16))
        input_imag = upcast(input_imag.astype(jnp.bfloat16))
        input_rows = jnp.einsum('lcf,fx->cxl', input_real, cos_wide) - jnp.einsum('lcf,fx->cxl', input_imag, sin_wide)
        input_rows = lax.optimization_barrier(input_rows.astype(jnp.bfloat16))
        skip_back = jnp.einsum('oc,oxl->cxl', skip_wide, gate_wide)
        return (grad_sum, (upcast(input_rows) + skip_back).astype(jnp.bfloat16))
    start_sum = jnp.zeros((2, MODES, C, C), jnp.float32)
    grad_whole, input_grad = lax.scan(one_sample, start_sum, (density, upstream, keep_modes))
    weight_grad = grad_whole.reshape(2 * MODES * C, C)
    new_moment_one = beta_first * moment_one + (1.0 - beta_first) * weight_grad
    new_moment_two = beta_second * moment_two + (1.0 - beta_second) * weight_grad * weight_grad
    first_hat = new_moment_one / (1.0 - beta_first ** STEP)
    second_hat = new_moment_two / (1.0 - beta_second ** STEP)
    new_weight = spectral_weight - learn_rate * (first_hat / (jnp.sqrt(second_hat) + epsilon) + decay_rate * spectral_weight)
    return (input_grad, new_weight, new_moment_one, new_moment_two)
```

```python
import functools
import math

import jax
import jax.numpy as jnp
import numpy as np
from jax import lax
from jax.experimental import pallas as pl
from jax.experimental.pallas import tpu as pltpu
from jax.sharding import PartitionSpec as P

MODES = 16
STEP = 10


learn_rate = 0.01
beta_first = 0.9
beta_second = 0.95
decay_rate = 0.1
epsilon = 1e-08


def axis_parts(count_xdim):
    freq_list = jnp.arange(MODES, dtype=jnp.int32)
    cell_list = jnp.arange(count_xdim, dtype=jnp.int32)
    phases = (
        jnp.mod(freq_list[:, None] * cell_list[None, :], count_xdim).astype(jnp.float32)
        / count_xdim
    )
    angles = 2.0 * math.pi * phases
    scaling = 1.0 / math.sqrt(count_xdim)
    return (
        (jnp.cos(angles) * scaling).astype(jnp.bfloat16),
        (jnp.sin(angles) * scaling).astype(jnp.bfloat16),
    )


def doubling_table():
    return jnp.where(jnp.arange(MODES, dtype=jnp.int32) > 0, 2.0, 1.0).astype(jnp.float32)


def gelu_slope(values):
    cumulative = 0.5 * (1.0 + lax.erf(values * 0.7071067811865476))
    bell_curve = jnp.exp(-0.5 * values * values) * 0.3989422804014327
    return cumulative + values * bell_curve


def send_pencils(field):
    return lax.all_to_all(field, "dom", split_axis=3, concat_axis=2, tiled=True)


def send_slabs(field):
    return lax.all_to_all(field, "dom", split_axis=2, concat_axis=3, tiled=True)


def forward_parts(field, cosines, sines):
    real_part = jnp.einsum("scxl,fx->slcf", field, cosines, preferred_element_type=jnp.float32)
    imag_part = -jnp.einsum("scxl,fx->slcf", field, sines, preferred_element_type=jnp.float32)
    return (real_part, imag_part)


def inverse_cells(values_real, values_imag, cosines, sines):
    first = jnp.einsum("slcf,fx->scxl", values_real, cosines, preferred_element_type=jnp.float32)
    second = jnp.einsum("slcf,fx->scxl", values_imag, sines, preferred_element_type=jnp.float32)
    return (first - second).astype(jnp.bfloat16)


def on_device(
    density, upstream, spectral_weight, moment_one, moment_two, skip_weight, skip_bias, mode_counts
):
    samples, channels, slab_rows, line_count = density.shape
    count_xdim = slab_rows * lax.axis_size("dom")
    cosines, sines = axis_parts(count_xdim)
    doubling = doubling_table()
    doubling_low = doubling.astype(jnp.bfloat16)
    counts_here = lax.dynamic_slice_in_dim(mode_counts, lax.axis_index("dp") * samples, samples, 0)
    keep_modes = (jnp.arange(MODES, dtype=jnp.int32)[None, :] < counts_here[:, None]).astype(
        jnp.float32
    )
    keep_wide = keep_modes[:, None, None, :]
    weight_short = spectral_weight.astype(jnp.bfloat16)
    group_low = lax.all_gather(weight_short, "dom", axis=0, tiled=True)
    weight_low = lax.all_gather(group_low, "dp", axis=0, tiled=True)
    weight_low = weight_low.reshape(2, MODES, channels, channels)
    weight_real = weight_low[0]
    weight_imag = weight_low[1]
    density_lines = send_pencils(density)
    real_part, imag_part = forward_parts(density_lines, cosines, sines)
    spec_real = real_part.astype(jnp.bfloat16)
    spec_imag = imag_part.astype(jnp.bfloat16)
    form = "slcf,fco->slof"
    mixed_real = jnp.einsum(
        form, spec_real, weight_real, preferred_element_type=jnp.float32
    ) - jnp.einsum(form, spec_imag, weight_imag, preferred_element_type=jnp.float32)
    mixed_imag = jnp.einsum(
        form, spec_imag, weight_real, preferred_element_type=jnp.float32
    ) + jnp.einsum(form, spec_real, weight_imag, preferred_element_type=jnp.float32)
    mixed_real = (mixed_real * keep_wide).astype(jnp.bfloat16) * doubling_low
    mixed_imag = (mixed_imag * keep_wide).astype(jnp.bfloat16) * doubling_low
    back_lines = inverse_cells(mixed_real, mixed_imag, cosines, sines)
    back_rows = send_slabs(back_lines)
    skip_part = jnp.einsum(
        "oc,scxl->soxl", skip_weight, density, preferred_element_type=jnp.float32
    )
    before = back_rows.astype(jnp.float32) + skip_part + skip_bias[None, :, None, None]
    gate_grad = (upstream.astype(jnp.float32) * gelu_slope(before)).astype(jnp.bfloat16)
    gate_lines = send_pencils(gate_grad)
    grad_real, grad_imag = forward_parts(gate_lines, cosines, sines)
    scale = keep_wide * doubling
    grad_real = (grad_real * scale).astype(jnp.bfloat16)
    grad_imag = (grad_imag * scale).astype(jnp.bfloat16)
    outer = "slof,slcf->fco"
    part_real = jnp.einsum(
        outer, grad_real, spec_real, preferred_element_type=jnp.float32
    ) + jnp.einsum(outer, grad_imag, spec_imag, preferred_element_type=jnp.float32)
    part_imag = jnp.einsum(
        outer, grad_imag, spec_real, preferred_element_type=jnp.float32
    ) - jnp.einsum(outer, grad_real, spec_imag, preferred_element_type=jnp.float32)
    grad_local = jnp.stack([part_real, part_imag], 0).reshape(2 * MODES * channels, channels)
    group_grad = lax.psum_scatter(
        grad_local.astype(jnp.bfloat16), "dp", scatter_dimension=0, tiled=True
    ).astype(jnp.float32)
    weight_grad = lax.psum_scatter(group_grad, "dom", scatter_dimension=0, tiled=True)
    inner = "fco,slof->slcf"
    input_real = jnp.einsum(
        inner, weight_real, grad_real, preferred_element_type=jnp.float32
    ) + jnp.einsum(inner, weight_imag, grad_imag, preferred_element_type=jnp.float32)
    input_imag = jnp.einsum(
        inner, weight_real, grad_imag, preferred_element_type=jnp.float32
    ) - jnp.einsum(inner, weight_imag, grad_real, preferred_element_type=jnp.float32)
    input_lines = inverse_cells(
        input_real.astype(jnp.bfloat16), input_imag.astype(jnp.bfloat16), cosines, sines
    )
    input_rows = send_slabs(input_lines)
    skip_back = jnp.einsum(
        "oc,soxl->scxl", skip_weight, gate_grad, preferred_element_type=jnp.float32
    )
    input_grad = (input_rows.astype(jnp.float32) + skip_back).astype(jnp.bfloat16)
    new_moment_one = beta_first * moment_one + (1.0 - beta_first) * weight_grad
    new_moment_two = beta_second * moment_two + (1.0 - beta_second) * weight_grad * weight_grad
    first_hat = new_moment_one / (1.0 - beta_first**STEP)
    second_hat = new_moment_two / (1.0 - beta_second**STEP)
    new_weight = spectral_weight - learn_rate * (
        first_hat / (jnp.sqrt(second_hat) + epsilon) + decay_rate * spectral_weight
    )
    return (input_grad, new_weight, new_moment_one, new_moment_two)


MESH = pl.DeviceIdType.MESH
ROWS = 8
STREAMS = 2


def fixed_tables(devices, own, rows):
    cells = devices * rows
    freq = np.arange(MODES)[:, None]
    angles = 2.0 * np.pi * ((freq * np.arange(cells)[None, :]) % cells) / cells
    scaling = 1.0 / math.sqrt(cells)
    parts = np.stack([np.cos(angles) * scaling, -np.sin(angles) * scaling], 1)
    parts = parts.reshape(MODES, 2, 1, devices, 1, rows)
    same = np.eye(own).reshape(1, 1, own, 1, own, 1)
    transform = (parts * same).reshape(MODES * 2 * own, devices * own * rows)
    channels = devices * own
    order = np.zeros((2, devices, own, devices, 2, own))
    for part in range(2):
        for device in range(devices):
            for one in range(own):
                order[part, device, one, device, part, one] = 1.0
    order = order.reshape(2 * channels, 2 * channels)
    spread = np.repeat(np.eye(channels), rows, axis=0)
    low = lambda table: jnp.asarray(table.astype(np.float32), jnp.bfloat16)
    return low(transform), low(transform.T), low(order), low(order.T), low(spread)


def dot(left, right, dims=((1,), (0,))):
    return lax.dot_general(left, right, (dims, ((), ())), preferred_element_type=jnp.float32)


def step_kernel(
    n,
    dens,
    upst,
    weight,
    first,
    second,
    skip,
    bias,
    counts,
    trans,
    trans_back,
    order,
    order_back,
    spread,
    out,
    new_weight,
    new_first,
    new_second,
    a1r,
    a2s,
    a2r,
    b1s,
    b1r,
    b2s,
    b2r,
    c1s,
    c1r,
    c2s,
    c2r,
    d1s,
    d1r,
    d2s,
    d2r,
    skip_part,
    kept,
    wsend,
    wrecv,
    gsend,
    grecv,
    send_sem,
    recv_sem,
    pair_send,
    pair_recv,
):
    me = lax.axis_index("dom")
    core = lax.axis_index("dp")
    low, wide = jnp.bfloat16, jnp.float32
    block = dens.shape[0] // n
    width = dens.shape[1] // STREAMS
    channels = weight.shape[0]

    barrier = pltpu.get_barrier_semaphore()

    def greet(shift, carry):
        pl.semaphore_signal(
            barrier, inc=1, device_id=(core, lax.rem(me + shift, n)), device_id_type=MESH
        )
        return carry

    lax.fori_loop(1, n, greet, 0)
    pl.semaphore_signal(barrier, inc=1, device_id=(1 - core, me), device_id_type=MESH)
    pl.semaphore_wait(barrier, n)

    def remote(stage, stream, shift, source, target):
        return pltpu.make_async_remote_copy(
            src_ref=source,
            dst_ref=target,
            send_sem=send_sem.at[stage, stream, shift],
            recv_sem=recv_sem.at[stage, stream, shift],
            device_id=(core, lax.rem(me + shift, n)),
            device_id_type=MESH,
        )

    def send_all(stage, stream, source, target):
        def one(shift, carry):
            peer = lax.rem(me + shift, n)
            remote(stage, stream, shift, source.at[stream, peer], target.at[stream, me]).start()
            return carry

        lax.fori_loop(1, n, one, 0)
        target[stream, me] = source[stream, me]

    def wait_all(stage, stream, source, target):
        def one(shift, carry):
            remote(stage, stream, shift, source.at[stream, me], target.at[stream, me]).wait_recv()
            return carry

        lax.fori_loop(1, n, one, 0)

    def lanes(stream):
        return pl.ds(stream * width, width)

    def rows(device):
        return pl.ds(pl.multiple_of(device * block, block), block)

    for stream in range(STREAMS):

        def start_one(shift, carry):
            peer = lax.rem(me + shift, n)
            remote(
                0, stream, shift, dens.at[rows(peer), lanes(stream)], a1r.at[stream, me]
            ).start()
            return carry

        lax.fori_loop(1, n, start_one, 0)
        a1r[stream, me] = dens[rows(me), lanes(stream)]

    own_low = weight[...].astype(low)
    wsend[...] = jnp.concatenate([own_low, own_low], axis=1)
    swap = pltpu.make_async_remote_copy(
        src_ref=wsend,
        dst_ref=wrecv,
        send_sem=pair_send.at[0],
        recv_sem=pair_recv.at[0],
        device_id=(1 - core, me),
        device_id_type=MESH,
    )
    swap.start()

    size = dens.shape[0]
    same_row = lax.rem(lax.broadcasted_iota(jnp.int32, (size, size), 0), ROWS) == lax.rem(
        lax.broadcasted_iota(jnp.int32, (size, size), 1), ROWS
    )
    spread_low = spread[...]

    def wide_map(dims):
        tall = dot(spread_low, skip[...], dims).astype(low)
        full = dot(tall, spread_low, ((1,), (1,)))
        return jnp.where(same_row, full, 0.0).astype(low)

    skip_part[...] = dot(wide_map(((1,), (0,))), dens[...]) + bias[...]
    back_map = wide_map(((1,), (1,)))

    swap.wait_recv()
    mine = weight[...].astype(low).astype(wide)
    other = wrecv[...].astype(wide)[:, :channels]
    is_first = core == 0
    weight_real = jnp.where(is_first, mine, other)
    weight_imag = jnp.where(is_first, other, mine)
    mixer = jnp.concatenate(
        [
            jnp.concatenate([weight_real, weight_imag], axis=1),
            jnp.concatenate([-weight_imag, weight_real], axis=1),
        ],
        axis=0,
    )
    mixer_back = mixer.T.astype(low)
    mixer = mixer.astype(low)
    keep = jnp.where(me < counts[core], 1.0, 0.0)
    scale = keep * jnp.where(me == 0, 1.0, 2.0)

    def by_device(values):
        return values.reshape(n, values.shape[0] // n, values.shape[1])

    def flat(ref, stream):
        values = ref[stream]
        return values.reshape(values.shape[0] * values.shape[1], values.shape[2])

    for stream in range(STREAMS):
        wait_all(0, stream, a1r, a1r)
        a2s[stream] = by_device(dot(trans[...], flat(a1r, stream)))
        send_all(1, stream, a2s, a2r)
    for stream in range(STREAMS):
        wait_all(1, stream, a2s, a2r)
        spectrum = dot(order[...], flat(a2r, stream).astype(low)).astype(low)
        kept[stream] = spectrum
        mixed = (dot(mixer_back, spectrum) * scale).astype(low)
        b1s[stream] = by_device(dot(order_back[...], mixed))
        send_all(2, stream, b1s, b1r)
    for stream in range(STREAMS):
        wait_all(2, stream, b1s, b1r)
        b2s[stream] = by_device(dot(trans_back[...], flat(b1r, stream).astype(low)).astype(low))
        send_all(3, stream, b2s, b2r)
    for stream in range(STREAMS):

        def slope_block(device):
            before = b2r[stream, device].astype(wide) + skip_part[rows(device), lanes(stream)]
            cotangent = upst[rows(device), lanes(stream)].astype(wide)
            c1s[stream, device] = (cotangent * gelu_slope(before)).astype(low)

        slope_block(me)
        c1r[stream, me] = c1s[stream, me]

        def one_slope(step, carry):
            shift = n - step
            device = lax.rem(me + step, n)
            remote(3, stream, shift, b2s.at[stream, me], b2r.at[stream, me]).wait_recv()
            slope_block(device)
            remote(4, stream, step, c1s.at[stream, device], c1r.at[stream, me]).start()
            return carry

        lax.fori_loop(1, n, one_slope, 0)
    for stream in range(STREAMS):
        wait_all(4, stream, c1s, c1r)
        c2s[stream] = by_device(dot(trans[...], flat(c1r, stream)))
        send_all(5, stream, c2s, c2r)
    products = jnp.zeros((2 * channels, 2 * channels), wide)
    for stream in range(STREAMS):
        wait_all(5, stream, c2s, c2r)
        gradient = (dot(order[...], flat(c2r, stream).astype(low)) * scale).astype(low)
        returned = dot(mixer, gradient).astype(low)
        d1s[stream] = by_device(dot(order_back[...], returned))
        send_all(6, stream, d1s, d1r)
        products += dot(kept[stream], gradient, ((1,), (1,)))
    top, bottom = products[:channels], products[channels:]
    grad_real = top[:, :channels] + bottom[:, channels:]
    grad_imag = top[:, channels:] - bottom[:, :channels]
    theirs = jnp.where(is_first, grad_imag, grad_real)
    ours = jnp.where(is_first, grad_real, grad_imag)
    gsend[...] = jnp.concatenate([theirs, theirs], axis=1)
    swap_grad = pltpu.make_async_remote_copy(
        src_ref=gsend,
        dst_ref=grecv,
        send_sem=pair_send.at[1],
        recv_sem=pair_recv.at[1],
        device_id=(1 - core, me),
        device_id_type=MESH,
    )
    swap_grad.start()
    for stream in range(STREAMS):
        wait_all(6, stream, d1s, d1r)
        d2s[stream] = by_device(dot(trans_back[...], flat(d1r, stream).astype(low)).astype(low))
        send_all(7, stream, d2s, d2r)
    for stream in range(STREAMS):
        skip_part[:, lanes(stream)] = dot(back_map, flat(c1s, stream))
    swap_grad.wait_recv()
    weight_grad = ours + grecv[...][:, :channels]
    one = beta_first * first[...] + (1.0 - beta_first) * weight_grad
    two = beta_second * second[...] + (1.0 - beta_second) * weight_grad * weight_grad
    new_first[...] = one
    new_second[...] = two
    first_hat = one / (1.0 - beta_first**STEP)
    second_hat = two / (1.0 - beta_second**STEP)
    new_weight[...] = weight[...] - learn_rate * (
        first_hat / (jnp.sqrt(second_hat) + epsilon) + decay_rate * weight[...]
    )
    for stream in range(STREAMS):

        def final_block(device):
            total = d2r[stream, device].astype(wide) + skip_part[rows(device), lanes(stream)]
            out[rows(device), lanes(stream)] = total.astype(low)

        final_block(me)

        def one_final(step, carry):
            shift = n - step
            remote(7, stream, shift, d2s.at[stream, me], d2r.at[stream, me]).wait_recv()
            final_block(lax.rem(me + step, n))
            return carry

        lax.fori_loop(1, n, one_final, 0)

    swap.wait_send()
    swap_grad.wait_send()
    sources = (a1r, a2s, b1s, b2s, c1s, c2s, d1s, d2s)
    for stage, source in enumerate(sources):
        for stream in range(STREAMS):

            def sent(shift, carry):
                remote(
                    stage, stream, shift, source.at[stream, me], source.at[stream, me]
                ).wait_send()
                return carry

            lax.fori_loop(1, n, sent, 0)


def one_frequency_each(
    n, density, upstream, spectral_weight, moment_one, moment_two, skip_weight, skip_bias, mode_counts
):
    samples, channels, slab_rows, line_count = density.shape
    own = channels // n
    width = line_count // STREAMS
    size = channels * slab_rows
    tables = fixed_tables(n, own, slab_rows)
    low, wide = jnp.bfloat16, jnp.float32
    vmem = pl.BlockSpec(memory_space=pltpu.VMEM)
    cells = pltpu.VMEM((STREAMS, n, own * slab_rows, width), low)
    modes = pltpu.VMEM((STREAMS, n, 2 * own, width), wide)
    result = pl.pallas_call(
        functools.partial(step_kernel, n),
        out_shape=(
            jax.ShapeDtypeStruct((size, line_count), low),
            jax.ShapeDtypeStruct((channels, channels), wide),
            jax.ShapeDtypeStruct((channels, channels), wide),
            jax.ShapeDtypeStruct((channels, channels), wide),
        ),
        in_specs=[vmem] * 7 + [pl.BlockSpec(memory_space=pltpu.SMEM)] + [vmem] * 5,
        out_specs=(vmem,) * 4,
        scratch_shapes=[
            cells,
            modes,
            modes,
            modes,
            modes,
            cells,
            cells,
            cells,
            cells,
            modes,
            modes,
            modes,
            modes,
            cells,
            cells,
            pltpu.VMEM((size, line_count), wide),
            pltpu.VMEM((STREAMS, 2 * channels, width), low),
            pltpu.VMEM((channels, 2 * channels), low),
            pltpu.VMEM((channels, 2 * channels), low),
            pltpu.VMEM((channels, 2 * channels), wide),
            pltpu.VMEM((channels, 2 * channels), wide),
            pltpu.SemaphoreType.DMA((8, STREAMS, n)),
            pltpu.SemaphoreType.DMA((8, STREAMS, n)),
            pltpu.SemaphoreType.DMA((2,)),
            pltpu.SemaphoreType.DMA((2,)),
        ],
        compiler_params=pltpu.CompilerParams(
            collective_id=0, has_side_effects=True, vmem_limit_bytes=40 * 1024 * 1024
        ),
        cost_estimate=pl.CostEstimate(
            flops=1_000_000_000, bytes_accessed=2_000_000, transcendentals=300_000
        ),
    )(
        density.reshape(size, line_count),
        upstream.reshape(size, line_count),
        spectral_weight,
        moment_one,
        moment_two,
        skip_weight,
        jnp.repeat(skip_bias, slab_rows)[:, None],
        mode_counts,
        *tables,
    )
    return (result[0].reshape(density.shape), *result[1:])


def on_mesh(density, *others):
    samples, channels, slab_rows, line_count = density.shape
    n, groups = lax.axis_size("dom"), lax.axis_size("dp")
    fits = (
        n == MODES
        and groups == 2
        and samples == 1
        and slab_rows == ROWS
        and 2 * (channels // n) == 8
        and line_count % (128 * STREAMS) == 0
    )
    if fits:
        return one_frequency_each(n, density, *others)
    return on_device(density, *others)


def solution(mesh):
    placed = (
        P("dp", None, "dom", None),
        P("dp", None, "dom", None),
        P(("dp", "dom"), None),
        P(("dp", "dom"), None),
        P(("dp", "dom"), None),
        P(),
        P(),
        P(),
    )
    return jax.shard_map(
        on_mesh,
        mesh=mesh,
        in_specs=placed,
        out_specs=(
            P("dp", None, "dom", None),
            P(("dp", "dom"), None),
            P(("dp", "dom"), None),
            P(("dp", "dom"), None),
        ),
        check_vma=False,
    )
```

```python
import functools
import math

import jax
import jax.numpy as jnp
import numpy as np
from jax import lax
from jax.experimental import pallas as pl
from jax.experimental.pallas import tpu as pltpu
from jax.sharding import PartitionSpec as P

MODES = 16
STEP = 10


learn_rate = 0.01
beta_first = 0.9
beta_second = 0.95
decay_rate = 0.1
epsilon = 1e-08


def axis_parts(count_xdim):
    freq_list = jnp.arange(MODES, dtype=jnp.int32)
    cell_list = jnp.arange(count_xdim, dtype=jnp.int32)
    phases = (
        jnp.mod(freq_list[:, None] * cell_list[None, :], count_xdim).astype(jnp.float32)
        / count_xdim
    )
    angles = 2.0 * math.pi * phases
    scaling = 1.0 / math.sqrt(count_xdim)
    return (
        (jnp.cos(angles) * scaling).astype(jnp.bfloat16),
        (jnp.sin(angles) * scaling).astype(jnp.bfloat16),
    )


def doubling_table():
    return jnp.where(jnp.arange(MODES, dtype=jnp.int32) > 0, 2.0, 1.0).astype(jnp.float32)


def gelu_slope(values):
    cumulative = 0.5 * (1.0 + lax.erf(values * 0.7071067811865476))
    bell_curve = jnp.exp(-0.5 * values * values) * 0.3989422804014327
    return cumulative + values * bell_curve


def send_pencils(field):
    return lax.all_to_all(field, "dom", split_axis=3, concat_axis=2, tiled=True)


def send_slabs(field):
    return lax.all_to_all(field, "dom", split_axis=2, concat_axis=3, tiled=True)


def forward_parts(field, cosines, sines):
    real_part = jnp.einsum("scxl,fx->slcf", field, cosines, preferred_element_type=jnp.float32)
    imag_part = -jnp.einsum("scxl,fx->slcf", field, sines, preferred_element_type=jnp.float32)
    return (real_part, imag_part)


def inverse_cells(values_real, values_imag, cosines, sines):
    first = jnp.einsum("slcf,fx->scxl", values_real, cosines, preferred_element_type=jnp.float32)
    second = jnp.einsum("slcf,fx->scxl", values_imag, sines, preferred_element_type=jnp.float32)
    return (first - second).astype(jnp.bfloat16)


def on_device(
    density, upstream, spectral_weight, moment_one, moment_two, skip_weight, skip_bias, mode_counts
):
    samples, channels, slab_rows, line_count = density.shape
    count_xdim = slab_rows * lax.axis_size("dom")
    cosines, sines = axis_parts(count_xdim)
    doubling = doubling_table()
    doubling_low = doubling.astype(jnp.bfloat16)
    counts_here = lax.dynamic_slice_in_dim(mode_counts, lax.axis_index("dp") * samples, samples, 0)
    keep_modes = (jnp.arange(MODES, dtype=jnp.int32)[None, :] < counts_here[:, None]).astype(
        jnp.float32
    )
    keep_wide = keep_modes[:, None, None, :]
    weight_short = spectral_weight.astype(jnp.bfloat16)
    group_low = lax.all_gather(weight_short, "dom", axis=0, tiled=True)
    weight_low = lax.all_gather(group_low, "dp", axis=0, tiled=True)
    weight_low = weight_low.reshape(2, MODES, channels, channels)
    weight_real = weight_low[0]
    weight_imag = weight_low[1]
    density_lines = send_pencils(density)
    real_part, imag_part = forward_parts(density_lines, cosines, sines)
    spec_real = real_part.astype(jnp.bfloat16)
    spec_imag = imag_part.astype(jnp.bfloat16)
    form = "slcf,fco->slof"
    mixed_real = jnp.einsum(
        form, spec_real, weight_real, preferred_element_type=jnp.float32
    ) - jnp.einsum(form, spec_imag, weight_imag, preferred_element_type=jnp.float32)
    mixed_imag = jnp.einsum(
        form, spec_imag, weight_real, preferred_element_type=jnp.float32
    ) + jnp.einsum(form, spec_real, weight_imag, preferred_element_type=jnp.float32)
    mixed_real = (mixed_real * keep_wide).astype(jnp.bfloat16) * doubling_low
    mixed_imag = (mixed_imag * keep_wide).astype(jnp.bfloat16) * doubling_low
    back_lines = inverse_cells(mixed_real, mixed_imag, cosines, sines)
    back_rows = send_slabs(back_lines)
    skip_part = jnp.einsum(
        "oc,scxl->soxl", skip_weight, density, preferred_element_type=jnp.float32
    )
    before = back_rows.astype(jnp.float32) + skip_part + skip_bias[None, :, None, None]
    gate_grad = (upstream.astype(jnp.float32) * gelu_slope(before)).astype(jnp.bfloat16)
    gate_lines = send_pencils(gate_grad)
    grad_real, grad_imag = forward_parts(gate_lines, cosines, sines)
    scale = keep_wide * doubling
    grad_real = (grad_real * scale).astype(jnp.bfloat16)
    grad_imag = (grad_imag * scale).astype(jnp.bfloat16)
    outer = "slof,slcf->fco"
    part_real = jnp.einsum(
        outer, grad_real, spec_real, preferred_element_type=jnp.float32
    ) + jnp.einsum(outer, grad_imag, spec_imag, preferred_element_type=jnp.float32)
    part_imag = jnp.einsum(
        outer, grad_imag, spec_real, preferred_element_type=jnp.float32
    ) - jnp.einsum(outer, grad_real, spec_imag, preferred_element_type=jnp.float32)
    grad_local = jnp.stack([part_real, part_imag], 0).reshape(2 * MODES * channels, channels)
    group_grad = lax.psum_scatter(
        grad_local.astype(jnp.bfloat16), "dp", scatter_dimension=0, tiled=True
    ).astype(jnp.float32)
    weight_grad = lax.psum_scatter(group_grad, "dom", scatter_dimension=0, tiled=True)
    inner = "fco,slof->slcf"
    input_real = jnp.einsum(
        inner, weight_real, grad_real, preferred_element_type=jnp.float32
    ) + jnp.einsum(inner, weight_imag, grad_imag, preferred_element_type=jnp.float32)
    input_imag = jnp.einsum(
        inner, weight_real, grad_imag, preferred_element_type=jnp.float32
    ) - jnp.einsum(inner, weight_imag, grad_real, preferred_element_type=jnp.float32)
    input_lines = inverse_cells(
        input_real.astype(jnp.bfloat16), input_imag.astype(jnp.bfloat16), cosines, sines
    )
    input_rows = send_slabs(input_lines)
    skip_back = jnp.einsum(
        "oc,soxl->scxl", skip_weight, gate_grad, preferred_element_type=jnp.float32
    )
    input_grad = (input_rows.astype(jnp.float32) + skip_back).astype(jnp.bfloat16)
    new_moment_one = beta_first * moment_one + (1.0 - beta_first) * weight_grad
    new_moment_two = beta_second * moment_two + (1.0 - beta_second) * weight_grad * weight_grad
    first_hat = new_moment_one / (1.0 - beta_first**STEP)
    second_hat = new_moment_two / (1.0 - beta_second**STEP)
    new_weight = spectral_weight - learn_rate * (
        first_hat / (jnp.sqrt(second_hat) + epsilon) + decay_rate * spectral_weight
    )
    return (input_grad, new_weight, new_moment_one, new_moment_two)


MESH = pl.DeviceIdType.MESH
ROWS = 8
STREAMS = 2


def fixed_tables(devices, own, rows):
    cells = devices * rows
    freq = np.arange(MODES)[:, None]
    angles = 2.0 * np.pi * ((freq * np.arange(cells)[None, :]) % cells) / cells
    scaling = 1.0 / math.sqrt(cells)
    parts = np.stack([np.cos(angles) * scaling, -np.sin(angles) * scaling], 1)
    parts = parts.reshape(MODES, 2, 1, devices, 1, rows)
    same = np.eye(own).reshape(1, 1, own, 1, own, 1)
    transform = (parts * same).reshape(MODES * 2 * own, devices * own * rows)
    channels = devices * own
    order = np.zeros((2, devices, own, devices, 2, own))
    for part in range(2):
        for device in range(devices):
            for one in range(own):
                order[part, device, one, device, part, one] = 1.0
    order = order.reshape(2 * channels, 2 * channels)
    spread = np.repeat(np.eye(channels), rows, axis=0)
    low = lambda table: jnp.asarray(table.astype(np.float32), jnp.bfloat16)
    return low(transform.T), low(order), low(order.T), low(spread)


def dot(left, right, dims=((1,), (0,))):
    return lax.dot_general(left, right, (dims, ((), ())), preferred_element_type=jnp.float32)


def step_kernel(
    n,
    dens_hbm,
    upst_hbm,
    weight_hbm,
    skip_hbm,
    bias_hbm,
    counts,
    trans_back_hbm,
    order_hbm,
    order_back_hbm,
    spread_hbm,
    out,
    out_grad,
    dens,
    upst,
    weight,
    skip,
    bias,
    trans_back,
    order,
    order_back,
    spread,
    trans,
    a1r,
    a2s,
    a2r,
    b1s,
    b1r,
    b2s,
    b2r,
    c1s,
    c1r,
    c2s,
    c2r,
    d1s,
    d1r,
    d2s,
    d2r,
    skip_part,
    kept,
    wsend,
    wrecv,
    gsend,
    grecv,
    send_sem,
    recv_sem,
    block_sem,
    pair_send,
    pair_recv,
    load_sem,
):
    me = lax.axis_index("dom")
    core = lax.axis_index("dp")
    low, wide = jnp.bfloat16, jnp.float32
    block = dens.shape[0] // n
    width = dens.shape[1] // STREAMS
    channels = weight.shape[0]

    loads = [
        pltpu.make_async_copy(source, target, load_sem.at[index])
        for index, (source, target) in enumerate(
            (
                (dens_hbm, dens),
                (weight_hbm, weight),
                (skip_hbm, skip),
                (spread_hbm, spread),
                (bias_hbm, bias),
                (order_hbm, order),
                (order_back_hbm, order_back),
                (trans_back_hbm, trans_back),
                (upst_hbm, upst),
            )
        )
    ]
    for load in loads:
        load.start()

    barrier = pltpu.get_barrier_semaphore()

    def greet(shift, carry):
        pl.semaphore_signal(
            barrier, inc=1, device_id=(core, lax.rem(me + shift, n)), device_id_type=MESH
        )
        return carry

    lax.fori_loop(1, n, greet, 0, unroll=True)
    pl.semaphore_signal(barrier, inc=1, device_id=(1 - core, me), device_id_type=MESH)
    pl.semaphore_wait(barrier, n)
    loads[0].wait()

    def remote(stage, stream, shift, source, target, arrival=None):
        return pltpu.make_async_remote_copy(
            src_ref=source,
            dst_ref=target,
            send_sem=send_sem.at[stage, stream],
            recv_sem=recv_sem.at[stage, stream] if arrival is None else arrival,
            device_id=(core, lax.rem(me + shift, n)),
            device_id_type=MESH,
        )

    def send_all(stage, stream, source, target):
        def one(shift, carry):
            peer = lax.rem(me + shift, n)
            remote(stage, stream, shift, source.at[stream, peer], target.at[stream, me]).start()
            return carry

        lax.fori_loop(1, n, one, 0, unroll=True)
        target[stream, me] = source[stream, me]

    def send_blocks(stage, stream, source, target):
        def one(shift, carry):
            peer = lax.rem(me + shift, n)
            remote(
                stage,
                stream,
                shift,
                source.at[stream, peer],
                target.at[stream, me],
                block_sem.at[stage // 4, stream, shift],
            ).start()
            return carry

        lax.fori_loop(1, n, one, 0, unroll=True)

    def all_of(stage, stream, ref):
        blocks = ref.at[stream, pl.ds(0, n - 1)]
        return remote(stage, stream, 1, blocks, blocks)

    def lanes(stream):
        return pl.ds(stream * width, width)

    def rows(device):
        return pl.ds(pl.multiple_of(device * block, block), block)

    for stream in range(STREAMS):

        def start_one(shift, carry):
            peer = lax.rem(me + shift, n)
            remote(
                0, stream, shift, dens.at[rows(peer), lanes(stream)], a1r.at[stream, me]
            ).start()
            return carry

        lax.fori_loop(1, n, start_one, 0, unroll=True)
        a1r[stream, me] = dens[rows(me), lanes(stream)]

    loads[1].wait()
    own_low = weight[...].astype(low)
    wsend[...] = jnp.concatenate([own_low, own_low], axis=1)
    swap = pltpu.make_async_remote_copy(
        src_ref=wsend,
        dst_ref=wrecv,
        send_sem=pair_send.at[0],
        recv_sem=pair_recv.at[0],
        device_id=(1 - core, me),
        device_id_type=MESH,
    )
    swap.start()
    for load in loads[2:]:
        load.wait()

    size = dens.shape[0]

    def wide_map(dims):
        same_row = lax.rem(lax.broadcasted_iota(jnp.int32, (size, size), 0), ROWS) == lax.rem(
            lax.broadcasted_iota(jnp.int32, (size, size), 1), ROWS
        )
        tall = dot(spread[...], skip[...], dims).astype(low)
        full = dot(tall, spread[...], ((1,), (1,)))
        return jnp.where(same_row, full, 0.0).astype(low)

    trans[...] = trans_back[...].astype(wide).T.astype(low)
    forward_map = wide_map(((1,), (0,)))
    swap.wait_recv()
    mine = weight[...].astype(low).astype(wide)
    other = wrecv[...].astype(wide)[:, :channels]
    is_first = core == 0
    weight_real = jnp.where(is_first, mine, other)
    weight_imag = jnp.where(is_first, other, mine)
    mixer = jnp.concatenate(
        [
            jnp.concatenate([weight_real, weight_imag], axis=1),
            jnp.concatenate([-weight_imag, weight_real], axis=1),
        ],
        axis=0,
    )
    mixer_back = mixer.T.astype(low)
    mixer = mixer.astype(low)
    keep = jnp.where(me < counts[core], 1.0, 0.0)
    scale = keep * jnp.where(me == 0, 1.0, 2.0)

    def by_device(values):
        return values.reshape(n, values.shape[0] // n, values.shape[1]).astype(low)

    def flat(ref, stream):
        values = ref[stream]
        return values.reshape(values.shape[0] * values.shape[1], values.shape[2])

    def flat_modes(ref, stream):
        values = ref[stream].astype(wide)
        return values.reshape(values.shape[0] * values.shape[1], values.shape[2]).astype(low)

    for stream in range(STREAMS):
        all_of(0, stream, a1r).wait_recv()
        a2s[stream] = by_device(dot(trans[...], flat(a1r, stream)))
        send_all(1, stream, a2s, a2r)
    bias_column = jnp.sum(spread[...].astype(wide) * bias[...], axis=1, keepdims=True)
    skip_part[...] = dot(forward_map, dens[...]) + bias_column
    for stream in range(STREAMS):
        all_of(1, stream, a2r).wait_recv()
        spectrum = dot(order[...], flat_modes(a2r, stream)).astype(low)
        kept[stream] = spectrum
        mixed = (dot(mixer_back, spectrum) * scale).astype(low)
        b1s[stream] = by_device(dot(order_back[...], mixed))
        send_all(2, stream, b1s, b1r)
    back_map = wide_map(((1,), (1,)))
    for stream in range(STREAMS):
        all_of(2, stream, b1r).wait_recv()
        b2s[stream] = by_device(dot(trans_back[...], flat_modes(b1r, stream)))
        send_blocks(3, stream, b2s, b2r)
    for stream in range(STREAMS):

        def slope_block(device, cells):
            before = cells.astype(wide) + skip_part[rows(device), lanes(stream)]
            cotangent = upst[rows(device), lanes(stream)].astype(wide)
            c1s[stream, device] = (cotangent * gelu_slope(before)).astype(low)

        slope_block(me, b2s[stream, me])
        c1r[stream, me] = c1s[stream, me]

        def one_slope(step, carry):
            shift = n - step
            device = lax.rem(me + step, n)
            cells = b2r.at[stream, device]
            remote(3, stream, step, cells, cells, block_sem.at[0, stream, shift]).wait_recv()
            slope_block(device, cells[...])
            remote(4, stream, step, c1s.at[stream, device], c1r.at[stream, me]).start()
            return carry

        lax.fori_loop(1, n, one_slope, 0)
    for stream in range(STREAMS):
        all_of(4, stream, c1r).wait_recv()
        c2s[stream] = by_device(dot(trans[...], flat(c1r, stream)))
        send_all(5, stream, c2s, c2r)
    for stream in range(STREAMS):
        skip_part[:, lanes(stream)] = dot(back_map, flat(c1s, stream))
    products = jnp.zeros((2 * channels, 2 * channels), wide)
    for stream in range(STREAMS):
        all_of(5, stream, c2r).wait_recv()
        gradient = (dot(order[...], flat_modes(c2r, stream)) * scale).astype(low)
        returned = dot(mixer, gradient).astype(low)
        d1s[stream] = by_device(dot(order_back[...], returned))
        send_all(6, stream, d1s, d1r)
        products += dot(kept[stream], gradient, ((1,), (1,)))
    top, bottom = products[:channels], products[channels:]
    grad_real = top[:, :channels] + bottom[:, channels:]
    grad_imag = top[:, channels:] - bottom[:, :channels]
    theirs = jnp.where(is_first, grad_imag, grad_real)
    ours = jnp.where(is_first, grad_real, grad_imag)
    gsend[...] = jnp.concatenate([theirs, theirs], axis=1)
    swap_grad = pltpu.make_async_remote_copy(
        src_ref=gsend,
        dst_ref=grecv,
        send_sem=pair_send.at[1],
        recv_sem=pair_recv.at[1],
        device_id=(1 - core, me),
        device_id_type=MESH,
    )
    swap_grad.start()
    for stream in range(STREAMS):
        all_of(6, stream, d1r).wait_recv()
        d2s[stream] = by_device(dot(trans_back[...], flat_modes(d1r, stream)))
        send_blocks(7, stream, d2s, d2r)
    swap_grad.wait_recv()
    out_grad[...] = ours + grecv[...][:, :channels]
    swap.wait_send()
    swap_grad.wait_send()
    for stage, source in enumerate((a1r, a2r, b1r, b2r, c1r, c2r, d1r)):
        for stream in range(STREAMS):
            all_of(stage, stream, source).wait_send()
    for stream in range(STREAMS):

        def final_block(device, cells):
            total = cells.astype(wide) + skip_part[rows(device), lanes(stream)]
            out[rows(device), lanes(stream)] = total.astype(low)

        final_block(me, d2s[stream, me])

        def one_final(step, carry):
            shift = n - step
            device = lax.rem(me + step, n)
            cells = d2r.at[stream, device]
            remote(7, stream, step, cells, cells, block_sem.at[1, stream, shift]).wait_recv()
            final_block(device, cells[...])
            return carry

        lax.fori_loop(1, n, one_final, 0)
        all_of(7, stream, d2r).wait_send()


def one_frequency_each(
    n, density, upstream, spectral_weight, moment_one, moment_two, skip_weight, skip_bias, mode_counts
):
    samples, channels, slab_rows, line_count = density.shape
    own = channels // n
    width = line_count // STREAMS
    size = channels * slab_rows
    tables = fixed_tables(n, own, slab_rows)
    low, wide = jnp.bfloat16, jnp.float32
    vmem = pl.BlockSpec(memory_space=pltpu.VMEM)
    hbm = pl.BlockSpec(memory_space=pltpu.HBM)
    cells = pltpu.VMEM((STREAMS, n, own * slab_rows, width), low)
    modes = pltpu.VMEM((STREAMS, n, 2 * own, width), low)
    arrays = (
        density.reshape(size, line_count),
        upstream.reshape(size, line_count),
        spectral_weight,
        skip_weight,
        skip_bias.reshape(1, channels),
    )
    input_grad, weight_grad = pl.pallas_call(
        functools.partial(step_kernel, n),
        out_shape=(
            jax.ShapeDtypeStruct((size, line_count), low),
            jax.ShapeDtypeStruct((channels, channels), wide),
        ),
        in_specs=[hbm] * 5 + [pl.BlockSpec(memory_space=pltpu.SMEM)] + [hbm] * 4,
        out_specs=(vmem,) * 2,
        scratch_shapes=[pltpu.VMEM(each.shape, each.dtype) for each in arrays + tables]
        + [pltpu.VMEM(tables[0].shape[::-1], low)]
        + [cells, modes, modes, modes, modes, cells, cells]
        + [cells, cells, modes, modes, modes, modes, cells, cells]
        + [
            pltpu.VMEM((size, line_count), wide),
            pltpu.VMEM((STREAMS, 2 * channels, width), low),
            pltpu.VMEM((channels, 2 * channels), low),
            pltpu.VMEM((channels, 2 * channels), low),
            pltpu.VMEM((channels, 2 * channels), wide),
            pltpu.VMEM((channels, 2 * channels), wide),
            pltpu.SemaphoreType.DMA((8, STREAMS)),
            pltpu.SemaphoreType.DMA((8, STREAMS)),
            pltpu.SemaphoreType.DMA((2, STREAMS, n)),
            pltpu.SemaphoreType.DMA((2,)),
            pltpu.SemaphoreType.DMA((2,)),
            pltpu.SemaphoreType.DMA((9,)),
        ],
        compiler_params=pltpu.CompilerParams(
            collective_id=0, has_side_effects=True, vmem_limit_bytes=60 * 1024 * 1024
        ),
        cost_estimate=pl.CostEstimate(
            flops=1_000_000_000, bytes_accessed=2_000_000, transcendentals=300_000
        ),
    )(*arrays, mode_counts, *tables)
    updated = adam(weight_grad, spectral_weight, moment_one, moment_two)
    return (input_grad.reshape(density.shape), *updated)


def adam(weight_grad, spectral_weight, moment_one, moment_two):
    new_moment_one = beta_first * moment_one + (1.0 - beta_first) * weight_grad
    new_moment_two = beta_second * moment_two + (1.0 - beta_second) * weight_grad * weight_grad
    first_hat = new_moment_one / (1.0 - beta_first**STEP)
    second_hat = new_moment_two / (1.0 - beta_second**STEP)
    new_weight = spectral_weight - learn_rate * (
        first_hat / (jnp.sqrt(second_hat) + epsilon) + decay_rate * spectral_weight
    )
    return (new_weight, new_moment_one, new_moment_two)


def on_mesh(density, *others):
    samples, channels, slab_rows, line_count = density.shape
    n, groups = lax.axis_size("dom"), lax.axis_size("dp")
    fits = (
        n == MODES
        and groups == 2
        and samples == 1
        and slab_rows == ROWS
        and 2 * (channels // n) == 8
        and line_count % (128 * STREAMS) == 0
    )
    if fits:
        return one_frequency_each(n, density, *others)
    return on_device(density, *others)


def solution(mesh):
    placed = (
        P("dp", None, "dom", None),
        P("dp", None, "dom", None),
        P(("dp", "dom"), None),
        P(("dp", "dom"), None),
        P(("dp", "dom"), None),
        P(),
        P(),
        P(),
    )
    return jax.shard_map(
        on_mesh,
        mesh=mesh,
        in_specs=placed,
        out_specs=(
            P("dp", None, "dom", None),
            P(("dp", "dom"), None),
            P(("dp", "dom"), None),
            P(("dp", "dom"), None),
        ),
        check_vma=False,
    )
```

```python
import functools
import math

import jax
import jax.numpy as jnp
import numpy as np
from jax import lax
from jax.experimental import pallas as pl
from jax.experimental.pallas import tpu as pltpu
from jax.sharding import PartitionSpec as P

MODES = 16
STEP = 10


learn_rate = 0.01
beta_first = 0.9
beta_second = 0.95
decay_rate = 0.1
epsilon = 1e-08


def axis_parts(count_xdim):
    freq_list = jnp.arange(MODES, dtype=jnp.int32)
    cell_list = jnp.arange(count_xdim, dtype=jnp.int32)
    phases = (
        jnp.mod(freq_list[:, None] * cell_list[None, :], count_xdim).astype(jnp.float32)
        / count_xdim
    )
    angles = 2.0 * math.pi * phases
    scaling = 1.0 / math.sqrt(count_xdim)
    return (
        (jnp.cos(angles) * scaling).astype(jnp.bfloat16),
        (jnp.sin(angles) * scaling).astype(jnp.bfloat16),
    )


def doubling_table():
    return jnp.where(jnp.arange(MODES, dtype=jnp.int32) > 0, 2.0, 1.0).astype(jnp.float32)


def gelu_slope(values):
    cumulative = 0.5 * (1.0 + lax.erf(values * 0.7071067811865476))
    bell_curve = jnp.exp(-0.5 * values * values) * 0.3989422804014327
    return cumulative + values * bell_curve


def send_pencils(field):
    return lax.all_to_all(field, "dom", split_axis=3, concat_axis=2, tiled=True)


def send_slabs(field):
    return lax.all_to_all(field, "dom", split_axis=2, concat_axis=3, tiled=True)


def forward_parts(field, cosines, sines):
    real_part = jnp.einsum("scxl,fx->slcf", field, cosines, preferred_element_type=jnp.float32)
    imag_part = -jnp.einsum("scxl,fx->slcf", field, sines, preferred_element_type=jnp.float32)
    return (real_part, imag_part)


def inverse_cells(values_real, values_imag, cosines, sines):
    first = jnp.einsum("slcf,fx->scxl", values_real, cosines, preferred_element_type=jnp.float32)
    second = jnp.einsum("slcf,fx->scxl", values_imag, sines, preferred_element_type=jnp.float32)
    return (first - second).astype(jnp.bfloat16)


def on_device(
    density, upstream, spectral_weight, moment_one, moment_two, skip_weight, skip_bias, mode_counts
):
    samples, channels, slab_rows, line_count = density.shape
    count_xdim = slab_rows * lax.axis_size("dom")
    cosines, sines = axis_parts(count_xdim)
    doubling = doubling_table()
    doubling_low = doubling.astype(jnp.bfloat16)
    counts_here = lax.dynamic_slice_in_dim(mode_counts, lax.axis_index("dp") * samples, samples, 0)
    keep_modes = (jnp.arange(MODES, dtype=jnp.int32)[None, :] < counts_here[:, None]).astype(
        jnp.float32
    )
    keep_wide = keep_modes[:, None, None, :]
    weight_short = spectral_weight.astype(jnp.bfloat16)
    group_low = lax.all_gather(weight_short, "dom", axis=0, tiled=True)
    weight_low = lax.all_gather(group_low, "dp", axis=0, tiled=True)
    weight_low = weight_low.reshape(2, MODES, channels, channels)
    weight_real = weight_low[0]
    weight_imag = weight_low[1]
    density_lines = send_pencils(density)
    real_part, imag_part = forward_parts(density_lines, cosines, sines)
    spec_real = real_part.astype(jnp.bfloat16)
    spec_imag = imag_part.astype(jnp.bfloat16)
    form = "slcf,fco->slof"
    mixed_real = jnp.einsum(
        form, spec_real, weight_real, preferred_element_type=jnp.float32
    ) - jnp.einsum(form, spec_imag, weight_imag, preferred_element_type=jnp.float32)
    mixed_imag = jnp.einsum(
        form, spec_imag, weight_real, preferred_element_type=jnp.float32
    ) + jnp.einsum(form, spec_real, weight_imag, preferred_element_type=jnp.float32)
    mixed_real = (mixed_real * keep_wide).astype(jnp.bfloat16) * doubling_low
    mixed_imag = (mixed_imag * keep_wide).astype(jnp.bfloat16) * doubling_low
    back_lines = inverse_cells(mixed_real, mixed_imag, cosines, sines)
    back_rows = send_slabs(back_lines)
    skip_part = jnp.einsum(
        "oc,scxl->soxl", skip_weight, density, preferred_element_type=jnp.float32
    )
    before = back_rows.astype(jnp.float32) + skip_part + skip_bias[None, :, None, None]
    gate_grad = (upstream.astype(jnp.float32) * gelu_slope(before)).astype(jnp.bfloat16)
    gate_lines = send_pencils(gate_grad)
    grad_real, grad_imag = forward_parts(gate_lines, cosines, sines)
    scale = keep_wide * doubling
    grad_real = (grad_real * scale).astype(jnp.bfloat16)
    grad_imag = (grad_imag * scale).astype(jnp.bfloat16)
    outer = "slof,slcf->fco"
    part_real = jnp.einsum(
        outer, grad_real, spec_real, preferred_element_type=jnp.float32
    ) + jnp.einsum(outer, grad_imag, spec_imag, preferred_element_type=jnp.float32)
    part_imag = jnp.einsum(
        outer, grad_imag, spec_real, preferred_element_type=jnp.float32
    ) - jnp.einsum(outer, grad_real, spec_imag, preferred_element_type=jnp.float32)
    grad_local = jnp.stack([part_real, part_imag], 0).reshape(2 * MODES * channels, channels)
    group_grad = lax.psum_scatter(
        grad_local.astype(jnp.bfloat16), "dp", scatter_dimension=0, tiled=True
    ).astype(jnp.float32)
    weight_grad = lax.psum_scatter(group_grad, "dom", scatter_dimension=0, tiled=True)
    inner = "fco,slof->slcf"
    input_real = jnp.einsum(
        inner, weight_real, grad_real, preferred_element_type=jnp.float32
    ) + jnp.einsum(inner, weight_imag, grad_imag, preferred_element_type=jnp.float32)
    input_imag = jnp.einsum(
        inner, weight_real, grad_imag, preferred_element_type=jnp.float32
    ) - jnp.einsum(inner, weight_imag, grad_real, preferred_element_type=jnp.float32)
    input_lines = inverse_cells(
        input_real.astype(jnp.bfloat16), input_imag.astype(jnp.bfloat16), cosines, sines
    )
    input_rows = send_slabs(input_lines)
    skip_back = jnp.einsum(
        "oc,soxl->scxl", skip_weight, gate_grad, preferred_element_type=jnp.float32
    )
    input_grad = (input_rows.astype(jnp.float32) + skip_back).astype(jnp.bfloat16)
    new_moment_one = beta_first * moment_one + (1.0 - beta_first) * weight_grad
    new_moment_two = beta_second * moment_two + (1.0 - beta_second) * weight_grad * weight_grad
    first_hat = new_moment_one / (1.0 - beta_first**STEP)
    second_hat = new_moment_two / (1.0 - beta_second**STEP)
    new_weight = spectral_weight - learn_rate * (
        first_hat / (jnp.sqrt(second_hat) + epsilon) + decay_rate * spectral_weight
    )
    return (input_grad, new_weight, new_moment_one, new_moment_two)


MESH = pl.DeviceIdType.MESH
ROWS = 8
STREAMS = 2


def fixed_tables(devices, own, rows):
    cells = devices * rows
    freq = np.arange(MODES)[:, None]
    angles = 2.0 * np.pi * ((freq * np.arange(cells)[None, :]) % cells) / cells
    scaling = 1.0 / math.sqrt(cells)
    parts = np.stack([np.cos(angles) * scaling, -np.sin(angles) * scaling], 1)
    parts = parts.reshape(MODES, 2, 1, devices, 1, rows)
    same = np.eye(own).reshape(1, 1, own, 1, own, 1)
    transform = (parts * same).reshape(MODES * 2 * own, devices * own * rows)
    channels = devices * own
    order = np.zeros((2, devices, own, devices, 2, own))
    for part in range(2):
        for device in range(devices):
            for one in range(own):
                order[part, device, one, device, part, one] = 1.0
    order = order.reshape(2 * channels, 2 * channels)
    spread = np.repeat(np.eye(channels), rows, axis=0)
    low = lambda table: jnp.asarray(table.astype(np.float32), jnp.bfloat16)
    return low(transform.T), low(order), low(order.T), low(spread)


def dot(left, right, dims=((1,), (0,))):
    return lax.dot_general(left, right, (dims, ((), ())), preferred_element_type=jnp.float32)


def step_kernel(
    n,
    dens_hbm,
    upst_hbm,
    weight_hbm,
    skip_hbm,
    bias_hbm,
    counts,
    trans_back_hbm,
    order_hbm,
    order_back_hbm,
    spread_hbm,
    out,
    out_grad,
    dens,
    upst,
    weight,
    skip,
    bias,
    trans_back,
    order,
    order_back,
    spread,
    trans,
    a1r,
    a2s,
    a2r,
    b1s,
    b1r,
    b2s,
    b2r,
    c1s,
    c1r,
    c2s,
    c2r,
    d1s,
    d1r,
    d2s,
    d2r,
    skip_part,
    kept,
    wsend,
    wrecv,
    gsend,
    grecv,
    send_sem,
    recv_sem,
    block_sem,
    pair_send,
    pair_recv,
    load_sem,
):
    me = lax.axis_index("dom")
    core = lax.axis_index("dp")
    low, wide = jnp.bfloat16, jnp.float32
    block = dens.shape[0] // n
    width = dens.shape[1] // STREAMS
    channels = weight.shape[0]

    loads = [
        pltpu.make_async_copy(source, target, load_sem.at[index])
        for index, (source, target) in enumerate(
            (
                (dens_hbm, dens),
                (weight_hbm, weight),
                (skip_hbm, skip),
                (spread_hbm, spread),
                (bias_hbm, bias),
                (order_hbm, order),
                (order_back_hbm, order_back),
                (trans_back_hbm, trans_back),
                (upst_hbm, upst),
            )
        )
    ]
    for load in loads:
        load.start()

    barrier = pltpu.get_barrier_semaphore()

    def greet(shift, carry):
        pl.semaphore_signal(
            barrier, inc=1, device_id=(core, lax.rem(me + shift, n)), device_id_type=MESH
        )
        return carry

    lax.fori_loop(1, n, greet, 0, unroll=True)
    pl.semaphore_wait(barrier, n - 1 + core)

    @pl.when(core == 0)
    def _():
        pl.semaphore_signal(barrier, inc=1, device_id=(1 - core, me), device_id_type=MESH)

    loads[0].wait()

    def remote(stage, stream, shift, source, target, arrival=None):
        return pltpu.make_async_remote_copy(
            src_ref=source,
            dst_ref=target,
            send_sem=send_sem.at[stage, stream],
            recv_sem=recv_sem.at[stage, stream] if arrival is None else arrival,
            device_id=(core, lax.rem(me + shift, n)),
            device_id_type=MESH,
        )

    def send_all(stage, stream, source, target):
        def one(shift, carry):
            peer = lax.rem(me + shift, n)
            remote(stage, stream, shift, source.at[stream, peer], target.at[stream, me]).start()
            return carry

        lax.fori_loop(1, n, one, 0, unroll=True)
        target[stream, me] = source[stream, me]

    def send_blocks(stage, stream, source, target):
        def one(shift, carry):
            peer = lax.rem(me + shift, n)
            remote(
                stage,
                stream,
                shift,
                source.at[stream, peer],
                target.at[stream, me],
                block_sem.at[stage // 4, stream, shift],
            ).start()
            return carry

        lax.fori_loop(1, n, one, 0, unroll=True)

    def all_of(stage, stream, ref):
        blocks = ref.at[stream, pl.ds(0, n - 1)]
        return remote(stage, stream, 1, blocks, blocks)

    def lanes(stream):
        return pl.ds(stream * width, width)

    def rows(device):
        return pl.ds(pl.multiple_of(device * block, block), block)

    for stream in range(STREAMS):

        def start_one(shift, carry):
            peer = lax.rem(me + shift, n)
            remote(
                0, stream, shift, dens.at[rows(peer), lanes(stream)], a1r.at[stream, me]
            ).start()
            return carry

        lax.fori_loop(1, n, start_one, 0, unroll=True)
        a1r[stream, me] = dens[rows(me), lanes(stream)]

    loads[1].wait()
    own_low = weight[...].astype(low)
    wsend[...] = jnp.concatenate([own_low, own_low], axis=1)
    swap = pltpu.make_async_remote_copy(
        src_ref=wsend,
        dst_ref=wrecv,
        send_sem=pair_send.at[0],
        recv_sem=pair_recv.at[0],
        device_id=(1 - core, me),
        device_id_type=MESH,
    )

    @pl.when(core == 1)
    def _():
        swap.start()

    for load in loads[2:]:
        load.wait()

    size = dens.shape[0]

    def wide_map(dims):
        same_row = lax.rem(lax.broadcasted_iota(jnp.int32, (size, size), 0), ROWS) == lax.rem(
            lax.broadcasted_iota(jnp.int32, (size, size), 1), ROWS
        )
        tall = dot(spread[...], skip[...], dims).astype(low)
        full = dot(tall, spread[...], ((1,), (1,)))
        return jnp.where(same_row, full, 0.0).astype(low)

    trans[...] = trans_back[...].astype(wide).T.astype(low)
    forward_map = wide_map(((1,), (0,)))
    def by_device(values):
        return values.reshape(n, values.shape[0] // n, values.shape[1]).astype(low)

    def flat(ref, stream):
        values = ref[stream]
        return values.reshape(values.shape[0] * values.shape[1], values.shape[2])

    def flat_modes(ref, stream):
        values = ref[stream].astype(wide)
        return values.reshape(values.shape[0] * values.shape[1], values.shape[2]).astype(low)

    for stream in range(STREAMS):
        all_of(0, stream, a1r).wait_recv()
        a2s[stream] = by_device(dot(trans[...], flat(a1r, stream)))
        send_all(1, stream, a2s, a2r)
    bias_column = jnp.sum(spread[...].astype(wide) * bias[...], axis=1, keepdims=True)
    skip_part[...] = dot(forward_map, dens[...]) + bias_column
    swap.wait_recv()

    @pl.when(core == 0)
    def _():
        swap.start()

    mine = weight[...].astype(low).astype(wide)
    other = wrecv[...].astype(wide)[:, :channels]
    is_first = core == 0
    weight_real = jnp.where(is_first, mine, other)
    weight_imag = jnp.where(is_first, other, mine)
    mixer = jnp.concatenate(
        [
            jnp.concatenate([weight_real, weight_imag], axis=1),
            jnp.concatenate([-weight_imag, weight_real], axis=1),
        ],
        axis=0,
    )
    mixer_back = mixer.T.astype(low)
    mixer = mixer.astype(low)
    keep = jnp.where(me < counts[core], 1.0, 0.0)
    scale = keep * jnp.where(me == 0, 1.0, 2.0)

    for stream in range(STREAMS):
        all_of(1, stream, a2r).wait_recv()
        spectrum = dot(order[...], flat_modes(a2r, stream)).astype(low)
        kept[stream] = spectrum
        mixed = (dot(mixer_back, spectrum) * scale).astype(low)
        b1s[stream] = by_device(dot(order_back[...], mixed))
        send_all(2, stream, b1s, b1r)
    back_map = wide_map(((1,), (1,)))
    for stream in range(STREAMS):
        all_of(2, stream, b1r).wait_recv()
        b2s[stream] = by_device(dot(trans_back[...], flat_modes(b1r, stream)))
        send_blocks(3, stream, b2s, b2r)
    for stream in range(STREAMS):

        def slope_block(device, cells):
            before = cells.astype(wide) + skip_part[rows(device), lanes(stream)]
            cotangent = upst[rows(device), lanes(stream)].astype(wide)
            c1s[stream, device] = (cotangent * gelu_slope(before)).astype(low)

        slope_block(me, b2s[stream, me])
        c1r[stream, me] = c1s[stream, me]

        def one_slope(step, carry):
            shift = n - step
            device = lax.rem(me + step, n)
            cells = b2r.at[stream, device]
            remote(3, stream, step, cells, cells, block_sem.at[0, stream, shift]).wait_recv()
            slope_block(device, cells[...])
            remote(4, stream, step, c1s.at[stream, device], c1r.at[stream, me]).start()
            return carry

        lax.fori_loop(1, n, one_slope, 0)
    for stream in range(STREAMS):
        all_of(4, stream, c1r).wait_recv()
        c2s[stream] = by_device(dot(trans[...], flat(c1r, stream)))
        send_all(5, stream, c2s, c2r)
    for stream in range(STREAMS):
        skip_part[:, lanes(stream)] = dot(back_map, flat(c1s, stream))
    products = jnp.zeros((2 * channels, 2 * channels), wide)
    for stream in range(STREAMS):
        all_of(5, stream, c2r).wait_recv()
        gradient = (dot(order[...], flat_modes(c2r, stream)) * scale).astype(low)
        returned = dot(mixer, gradient).astype(low)
        d1s[stream] = by_device(dot(order_back[...], returned))
        send_all(6, stream, d1s, d1r)
        products += dot(kept[stream], gradient, ((1,), (1,)))
    top, bottom = products[:channels], products[channels:]
    grad_real = top[:, :channels] + bottom[:, channels:]
    grad_imag = top[:, channels:] - bottom[:, :channels]
    theirs = jnp.where(is_first, grad_imag, grad_real)
    ours = jnp.where(is_first, grad_real, grad_imag)
    gsend[...] = jnp.concatenate([theirs, theirs], axis=1)
    swap_grad = pltpu.make_async_remote_copy(
        src_ref=gsend,
        dst_ref=grecv,
        send_sem=pair_send.at[1],
        recv_sem=pair_recv.at[1],
        device_id=(1 - core, me),
        device_id_type=MESH,
    )
    swap_grad.start()
    for stream in range(STREAMS):
        all_of(6, stream, d1r).wait_recv()
        d2s[stream] = by_device(dot(trans_back[...], flat_modes(d1r, stream)))
        send_blocks(7, stream, d2s, d2r)
    swap_grad.wait_recv()
    out_grad[...] = ours + grecv[...][:, :channels]
    swap.wait_send()
    swap_grad.wait_send()
    for stage, source in enumerate((a1r, a2r, b1r, b2r, c1r, c2r, d1r)):
        for stream in range(STREAMS):
            all_of(stage, stream, source).wait_send()
    for stream in range(STREAMS):

        def final_block(device, cells):
            total = cells.astype(wide) + skip_part[rows(device), lanes(stream)]
            out[rows(device), lanes(stream)] = total.astype(low)

        final_block(me, d2s[stream, me])

        def one_final(step, carry):
            shift = n - step
            device = lax.rem(me + step, n)
            cells = d2r.at[stream, device]
            remote(7, stream, step, cells, cells, block_sem.at[1, stream, shift]).wait_recv()
            final_block(device, cells[...])
            return carry

        lax.fori_loop(1, n, one_final, 0)
        all_of(7, stream, d2r).wait_send()


def one_frequency_each(
    n, density, upstream, spectral_weight, moment_one, moment_two, skip_weight, skip_bias, mode_counts
):
    samples, channels, slab_rows, line_count = density.shape
    own = channels // n
    width = line_count // STREAMS
    size = channels * slab_rows
    tables = fixed_tables(n, own, slab_rows)
    low, wide = jnp.bfloat16, jnp.float32
    vmem = pl.BlockSpec(memory_space=pltpu.VMEM)
    hbm = pl.BlockSpec(memory_space=pltpu.HBM)
    cells = pltpu.VMEM((STREAMS, n, own * slab_rows, width), low)
    modes = pltpu.VMEM((STREAMS, n, 2 * own, width), low)
    arrays = (
        density.reshape(size, line_count),
        upstream.reshape(size, line_count),
        spectral_weight,
        skip_weight,
        skip_bias.reshape(1, channels),
    )
    input_grad, weight_grad = pl.pallas_call(
        functools.partial(step_kernel, n),
        out_shape=(
            jax.ShapeDtypeStruct((size, line_count), low),
            jax.ShapeDtypeStruct((channels, channels), wide),
        ),
        in_specs=[hbm] * 5 + [pl.BlockSpec(memory_space=pltpu.SMEM)] + [hbm] * 4,
        out_specs=(vmem,) * 2,
        scratch_shapes=[pltpu.VMEM(each.shape, each.dtype) for each in arrays + tables]
        + [pltpu.VMEM(tables[0].shape[::-1], low)]
        + [cells, modes, modes, modes, modes, cells, cells]
        + [cells, cells, modes, modes, modes, modes, cells, cells]
        + [
            pltpu.VMEM((size, line_count), wide),
            pltpu.VMEM((STREAMS, 2 * channels, width), low),
            pltpu.VMEM((channels, 2 * channels), low),
            pltpu.VMEM((channels, 2 * channels), low),
            pltpu.VMEM((channels, 2 * channels), wide),
            pltpu.VMEM((channels, 2 * channels), wide),
            pltpu.SemaphoreType.DMA((8, STREAMS)),
            pltpu.SemaphoreType.DMA((8, STREAMS)),
            pltpu.SemaphoreType.DMA((2, STREAMS, n)),
            pltpu.SemaphoreType.DMA((2,)),
            pltpu.SemaphoreType.DMA((2,)),
            pltpu.SemaphoreType.DMA((9,)),
        ],
        compiler_params=pltpu.CompilerParams(
            collective_id=0, has_side_effects=True, vmem_limit_bytes=60 * 1024 * 1024
        ),
        cost_estimate=pl.CostEstimate(
            flops=1_000_000_000, bytes_accessed=2_000_000, transcendentals=300_000
        ),
    )(*arrays, mode_counts, *tables)
    updated = adam(weight_grad, spectral_weight, moment_one, moment_two)
    return (input_grad.reshape(density.shape), *updated)


def adam(weight_grad, spectral_weight, moment_one, moment_two):
    new_moment_one = beta_first * moment_one + (1.0 - beta_first) * weight_grad
    new_moment_two = beta_second * moment_two + (1.0 - beta_second) * weight_grad * weight_grad
    first_hat = new_moment_one / (1.0 - beta_first**STEP)
    second_hat = new_moment_two / (1.0 - beta_second**STEP)
    new_weight = spectral_weight - learn_rate * (
        first_hat / (jnp.sqrt(second_hat) + epsilon) + decay_rate * spectral_weight
    )
    return (new_weight, new_moment_one, new_moment_two)


def on_mesh(density, *others):
    samples, channels, slab_rows, line_count = density.shape
    n, groups = lax.axis_size("dom"), lax.axis_size("dp")
    fits = (
        n == MODES
        and groups == 2
        and samples == 1
        and slab_rows == ROWS
        and 2 * (channels // n) == 8
        and line_count % (128 * STREAMS) == 0
    )
    if fits:
        return one_frequency_each(n, density, *others)
    return on_device(density, *others)


def solution(mesh):
    placed = (
        P("dp", None, "dom", None),
        P("dp", None, "dom", None),
        P(("dp", "dom"), None),
        P(("dp", "dom"), None),
        P(("dp", "dom"), None),
        P(),
        P(),
        P(),
    )
    return jax.shard_map(
        on_mesh,
        mesh=mesh,
        in_specs=placed,
        out_specs=(
            P("dp", None, "dom", None),
            P(("dp", "dom"), None),
            P(("dp", "dom"), None),
            P(("dp", "dom"), None),
        ),
        check_vma=False,
    )
```

```python
import functools
import math

import jax
import jax.numpy as jnp
import numpy as np
from jax import lax
from jax.experimental import pallas as pl
from jax.experimental.pallas import tpu as pltpu
from jax.sharding import PartitionSpec as P

MODES = 16
STEP = 10


learn_rate = 0.01
beta_first = 0.9
beta_second = 0.95
decay_rate = 0.1
epsilon = 1e-08


def axis_parts(count_xdim):
    freq_list = jnp.arange(MODES, dtype=jnp.int32)
    cell_list = jnp.arange(count_xdim, dtype=jnp.int32)
    phases = (
        jnp.mod(freq_list[:, None] * cell_list[None, :], count_xdim).astype(jnp.float32)
        / count_xdim
    )
    angles = 2.0 * math.pi * phases
    scaling = 1.0 / math.sqrt(count_xdim)
    return (
        (jnp.cos(angles) * scaling).astype(jnp.bfloat16),
        (jnp.sin(angles) * scaling).astype(jnp.bfloat16),
    )


def doubling_table():
    return jnp.where(jnp.arange(MODES, dtype=jnp.int32) > 0, 2.0, 1.0).astype(jnp.float32)


def gelu_slope(values):
    cumulative = 0.5 * (1.0 + lax.erf(values * 0.7071067811865476))
    bell_curve = jnp.exp(-0.5 * values * values) * 0.3989422804014327
    return cumulative + values * bell_curve


def send_pencils(field):
    return lax.all_to_all(field, "dom", split_axis=3, concat_axis=2, tiled=True)


def send_slabs(field):
    return lax.all_to_all(field, "dom", split_axis=2, concat_axis=3, tiled=True)


def forward_parts(field, cosines, sines):
    real_part = jnp.einsum("scxl,fx->slcf", field, cosines, preferred_element_type=jnp.float32)
    imag_part = -jnp.einsum("scxl,fx->slcf", field, sines, preferred_element_type=jnp.float32)
    return (real_part, imag_part)


def inverse_cells(values_real, values_imag, cosines, sines):
    first = jnp.einsum("slcf,fx->scxl", values_real, cosines, preferred_element_type=jnp.float32)
    second = jnp.einsum("slcf,fx->scxl", values_imag, sines, preferred_element_type=jnp.float32)
    return (first - second).astype(jnp.bfloat16)


def on_device(
    density, upstream, spectral_weight, moment_one, moment_two, skip_weight, skip_bias, mode_counts
):
    samples, channels, slab_rows, line_count = density.shape
    count_xdim = slab_rows * lax.axis_size("dom")
    cosines, sines = axis_parts(count_xdim)
    doubling = doubling_table()
    doubling_low = doubling.astype(jnp.bfloat16)
    counts_here = lax.dynamic_slice_in_dim(mode_counts, lax.axis_index("dp") * samples, samples, 0)
    keep_modes = (jnp.arange(MODES, dtype=jnp.int32)[None, :] < counts_here[:, None]).astype(
        jnp.float32
    )
    keep_wide = keep_modes[:, None, None, :]
    weight_short = spectral_weight.astype(jnp.bfloat16)
    group_low = lax.all_gather(weight_short, "dom", axis=0, tiled=True)
    weight_low = lax.all_gather(group_low, "dp", axis=0, tiled=True)
    weight_low = weight_low.reshape(2, MODES, channels, channels)
    weight_real = weight_low[0]
    weight_imag = weight_low[1]
    density_lines = send_pencils(density)
    real_part, imag_part = forward_parts(density_lines, cosines, sines)
    spec_real = real_part.astype(jnp.bfloat16)
    spec_imag = imag_part.astype(jnp.bfloat16)
    form = "slcf,fco->slof"
    mixed_real = jnp.einsum(
        form, spec_real, weight_real, preferred_element_type=jnp.float32
    ) - jnp.einsum(form, spec_imag, weight_imag, preferred_element_type=jnp.float32)
    mixed_imag = jnp.einsum(
        form, spec_imag, weight_real, preferred_element_type=jnp.float32
    ) + jnp.einsum(form, spec_real, weight_imag, preferred_element_type=jnp.float32)
    mixed_real = (mixed_real * keep_wide).astype(jnp.bfloat16) * doubling_low
    mixed_imag = (mixed_imag * keep_wide).astype(jnp.bfloat16) * doubling_low
    back_lines = inverse_cells(mixed_real, mixed_imag, cosines, sines)
    back_rows = send_slabs(back_lines)
    skip_part = jnp.einsum(
        "oc,scxl->soxl", skip_weight, density, preferred_element_type=jnp.float32
    )
    before = back_rows.astype(jnp.float32) + skip_part + skip_bias[None, :, None, None]
    gate_grad = (upstream.astype(jnp.float32) * gelu_slope(before)).astype(jnp.bfloat16)
    gate_lines = send_pencils(gate_grad)
    grad_real, grad_imag = forward_parts(gate_lines, cosines, sines)
    scale = keep_wide * doubling
    grad_real = (grad_real * scale).astype(jnp.bfloat16)
    grad_imag = (grad_imag * scale).astype(jnp.bfloat16)
    outer = "slof,slcf->fco"
    part_real = jnp.einsum(
        outer, grad_real, spec_real, preferred_element_type=jnp.float32
    ) + jnp.einsum(outer, grad_imag, spec_imag, preferred_element_type=jnp.float32)
    part_imag = jnp.einsum(
        outer, grad_imag, spec_real, preferred_element_type=jnp.float32
    ) - jnp.einsum(outer, grad_real, spec_imag, preferred_element_type=jnp.float32)
    grad_local = jnp.stack([part_real, part_imag], 0).reshape(2 * MODES * channels, channels)
    group_grad = lax.psum_scatter(
        grad_local.astype(jnp.bfloat16), "dp", scatter_dimension=0, tiled=True
    ).astype(jnp.float32)
    weight_grad = lax.psum_scatter(group_grad, "dom", scatter_dimension=0, tiled=True)
    inner = "fco,slof->slcf"
    input_real = jnp.einsum(
        inner, weight_real, grad_real, preferred_element_type=jnp.float32
    ) + jnp.einsum(inner, weight_imag, grad_imag, preferred_element_type=jnp.float32)
    input_imag = jnp.einsum(
        inner, weight_real, grad_imag, preferred_element_type=jnp.float32
    ) - jnp.einsum(inner, weight_imag, grad_real, preferred_element_type=jnp.float32)
    input_lines = inverse_cells(
        input_real.astype(jnp.bfloat16), input_imag.astype(jnp.bfloat16), cosines, sines
    )
    input_rows = send_slabs(input_lines)
    skip_back = jnp.einsum(
        "oc,soxl->scxl", skip_weight, gate_grad, preferred_element_type=jnp.float32
    )
    input_grad = (input_rows.astype(jnp.float32) + skip_back).astype(jnp.bfloat16)
    new_moment_one = beta_first * moment_one + (1.0 - beta_first) * weight_grad
    new_moment_two = beta_second * moment_two + (1.0 - beta_second) * weight_grad * weight_grad
    first_hat = new_moment_one / (1.0 - beta_first**STEP)
    second_hat = new_moment_two / (1.0 - beta_second**STEP)
    new_weight = spectral_weight - learn_rate * (
        first_hat / (jnp.sqrt(second_hat) + epsilon) + decay_rate * spectral_weight
    )
    return (input_grad, new_weight, new_moment_one, new_moment_two)


MESH = pl.DeviceIdType.MESH
ROWS = 8
STREAMS = 1


def fixed_tables(devices, own, rows):
    cells = devices * rows
    freq = np.arange(MODES)[:, None]
    angles = 2.0 * np.pi * ((freq * np.arange(cells)[None, :]) % cells) / cells
    scaling = 1.0 / math.sqrt(cells)
    parts = np.stack([np.cos(angles) * scaling, -np.sin(angles) * scaling], 1)
    parts = parts.reshape(MODES, 2, 1, devices, 1, rows)
    same = np.eye(own).reshape(1, 1, own, 1, own, 1)
    transform = (parts * same).reshape(MODES * 2 * own, devices * own * rows)
    channels = devices * own
    order = np.zeros((2, devices, own, devices, 2, own))
    for part in range(2):
        for device in range(devices):
            for one in range(own):
                order[part, device, one, device, part, one] = 1.0
    order = order.reshape(2 * channels, 2 * channels)
    spread = np.repeat(np.eye(channels), rows, axis=0)
    low = lambda table: jnp.asarray(table.astype(np.float32), jnp.bfloat16)
    return low(transform.T), low(order), low(order.T), low(spread)


def dot(left, right, dims=((1,), (0,))):
    return lax.dot_general(left, right, (dims, ((), ())), preferred_element_type=jnp.float32)


def step_kernel(
    n,
    dens_hbm,
    upst_hbm,
    weight_hbm,
    skip_hbm,
    bias_hbm,
    counts,
    trans_back_hbm,
    order_hbm,
    order_back_hbm,
    spread_hbm,
    out,
    out_grad,
    dens,
    upst,
    weight,
    skip,
    bias,
    trans_back,
    order,
    order_back,
    spread,
    trans,
    a1r,
    a2s,
    a2r,
    b1s,
    b1r,
    b2s,
    b2r,
    c1s,
    c1r,
    c2s,
    c2r,
    d1s,
    d1r,
    d2s,
    d2r,
    skip_part,
    kept,
    wsend,
    wrecv,
    gsend,
    grecv,
    send_sem,
    recv_sem,
    block_sem,
    pair_send,
    pair_recv,
    load_sem,
):
    me = lax.axis_index("dom")
    core = lax.axis_index("dp")
    low, wide = jnp.bfloat16, jnp.float32
    block = dens.shape[0] // n
    width = dens.shape[1] // STREAMS
    channels = weight.shape[0]

    loads = [
        pltpu.make_async_copy(source, target, load_sem.at[index])
        for index, (source, target) in enumerate(
            (
                (dens_hbm, dens),
                (weight_hbm, weight),
                (skip_hbm, skip),
                (spread_hbm, spread),
                (bias_hbm, bias),
                (order_hbm, order),
                (order_back_hbm, order_back),
                (trans_back_hbm, trans_back),
                (upst_hbm, upst),
            )
        )
    ]
    for load in loads:
        load.start()

    barrier = pltpu.get_barrier_semaphore()

    def greet(shift, carry):
        pl.semaphore_signal(
            barrier, inc=1, device_id=(core, lax.rem(me + shift, n)), device_id_type=MESH
        )
        return carry

    lax.fori_loop(1, n, greet, 0, unroll=True)
    pl.semaphore_signal(barrier, inc=1, device_id=(1 - core, me), device_id_type=MESH)
    pl.semaphore_wait(barrier, n)
    loads[0].wait()

    def remote(stage, stream, shift, source, target, arrival=None):
        return pltpu.make_async_remote_copy(
            src_ref=source,
            dst_ref=target,
            send_sem=send_sem.at[stage, stream],
            recv_sem=recv_sem.at[stage, stream] if arrival is None else arrival,
            device_id=(core, lax.rem(me + shift, n)),
            device_id_type=MESH,
        )

    def send_all(stage, stream, source, target):
        def one(shift, carry):
            peer = lax.rem(me + shift, n)
            remote(stage, stream, shift, source.at[stream, peer], target.at[stream, me]).start()
            return carry

        lax.fori_loop(1, n, one, 0, unroll=True)
        target[stream, me] = source[stream, me]

    def send_blocks(stage, stream, source, target):
        def one(shift, carry):
            peer = lax.rem(me + shift, n)
            remote(
                stage,
                stream,
                shift,
                source.at[stream, peer],
                target.at[stream, me],
                block_sem.at[stage // 4, stream, shift],
            ).start()
            return carry

        lax.fori_loop(1, n, one, 0, unroll=True)

    def all_of(stage, stream, ref):
        blocks = ref.at[stream, pl.ds(0, n - 1)]
        return remote(stage, stream, 1, blocks, blocks)

    def lanes(stream):
        return pl.ds(stream * width, width)

    def rows(device):
        return pl.ds(pl.multiple_of(device * block, block), block)

    for stream in range(STREAMS):

        def start_one(shift, carry):
            peer = lax.rem(me + shift, n)
            remote(
                0, stream, shift, dens.at[rows(peer), lanes(stream)], a1r.at[stream, me]
            ).start()
            return carry

        lax.fori_loop(1, n, start_one, 0, unroll=True)
        a1r[stream, me] = dens[rows(me), lanes(stream)]

    loads[1].wait()
    own_low = weight[...].astype(low)
    wsend[...] = jnp.concatenate([own_low, own_low], axis=1)
    swap = pltpu.make_async_remote_copy(
        src_ref=wsend,
        dst_ref=wrecv,
        send_sem=pair_send.at[0],
        recv_sem=pair_recv.at[0],
        device_id=(1 - core, me),
        device_id_type=MESH,
    )
    swap.start()
    for load in loads[2:]:
        load.wait()

    size = dens.shape[0]

    def wide_map(dims):
        same_row = lax.rem(lax.broadcasted_iota(jnp.int32, (size, size), 0), ROWS) == lax.rem(
            lax.broadcasted_iota(jnp.int32, (size, size), 1), ROWS
        )
        tall = dot(spread[...], skip[...], dims).astype(low)
        full = dot(tall, spread[...], ((1,), (1,)))
        return jnp.where(same_row, full, 0.0).astype(low)

    trans[...] = trans_back[...].astype(wide).T.astype(low)
    forward_map = wide_map(((1,), (0,)))
    swap.wait_recv()
    mine = weight[...].astype(low).astype(wide)
    other = wrecv[...].astype(wide)[:, :channels]
    is_first = core == 0
    weight_real = jnp.where(is_first, mine, other)
    weight_imag = jnp.where(is_first, other, mine)
    mixer = jnp.concatenate(
        [
            jnp.concatenate([weight_real, weight_imag], axis=1),
            jnp.concatenate([-weight_imag, weight_real], axis=1),
        ],
        axis=0,
    )
    mixer_back = mixer.T.astype(low)
    mixer = mixer.astype(low)
    keep = jnp.where(me < counts[core], 1.0, 0.0)
    scale = keep * jnp.where(me == 0, 1.0, 2.0)

    def by_device(values):
        return values.reshape(n, values.shape[0] // n, values.shape[1]).astype(low)

    def flat(ref, stream):
        values = ref[stream]
        return values.reshape(values.shape[0] * values.shape[1], values.shape[2])

    def flat_modes(ref, stream):
        values = ref[stream].astype(wide)
        return values.reshape(values.shape[0] * values.shape[1], values.shape[2]).astype(low)

    for stream in range(STREAMS):
        all_of(0, stream, a1r).wait_recv()
        a2s[stream] = by_device(dot(trans[...], flat(a1r, stream)))
        send_all(1, stream, a2s, a2r)
    bias_column = jnp.sum(spread[...].astype(wide) * bias[...], axis=1, keepdims=True)
    skip_part[...] = dot(forward_map, dens[...]) + bias_column
    for stream in range(STREAMS):
        all_of(1, stream, a2r).wait_recv()
        spectrum = dot(order[...], flat_modes(a2r, stream)).astype(low)
        kept[stream] = spectrum
        mixed = (dot(mixer_back, spectrum) * scale).astype(low)
        b1s[stream] = by_device(dot(order_back[...], mixed))
        send_all(2, stream, b1s, b1r)
    back_map = wide_map(((1,), (1,)))
    for stream in range(STREAMS):
        all_of(2, stream, b1r).wait_recv()
        b2s[stream] = by_device(dot(trans_back[...], flat_modes(b1r, stream)))
        send_blocks(3, stream, b2s, b2r)
    for stream in range(STREAMS):

        def slope_block(device, cells):
            before = cells.astype(wide) + skip_part[rows(device), lanes(stream)]
            cotangent = upst[rows(device), lanes(stream)].astype(wide)
            c1s[stream, device] = (cotangent * gelu_slope(before)).astype(low)

        slope_block(me, b2s[stream, me])
        c1r[stream, me] = c1s[stream, me]

        def one_slope(step, carry):
            shift = n - step
            device = lax.rem(me + step, n)
            cells = b2r.at[stream, device]
            remote(3, stream, step, cells, cells, block_sem.at[0, stream, shift]).wait_recv()
            slope_block(device, cells[...])
            remote(4, stream, step, c1s.at[stream, device], c1r.at[stream, me]).start()
            return carry

        lax.fori_loop(1, n, one_slope, 0)
    for stream in range(STREAMS):
        all_of(4, stream, c1r).wait_recv()
        c2s[stream] = by_device(dot(trans[...], flat(c1r, stream)))
        send_all(5, stream, c2s, c2r)
    for stream in range(STREAMS):
        skip_part[:, lanes(stream)] = dot(back_map, flat(c1s, stream))
    products = jnp.zeros((2 * channels, 2 * channels), wide)
    for stream in range(STREAMS):
        all_of(5, stream, c2r).wait_recv()
        gradient = (dot(order[...], flat_modes(c2r, stream)) * scale).astype(low)
        returned = dot(mixer, gradient).astype(low)
        d1s[stream] = by_device(dot(order_back[...], returned))
        send_all(6, stream, d1s, d1r)
        products += dot(kept[stream], gradient, ((1,), (1,)))
    top, bottom = products[:channels], products[channels:]
    grad_real = top[:, :channels] + bottom[:, channels:]
    grad_imag = top[:, channels:] - bottom[:, :channels]
    theirs = jnp.where(is_first, grad_imag, grad_real)
    ours = jnp.where(is_first, grad_real, grad_imag)
    gsend[...] = jnp.concatenate([theirs, theirs], axis=1)
    swap_grad = pltpu.make_async_remote_copy(
        src_ref=gsend,
        dst_ref=grecv,
        send_sem=pair_send.at[1],
        recv_sem=pair_recv.at[1],
        device_id=(1 - core, me),
        device_id_type=MESH,
    )
    swap_grad.start()
    for stream in range(STREAMS):
        all_of(6, stream, d1r).wait_recv()
        d2s[stream] = by_device(dot(trans_back[...], flat_modes(d1r, stream)))
        send_blocks(7, stream, d2s, d2r)
    swap_grad.wait_recv()
    out_grad[...] = ours + grecv[...][:, :channels]
    swap.wait_send()
    swap_grad.wait_send()
    for stage, source in enumerate((a1r, a2r, b1r, b2r, c1r, c2r, d1r)):
        for stream in range(STREAMS):
            all_of(stage, stream, source).wait_send()
    for stream in range(STREAMS):

        def final_block(device, cells):
            total = cells.astype(wide) + skip_part[rows(device), lanes(stream)]
            out[rows(device), lanes(stream)] = total.astype(low)

        final_block(me, d2s[stream, me])

        def one_final(step, carry):
            shift = n - step
            device = lax.rem(me + step, n)
            cells = d2r.at[stream, device]
            remote(7, stream, step, cells, cells, block_sem.at[1, stream, shift]).wait_recv()
            final_block(device, cells[...])
            return carry

        lax.fori_loop(1, n, one_final, 0)
        all_of(7, stream, d2r).wait_send()


def one_frequency_each(
    n, density, upstream, spectral_weight, moment_one, moment_two, skip_weight, skip_bias, mode_counts
):
    samples, channels, slab_rows, line_count = density.shape
    own = channels // n
    width = line_count // STREAMS
    size = channels * slab_rows
    tables = fixed_tables(n, own, slab_rows)
    low, wide = jnp.bfloat16, jnp.float32
    vmem = pl.BlockSpec(memory_space=pltpu.VMEM)
    hbm = pl.BlockSpec(memory_space=pltpu.HBM)
    cells = pltpu.VMEM((STREAMS, n, own * slab_rows, width), low)
    modes = pltpu.VMEM((STREAMS, n, 2 * own, width), low)
    arrays = (
        density.reshape(size, line_count),
        upstream.reshape(size, line_count),
        spectral_weight,
        skip_weight,
        skip_bias.reshape(1, channels),
    )
    input_grad, weight_grad = pl.pallas_call(
        functools.partial(step_kernel, n),
        out_shape=(
            jax.ShapeDtypeStruct((size, line_count), low),
            jax.ShapeDtypeStruct((channels, channels), wide),
        ),
        in_specs=[hbm] * 5 + [pl.BlockSpec(memory_space=pltpu.SMEM)] + [hbm] * 4,
        out_specs=(vmem,) * 2,
        scratch_shapes=[pltpu.VMEM(each.shape, each.dtype) for each in arrays + tables]
        + [pltpu.VMEM(tables[0].shape[::-1], low)]
        + [cells, modes, modes, modes, modes, cells, cells]
        + [cells, cells, modes, modes, modes, modes, cells, cells]
        + [
            pltpu.VMEM((size, line_count), wide),
            pltpu.VMEM((STREAMS, 2 * channels, width), low),
            pltpu.VMEM((channels, 2 * channels), low),
            pltpu.VMEM((channels, 2 * channels), low),
            pltpu.VMEM((channels, 2 * channels), wide),
            pltpu.VMEM((channels, 2 * channels), wide),
            pltpu.SemaphoreType.DMA((8, STREAMS)),
            pltpu.SemaphoreType.DMA((8, STREAMS)),
            pltpu.SemaphoreType.DMA((2, STREAMS, n)),
            pltpu.SemaphoreType.DMA((2,)),
            pltpu.SemaphoreType.DMA((2,)),
            pltpu.SemaphoreType.DMA((9,)),
        ],
        compiler_params=pltpu.CompilerParams(
            collective_id=0, has_side_effects=True, vmem_limit_bytes=60 * 1024 * 1024
        ),
        cost_estimate=pl.CostEstimate(
            flops=1_000_000_000, bytes_accessed=2_000_000, transcendentals=300_000
        ),
    )(*arrays, mode_counts, *tables)
    updated = adam(weight_grad, spectral_weight, moment_one, moment_two)
    return (input_grad.reshape(density.shape), *updated)


def adam(weight_grad, spectral_weight, moment_one, moment_two):
    new_moment_one = beta_first * moment_one + (1.0 - beta_first) * weight_grad
    new_moment_two = beta_second * moment_two + (1.0 - beta_second) * weight_grad * weight_grad
    first_hat = new_moment_one / (1.0 - beta_first**STEP)
    second_hat = new_moment_two / (1.0 - beta_second**STEP)
    new_weight = spectral_weight - learn_rate * (
        first_hat / (jnp.sqrt(second_hat) + epsilon) + decay_rate * spectral_weight
    )
    return (new_weight, new_moment_one, new_moment_two)


def on_mesh(density, *others):
    samples, channels, slab_rows, line_count = density.shape
    n, groups = lax.axis_size("dom"), lax.axis_size("dp")
    fits = (
        n == MODES
        and groups == 2
        and samples == 1
        and slab_rows == ROWS
        and 2 * (channels // n) == 8
        and line_count % (128 * STREAMS) == 0
    )
    if fits:
        return one_frequency_each(n, density, *others)
    return on_device(density, *others)


def solution(mesh):
    placed = (
        P("dp", None, "dom", None),
        P("dp", None, "dom", None),
        P(("dp", "dom"), None),
        P(("dp", "dom"), None),
        P(("dp", "dom"), None),
        P(),
        P(),
        P(),
    )
    return jax.shard_map(
        on_mesh,
        mesh=mesh,
        in_specs=placed,
        out_specs=(
            P("dp", None, "dom", None),
            P(("dp", "dom"), None),
            P(("dp", "dom"), None),
            P(("dp", "dom"), None),
        ),
        check_vma=False,
    )
```

```python
import functools
import math

import jax
import jax.numpy as jnp
import numpy as np
from jax import lax
from jax.experimental import pallas as pl
from jax.experimental.pallas import tpu as pltpu
from jax.sharding import PartitionSpec as P

MODES = 16
STEP = 10


learn_rate = 0.01
beta_first = 0.9
beta_second = 0.95
decay_rate = 0.1
epsilon = 1e-08


def axis_parts(count_xdim):
    freq_list = jnp.arange(MODES, dtype=jnp.int32)
    cell_list = jnp.arange(count_xdim, dtype=jnp.int32)
    phases = (
        jnp.mod(freq_list[:, None] * cell_list[None, :], count_xdim).astype(jnp.float32)
        / count_xdim
    )
    angles = 2.0 * math.pi * phases
    scaling = 1.0 / math.sqrt(count_xdim)
    return (
        (jnp.cos(angles) * scaling).astype(jnp.bfloat16),
        (jnp.sin(angles) * scaling).astype(jnp.bfloat16),
    )


def doubling_table():
    return jnp.where(jnp.arange(MODES, dtype=jnp.int32) > 0, 2.0, 1.0).astype(jnp.float32)


def gelu_slope(values):
    cumulative = 0.5 * (1.0 + lax.erf(values * 0.7071067811865476))
    bell_curve = jnp.exp(-0.5 * values * values) * 0.3989422804014327
    return cumulative + values * bell_curve


def send_pencils(field):
    return lax.all_to_all(field, "dom", split_axis=3, concat_axis=2, tiled=True)


def send_slabs(field):
    return lax.all_to_all(field, "dom", split_axis=2, concat_axis=3, tiled=True)


def forward_parts(field, cosines, sines):
    real_part = jnp.einsum("scxl,fx->slcf", field, cosines, preferred_element_type=jnp.float32)
    imag_part = -jnp.einsum("scxl,fx->slcf", field, sines, preferred_element_type=jnp.float32)
    return (real_part, imag_part)


def inverse_cells(values_real, values_imag, cosines, sines):
    first = jnp.einsum("slcf,fx->scxl", values_real, cosines, preferred_element_type=jnp.float32)
    second = jnp.einsum("slcf,fx->scxl", values_imag, sines, preferred_element_type=jnp.float32)
    return (first - second).astype(jnp.bfloat16)


def on_device(
    density, upstream, spectral_weight, moment_one, moment_two, skip_weight, skip_bias, mode_counts
):
    samples, channels, slab_rows, line_count = density.shape
    count_xdim = slab_rows * lax.axis_size("dom")
    cosines, sines = axis_parts(count_xdim)
    doubling = doubling_table()
    doubling_low = doubling.astype(jnp.bfloat16)
    counts_here = lax.dynamic_slice_in_dim(mode_counts, lax.axis_index("dp") * samples, samples, 0)
    keep_modes = (jnp.arange(MODES, dtype=jnp.int32)[None, :] < counts_here[:, None]).astype(
        jnp.float32
    )
    keep_wide = keep_modes[:, None, None, :]
    weight_short = spectral_weight.astype(jnp.bfloat16)
    group_low = lax.all_gather(weight_short, "dom", axis=0, tiled=True)
    weight_low = lax.all_gather(group_low, "dp", axis=0, tiled=True)
    weight_low = weight_low.reshape(2, MODES, channels, channels)
    weight_real = weight_low[0]
    weight_imag = weight_low[1]
    density_lines = send_pencils(density)
    real_part, imag_part = forward_parts(density_lines, cosines, sines)
    spec_real = real_part.astype(jnp.bfloat16)
    spec_imag = imag_part.astype(jnp.bfloat16)
    form = "slcf,fco->slof"
    mixed_real = jnp.einsum(
        form, spec_real, weight_real, preferred_element_type=jnp.float32
    ) - jnp.einsum(form, spec_imag, weight_imag, preferred_element_type=jnp.float32)
    mixed_imag = jnp.einsum(
        form, spec_imag, weight_real, preferred_element_type=jnp.float32
    ) + jnp.einsum(form, spec_real, weight_imag, preferred_element_type=jnp.float32)
    mixed_real = (mixed_real * keep_wide).astype(jnp.bfloat16) * doubling_low
    mixed_imag = (mixed_imag * keep_wide).astype(jnp.bfloat16) * doubling_low
    back_lines = inverse_cells(mixed_real, mixed_imag, cosines, sines)
    back_rows = send_slabs(back_lines)
    skip_part = jnp.einsum(
        "oc,scxl->soxl", skip_weight, density, preferred_element_type=jnp.float32
    )
    before = back_rows.astype(jnp.float32) + skip_part + skip_bias[None, :, None, None]
    gate_grad = (upstream.astype(jnp.float32) * gelu_slope(before)).astype(jnp.bfloat16)
    gate_lines = send_pencils(gate_grad)
    grad_real, grad_imag = forward_parts(gate_lines, cosines, sines)
    scale = keep_wide * doubling
    grad_real = (grad_real * scale).astype(jnp.bfloat16)
    grad_imag = (grad_imag * scale).astype(jnp.bfloat16)
    outer = "slof,slcf->fco"
    part_real = jnp.einsum(
        outer, grad_real, spec_real, preferred_element_type=jnp.float32
    ) + jnp.einsum(outer, grad_imag, spec_imag, preferred_element_type=jnp.float32)
    part_imag = jnp.einsum(
        outer, grad_imag, spec_real, preferred_element_type=jnp.float32
    ) - jnp.einsum(outer, grad_real, spec_imag, preferred_element_type=jnp.float32)
    grad_local = jnp.stack([part_real, part_imag], 0).reshape(2 * MODES * channels, channels)
    group_grad = lax.psum_scatter(
        grad_local.astype(jnp.bfloat16), "dp", scatter_dimension=0, tiled=True
    ).astype(jnp.float32)
    weight_grad = lax.psum_scatter(group_grad, "dom", scatter_dimension=0, tiled=True)
    inner = "fco,slof->slcf"
    input_real = jnp.einsum(
        inner, weight_real, grad_real, preferred_element_type=jnp.float32
    ) + jnp.einsum(inner, weight_imag, grad_imag, preferred_element_type=jnp.float32)
    input_imag = jnp.einsum(
        inner, weight_real, grad_imag, preferred_element_type=jnp.float32
    ) - jnp.einsum(inner, weight_imag, grad_real, preferred_element_type=jnp.float32)
    input_lines = inverse_cells(
        input_real.astype(jnp.bfloat16), input_imag.astype(jnp.bfloat16), cosines, sines
    )
    input_rows = send_slabs(input_lines)
    skip_back = jnp.einsum(
        "oc,soxl->scxl", skip_weight, gate_grad, preferred_element_type=jnp.float32
    )
    input_grad = (input_rows.astype(jnp.float32) + skip_back).astype(jnp.bfloat16)
    new_moment_one = beta_first * moment_one + (1.0 - beta_first) * weight_grad
    new_moment_two = beta_second * moment_two + (1.0 - beta_second) * weight_grad * weight_grad
    first_hat = new_moment_one / (1.0 - beta_first**STEP)
    second_hat = new_moment_two / (1.0 - beta_second**STEP)
    new_weight = spectral_weight - learn_rate * (
        first_hat / (jnp.sqrt(second_hat) + epsilon) + decay_rate * spectral_weight
    )
    return (input_grad, new_weight, new_moment_one, new_moment_two)


MESH = pl.DeviceIdType.MESH
ROWS = 8
STREAMS = 2
HALVES = 2
LANES = 128


def fixed_tables(halves, members, own, rows):
    cells = halves * members * rows
    freq = np.arange(MODES)[:, None]
    angles = 2.0 * np.pi * ((freq * np.arange(cells)[None, :]) % cells) / cells
    scaling = 1.0 / math.sqrt(cells)
    parts = np.stack([np.cos(angles) * scaling, -np.sin(angles) * scaling], 1)
    parts = parts.reshape(MODES, 2, halves, members, rows).transpose(2, 3, 4, 0, 1)
    parts = parts.reshape(halves, members, 1, rows, MODES, 2, 1)
    same = np.eye(own).reshape(1, 1, own, 1, 1, 1, own)
    transform = (parts * same).reshape(halves, members * own * rows, -1, LANES)
    transform = transform.transpose(0, 2, 1, 3)
    channels = members * own
    order = np.zeros((2, members, own, members, 2, own))
    for part in range(2):
        for device in range(members):
            for one in range(own):
                order[part, device, one, device, part, one] = 1.0
    order = order.reshape(2 * channels, 2 * channels)
    spread = np.repeat(np.eye(channels), rows, axis=0)
    low = lambda table: jnp.asarray(table.astype(np.float32), jnp.bfloat16)
    return low(transform), low(order), low(order.T), low(spread)


def dot(left, right, dims=((1,), (0,))):
    return lax.dot_general(left, right, (dims, ((), ())), preferred_element_type=jnp.float32)


def exact_dot(left, right):
    return jnp.dot(
        left, right, precision=lax.Precision.HIGHEST, preferred_element_type=jnp.float32
    )


def step_kernel(
    n,
    dens_hbm,
    upst_hbm,
    weight_hbm,
    skip_hbm,
    bias_hbm,
    counts,
    trans_back_hbm,
    order_hbm,
    order_back_hbm,
    spread_hbm,
    out,
    out_grad,
    dens,
    upst,
    weight,
    skip,
    bias,
    trans_back,
    order,
    order_back,
    spread,
    trans,
    a1r,
    a2s,
    a2r,
    b1s,
    b1r,
    b2s,
    b2r,
    c1s,
    c1r,
    c2s,
    c2r,
    d1s,
    d1r,
    d2s,
    d2r,
    skip_part,
    kept,
    wsend,
    wrecv,
    gsend,
    grecv,
    send_sem,
    recv_sem,
    block_sem,
    pair_send,
    pair_recv,
    load_sem,
):
    me = lax.axis_index("dom")
    core = lax.axis_index("dp")
    low, wide = jnp.bfloat16, jnp.float32
    members = n // HALVES
    half, member = me // members, lax.rem(me, members)
    block = dens.shape[0] // members
    width = dens.shape[1] // STREAMS
    channels = weight.shape[0]

    loads = [
        pltpu.make_async_copy(source, target, load_sem.at[index])
        for index, (source, target) in enumerate(
            (
                (dens_hbm, dens),
                (weight_hbm, weight),
                (skip_hbm, skip),
                (spread_hbm, spread),
                (bias_hbm, bias),
                (order_hbm, order),
                (order_back_hbm, order_back),
                *(
                    (trans_back_hbm.at[half, tile], trans_back.at[:, pl.ds(tile * LANES, LANES)])
                    for tile in range(trans_back_hbm.shape[1])
                ),
                (upst_hbm, upst),
            )
        )
    ]
    for load in loads:
        load.start()

    barrier = pltpu.get_barrier_semaphore()

    def greet(shift, carry):
        pl.semaphore_signal(
            barrier, inc=1, device_id=(core, lax.rem(me + shift, n)), device_id_type=MESH
        )
        return carry

    lax.fori_loop(1, n, greet, 0, unroll=True)
    pl.semaphore_signal(barrier, inc=1, device_id=(1 - core, me), device_id_type=MESH)
    pl.semaphore_wait(barrier, n)
    loads[0].wait()

    def remote(stage, stream, peer, source, target, arrival=None):
        return pltpu.make_async_remote_copy(
            src_ref=source,
            dst_ref=target,
            send_sem=send_sem.at[stage, stream],
            recv_sem=recv_sem.at[stage, stream] if arrival is None else arrival,
            device_id=(core, peer),
            device_id_type=MESH,
        )

    def send_modes(stage, stream, source, target, slots):
        def one(shift, carry):
            peer = lax.rem(me + shift, n)
            remote(
                stage,
                stream,
                peer,
                source.at[stream, lax.rem(peer, slots)],
                target.at[stream, me],
            ).start()
            return carry

        lax.fori_loop(1, n, one, 0, unroll=True)
        target[stream, me] = source[stream, lax.rem(me, slots)]

    def near(step):
        return lax.rem(member + step, members)

    def send_blocks(stage, stream, source, target):
        def one(shift, carry):
            peer = near(shift)
            remote(
                stage,
                stream,
                half * members + peer,
                source.at[stream, peer],
                target.at[stream, member],
                block_sem.at[stage // 4, stream, shift],
            ).start()
            return carry

        lax.fori_loop(1, members, one, 0, unroll=True)

    def all_of(stage, stream, ref):
        blocks = ref.at[stream, pl.ds(0, ref.shape[1] - 1)]
        return remote(stage, stream, me, blocks, blocks)

    def lanes(stream):
        return pl.ds(stream * width, width)

    def rows(device):
        return pl.ds(pl.multiple_of(device * block, block), block)

    for stream in range(STREAMS):

        def start_one(shift, carry):
            peer = near(shift)
            remote(
                0,
                stream,
                half * members + peer,
                dens.at[rows(peer), lanes(stream)],
                a1r.at[stream, member],
            ).start()
            return carry

        lax.fori_loop(1, members, start_one, 0, unroll=True)
        a1r[stream, member] = dens[rows(member), lanes(stream)]

    loads[1].wait()
    own_low = weight[...].astype(low)
    wsend[...] = jnp.concatenate([own_low, own_low], axis=1)
    swap = pltpu.make_async_remote_copy(
        src_ref=wsend,
        dst_ref=wrecv,
        send_sem=pair_send.at[0],
        recv_sem=pair_recv.at[0],
        device_id=(1 - core, me),
        device_id_type=MESH,
    )
    swap.start()
    for load in loads[2:]:
        load.wait()

    size = dens.shape[0]

    def wide_map(dims):
        same_row = lax.rem(lax.broadcasted_iota(jnp.int32, (size, size), 0), ROWS) == lax.rem(
            lax.broadcasted_iota(jnp.int32, (size, size), 1), ROWS
        )
        tall = dot(spread[...], skip[...], dims).astype(low)
        full = dot(tall, spread[...], ((1,), (1,)))
        return jnp.where(same_row, full, 0.0).astype(low)

    trans[...] = trans_back[...].astype(wide).T.astype(low)
    forward_map = wide_map(((1,), (0,)))
    swap.wait_recv()
    mine = weight[...].astype(low).astype(wide)
    other = wrecv[...].astype(wide)[:, :channels]
    is_first = core == 0
    weight_real = jnp.where(is_first, mine, other)
    weight_imag = jnp.where(is_first, other, mine)
    mixer = jnp.concatenate(
        [
            jnp.concatenate([weight_real, weight_imag], axis=1),
            jnp.concatenate([-weight_imag, weight_real], axis=1),
        ],
        axis=0,
    )
    mixer = dot(dot(order_back[...], mixer.astype(low)).astype(low), order[...])
    mixer_back = mixer.T.astype(low)
    mixer = mixer.astype(low)
    keep = jnp.where(me < counts[core], 1.0, 0.0)
    scale = keep * jnp.where(me == 0, 1.0, 2.0)

    def blocks_of(values, count):
        return values.astype(low).reshape(count, values.shape[0] // count, values.shape[1])

    def flat(ref, stream):
        values = ref[stream]
        return values.reshape(values.shape[0] * values.shape[1], values.shape[2])

    def added(ref, stream):
        values = ref[stream].astype(wide)
        total = values[:members]
        for other in range(1, HALVES):
            total += values[other * members : (other + 1) * members]
        return total.reshape(members * values.shape[1], values.shape[2])

    for stream in range(STREAMS):
        all_of(0, stream, a1r).wait_recv()
        a2s[stream] = blocks_of(dot(trans[...], flat(a1r, stream)), n)
        send_modes(1, stream, a2s, a2r, n)
    bias_column = jnp.sum(spread[...].astype(wide) * bias[...], axis=1, keepdims=True)
    skip_part[...] = dot(forward_map, dens[...]) + bias_column
    for stream in range(STREAMS):
        all_of(1, stream, a2r).wait_recv()
        spectrum = added(a2r, stream).astype(low)
        kept[stream] = spectrum
        b1s[stream] = blocks_of(dot(mixer_back, spectrum) * scale, members)
        send_modes(2, stream, b1s, b1r, members)
    back_map = wide_map(((1,), (1,)))
    for stream in range(STREAMS):
        all_of(2, stream, b1r).wait_recv()
        b2s[stream] = blocks_of(dot(trans_back[...], flat(b1r, stream)), members)
        send_blocks(3, stream, b2s, b2r)
    for stream in range(STREAMS):

        def slope_block(device, cells):
            before = cells.astype(wide) + skip_part[rows(device), lanes(stream)]
            cotangent = upst[rows(device), lanes(stream)].astype(wide)
            c1s[stream, device] = (cotangent * gelu_slope(before)).astype(low)

        slope_block(member, b2s[stream, member])
        c1r[stream, member] = c1s[stream, member]

        def one_slope(step, carry):
            device = near(step)
            cells = b2r.at[stream, device]
            remote(
                3, stream, me, cells, cells, block_sem.at[0, stream, members - step]
            ).wait_recv()
            slope_block(device, cells[...])
            remote(
                4,
                stream,
                half * members + device,
                c1s.at[stream, device],
                c1r.at[stream, member],
            ).start()
            return carry

        lax.fori_loop(1, members, one_slope, 0)
    for stream in range(STREAMS):
        all_of(4, stream, c1r).wait_recv()
        c2s[stream] = blocks_of(dot(trans[...], flat(c1r, stream)), n)
        send_modes(5, stream, c2s, c2r, n)
    for stream in range(STREAMS):
        skip_part[:, lanes(stream)] = dot(back_map, flat(c1s, stream))
    products = jnp.zeros((2 * channels, 2 * channels), wide)
    for stream in range(STREAMS):
        all_of(5, stream, c2r).wait_recv()
        gradient = (added(c2r, stream) * scale).astype(low)
        d1s[stream] = blocks_of(dot(mixer, gradient), members)
        send_modes(6, stream, d1s, d1r, members)
        products += dot(kept[stream], gradient, ((1,), (1,)))
    products = exact_dot(exact_dot(order[...].astype(wide), products), order_back[...].astype(wide))
    top, bottom = products[:channels], products[channels:]
    grad_real = top[:, :channels] + bottom[:, channels:]
    grad_imag = top[:, channels:] - bottom[:, :channels]
    theirs = jnp.where(is_first, grad_imag, grad_real)
    ours = jnp.where(is_first, grad_real, grad_imag)
    gsend[...] = jnp.concatenate([theirs, theirs], axis=1)
    swap_grad = pltpu.make_async_remote_copy(
        src_ref=gsend,
        dst_ref=grecv,
        send_sem=pair_send.at[1],
        recv_sem=pair_recv.at[1],
        device_id=(1 - core, me),
        device_id_type=MESH,
    )
    swap_grad.start()
    for stream in range(STREAMS):
        all_of(6, stream, d1r).wait_recv()
        d2s[stream] = blocks_of(dot(trans_back[...], flat(d1r, stream)), members)
        send_blocks(7, stream, d2s, d2r)
    swap_grad.wait_recv()
    out_grad[...] = ours + grecv[...][:, :channels]
    swap.wait_send()
    swap_grad.wait_send()
    for stage, source in enumerate((a1r, a2r, b1r, b2r, c1r, c2r, d1r)):
        for stream in range(STREAMS):
            all_of(stage, stream, source).wait_send()
    for stream in range(STREAMS):

        def final_block(device, cells):
            total = cells.astype(wide) + skip_part[rows(device), lanes(stream)]
            out[rows(device), lanes(stream)] = total.astype(low)

        final_block(member, d2s[stream, member])

        def one_final(step, carry):
            device = near(step)
            cells = d2r.at[stream, device]
            remote(
                7, stream, me, cells, cells, block_sem.at[1, stream, members - step]
            ).wait_recv()
            final_block(device, cells[...])
            return carry

        lax.fori_loop(1, members, one_final, 0)
        all_of(7, stream, d2r).wait_send()


def one_frequency_each(
    n, density, upstream, spectral_weight, moment_one, moment_two, skip_weight, skip_bias, mode_counts
):
    samples, channels, slab_rows, line_count = density.shape
    members = n // HALVES
    own = channels // members
    width = line_count // STREAMS
    size = channels * slab_rows
    tables = fixed_tables(HALVES, members, own, slab_rows)
    low, wide = jnp.bfloat16, jnp.float32
    vmem = pl.BlockSpec(memory_space=pltpu.VMEM)
    hbm = pl.BlockSpec(memory_space=pltpu.HBM)
    cells = pltpu.VMEM((STREAMS, members, own * slab_rows, width), low)
    modes = pltpu.VMEM((STREAMS, n, 2 * own, width), low)
    mixed = pltpu.VMEM((STREAMS, members, 2 * own, width), low)
    arrays = (
        density.reshape(size, line_count),
        upstream.reshape(size, line_count),
        spectral_weight,
        skip_weight,
        skip_bias.reshape(1, channels),
    )
    input_grad, weight_grad = pl.pallas_call(
        functools.partial(step_kernel, n),
        out_shape=(
            jax.ShapeDtypeStruct((size, line_count), low),
            jax.ShapeDtypeStruct((channels, channels), wide),
        ),
        in_specs=[hbm] * 5 + [pl.BlockSpec(memory_space=pltpu.SMEM)] + [hbm] * 4,
        out_specs=(vmem,) * 2,
        scratch_shapes=[pltpu.VMEM(each.shape, each.dtype) for each in arrays]
        + [pltpu.VMEM((size, 2 * MODES * own), low)]
        + [pltpu.VMEM(each.shape, each.dtype) for each in tables[1:]]
        + [pltpu.VMEM((2 * MODES * own, size), low)]
        + [cells, modes, modes, mixed, modes, cells, cells]
        + [cells, cells, modes, modes, mixed, modes, cells, cells]
        + [
            pltpu.VMEM((size, line_count), wide),
            pltpu.VMEM((STREAMS, 2 * channels, width), low),
            pltpu.VMEM((channels, 2 * channels), low),
            pltpu.VMEM((channels, 2 * channels), low),
            pltpu.VMEM((channels, 2 * channels), wide),
            pltpu.VMEM((channels, 2 * channels), wide),
            pltpu.SemaphoreType.DMA((8, STREAMS)),
            pltpu.SemaphoreType.DMA((8, STREAMS)),
            pltpu.SemaphoreType.DMA((2, STREAMS, n)),
            pltpu.SemaphoreType.DMA((2,)),
            pltpu.SemaphoreType.DMA((2,)),
            pltpu.SemaphoreType.DMA((8 + tables[0].shape[1],)),
        ],
        compiler_params=pltpu.CompilerParams(
            collective_id=0, has_side_effects=True, vmem_limit_bytes=60 * 1024 * 1024
        ),
        cost_estimate=pl.CostEstimate(
            flops=1_000_000_000, bytes_accessed=2_000_000, transcendentals=300_000
        ),
    )(*arrays, mode_counts, *tables)
    updated = adam(weight_grad, spectral_weight, moment_one, moment_two)
    return (input_grad.reshape(density.shape), *updated)


def adam(weight_grad, spectral_weight, moment_one, moment_two):
    new_moment_one = beta_first * moment_one + (1.0 - beta_first) * weight_grad
    new_moment_two = beta_second * moment_two + (1.0 - beta_second) * weight_grad * weight_grad
    first_hat = new_moment_one / (1.0 - beta_first**STEP)
    second_hat = new_moment_two / (1.0 - beta_second**STEP)
    new_weight = spectral_weight - learn_rate * (
        first_hat / (jnp.sqrt(second_hat) + epsilon) + decay_rate * spectral_weight
    )
    return (new_weight, new_moment_one, new_moment_two)


def on_mesh(density, *others):
    samples, channels, slab_rows, line_count = density.shape
    n, groups = lax.axis_size("dom"), lax.axis_size("dp")
    fits = (
        n == MODES
        and groups == 2
        and samples == 1
        and slab_rows == ROWS
        and n % HALVES == 0
        and 2 * (channels // (n // HALVES)) == 16
        and line_count % (128 * STREAMS) == 0
    )
    if fits:
        return one_frequency_each(n, density, *others)
    return on_device(density, *others)


def solution(mesh):
    placed = (
        P("dp", None, "dom", None),
        P("dp", None, "dom", None),
        P(("dp", "dom"), None),
        P(("dp", "dom"), None),
        P(("dp", "dom"), None),
        P(),
        P(),
        P(),
    )
    return jax.shard_map(
        on_mesh,
        mesh=mesh,
        in_specs=placed,
        out_specs=(
            P("dp", None, "dom", None),
            P(("dp", "dom"), None),
            P(("dp", "dom"), None),
            P(("dp", "dom"), None),
        ),
        check_vma=False,
    )
```

```python
import functools
import math

import jax
import jax.numpy as jnp
import numpy as np
from jax import lax
from jax.experimental import pallas as pl
from jax.experimental.pallas import tpu as pltpu
from jax.sharding import PartitionSpec as P

MODES = 16
STEP = 10


learn_rate = 0.01
beta_first = 0.9
beta_second = 0.95
decay_rate = 0.1
epsilon = 1e-08


def axis_parts(count_xdim):
    freq_list = jnp.arange(MODES, dtype=jnp.int32)
    cell_list = jnp.arange(count_xdim, dtype=jnp.int32)
    phases = (
        jnp.mod(freq_list[:, None] * cell_list[None, :], count_xdim).astype(jnp.float32)
        / count_xdim
    )
    angles = 2.0 * math.pi * phases
    scaling = 1.0 / math.sqrt(count_xdim)
    return (
        (jnp.cos(angles) * scaling).astype(jnp.bfloat16),
        (jnp.sin(angles) * scaling).astype(jnp.bfloat16),
    )


def doubling_table():
    return jnp.where(jnp.arange(MODES, dtype=jnp.int32) > 0, 2.0, 1.0).astype(jnp.float32)


def gelu_slope(values):
    cumulative = 0.5 * (1.0 + lax.erf(values * 0.7071067811865476))
    bell_curve = jnp.exp(-0.5 * values * values) * 0.3989422804014327
    return cumulative + values * bell_curve


def send_pencils(field):
    return lax.all_to_all(field, "dom", split_axis=3, concat_axis=2, tiled=True)


def send_slabs(field):
    return lax.all_to_all(field, "dom", split_axis=2, concat_axis=3, tiled=True)


def forward_parts(field, cosines, sines):
    real_part = jnp.einsum("scxl,fx->slcf", field, cosines, preferred_element_type=jnp.float32)
    imag_part = -jnp.einsum("scxl,fx->slcf", field, sines, preferred_element_type=jnp.float32)
    return (real_part, imag_part)


def inverse_cells(values_real, values_imag, cosines, sines):
    first = jnp.einsum("slcf,fx->scxl", values_real, cosines, preferred_element_type=jnp.float32)
    second = jnp.einsum("slcf,fx->scxl", values_imag, sines, preferred_element_type=jnp.float32)
    return (first - second).astype(jnp.bfloat16)


def on_device(
    density, upstream, spectral_weight, moment_one, moment_two, skip_weight, skip_bias, mode_counts
):
    samples, channels, slab_rows, line_count = density.shape
    count_xdim = slab_rows * lax.axis_size("dom")
    cosines, sines = axis_parts(count_xdim)
    doubling = doubling_table()
    doubling_low = doubling.astype(jnp.bfloat16)
    counts_here = lax.dynamic_slice_in_dim(mode_counts, lax.axis_index("dp") * samples, samples, 0)
    keep_modes = (jnp.arange(MODES, dtype=jnp.int32)[None, :] < counts_here[:, None]).astype(
        jnp.float32
    )
    keep_wide = keep_modes[:, None, None, :]
    weight_short = spectral_weight.astype(jnp.bfloat16)
    group_low = lax.all_gather(weight_short, "dom", axis=0, tiled=True)
    weight_low = lax.all_gather(group_low, "dp", axis=0, tiled=True)
    weight_low = weight_low.reshape(2, MODES, channels, channels)
    weight_real = weight_low[0]
    weight_imag = weight_low[1]
    density_lines = send_pencils(density)
    real_part, imag_part = forward_parts(density_lines, cosines, sines)
    spec_real = real_part.astype(jnp.bfloat16)
    spec_imag = imag_part.astype(jnp.bfloat16)
    form = "slcf,fco->slof"
    mixed_real = jnp.einsum(
        form, spec_real, weight_real, preferred_element_type=jnp.float32
    ) - jnp.einsum(form, spec_imag, weight_imag, preferred_element_type=jnp.float32)
    mixed_imag = jnp.einsum(
        form, spec_imag, weight_real, preferred_element_type=jnp.float32
    ) + jnp.einsum(form, spec_real, weight_imag, preferred_element_type=jnp.float32)
    mixed_real = (mixed_real * keep_wide).astype(jnp.bfloat16) * doubling_low
    mixed_imag = (mixed_imag * keep_wide).astype(jnp.bfloat16) * doubling_low
    back_lines = inverse_cells(mixed_real, mixed_imag, cosines, sines)
    back_rows = send_slabs(back_lines)
    skip_part = jnp.einsum(
        "oc,scxl->soxl", skip_weight, density, preferred_element_type=jnp.float32
    )
    before = back_rows.astype(jnp.float32) + skip_part + skip_bias[None, :, None, None]
    gate_grad = (upstream.astype(jnp.float32) * gelu_slope(before)).astype(jnp.bfloat16)
    gate_lines = send_pencils(gate_grad)
    grad_real, grad_imag = forward_parts(gate_lines, cosines, sines)
    scale = keep_wide * doubling
    grad_real = (grad_real * scale).astype(jnp.bfloat16)
    grad_imag = (grad_imag * scale).astype(jnp.bfloat16)
    outer = "slof,slcf->fco"
    part_real = jnp.einsum(
        outer, grad_real, spec_real, preferred_element_type=jnp.float32
    ) + jnp.einsum(outer, grad_imag, spec_imag, preferred_element_type=jnp.float32)
    part_imag = jnp.einsum(
        outer, grad_imag, spec_real, preferred_element_type=jnp.float32
    ) - jnp.einsum(outer, grad_real, spec_imag, preferred_element_type=jnp.float32)
    grad_local = jnp.stack([part_real, part_imag], 0).reshape(2 * MODES * channels, channels)
    group_grad = lax.psum_scatter(
        grad_local.astype(jnp.bfloat16), "dp", scatter_dimension=0, tiled=True
    ).astype(jnp.float32)
    weight_grad = lax.psum_scatter(group_grad, "dom", scatter_dimension=0, tiled=True)
    inner = "fco,slof->slcf"
    input_real = jnp.einsum(
        inner, weight_real, grad_real, preferred_element_type=jnp.float32
    ) + jnp.einsum(inner, weight_imag, grad_imag, preferred_element_type=jnp.float32)
    input_imag = jnp.einsum(
        inner, weight_real, grad_imag, preferred_element_type=jnp.float32
    ) - jnp.einsum(inner, weight_imag, grad_real, preferred_element_type=jnp.float32)
    input_lines = inverse_cells(
        input_real.astype(jnp.bfloat16), input_imag.astype(jnp.bfloat16), cosines, sines
    )
    input_rows = send_slabs(input_lines)
    skip_back = jnp.einsum(
        "oc,soxl->scxl", skip_weight, gate_grad, preferred_element_type=jnp.float32
    )
    input_grad = (input_rows.astype(jnp.float32) + skip_back).astype(jnp.bfloat16)
    new_moment_one = beta_first * moment_one + (1.0 - beta_first) * weight_grad
    new_moment_two = beta_second * moment_two + (1.0 - beta_second) * weight_grad * weight_grad
    first_hat = new_moment_one / (1.0 - beta_first**STEP)
    second_hat = new_moment_two / (1.0 - beta_second**STEP)
    new_weight = spectral_weight - learn_rate * (
        first_hat / (jnp.sqrt(second_hat) + epsilon) + decay_rate * spectral_weight
    )
    return (input_grad, new_weight, new_moment_one, new_moment_two)


MESH = pl.DeviceIdType.MESH
ROWS = 8
STREAMS = 2
HALVES = 2
LANES = 128


def fixed_tables(halves, members, own, rows):
    cells = halves * members * rows
    freq = np.arange(MODES)[:, None]
    angles = 2.0 * np.pi * ((freq * np.arange(cells)[None, :]) % cells) / cells
    scaling = 1.0 / math.sqrt(cells)
    parts = np.stack([np.cos(angles) * scaling, -np.sin(angles) * scaling], 1)
    parts = parts.reshape(MODES, 2, halves, members, rows).transpose(2, 3, 4, 0, 1)
    parts = parts.reshape(halves, members, 1, rows, MODES, 2, 1)
    same = np.eye(own).reshape(1, 1, own, 1, 1, 1, own)
    transform = (parts * same).reshape(halves, members * own * rows, -1, LANES)
    transform = transform.transpose(0, 2, 1, 3)
    channels = members * own
    order = np.zeros((2, members, own, members, 2, own))
    for part in range(2):
        for device in range(members):
            for one in range(own):
                order[part, device, one, device, part, one] = 1.0
    order = order.reshape(2 * channels, 2 * channels)
    spread = np.repeat(np.eye(channels), rows, axis=0)
    low = lambda table: jnp.asarray(table.astype(np.float32), jnp.bfloat16)
    return low(transform), low(order), low(order.T), low(spread)


def dot(left, right, dims=((1,), (0,))):
    return lax.dot_general(left, right, (dims, ((), ())), preferred_element_type=jnp.float32)


def exact_dot(left, right):
    return jnp.dot(
        left, right, precision=lax.Precision.HIGHEST, preferred_element_type=jnp.float32
    )


def step_kernel(
    n,
    dens_hbm,
    upst_hbm,
    weight_hbm,
    skip_hbm,
    bias_hbm,
    counts,
    trans_back_hbm,
    order_hbm,
    order_back_hbm,
    spread_hbm,
    out_rows,
    out_skip,
    out_grad,
    dens,
    upst,
    weight,
    skip,
    bias,
    trans_back,
    order,
    order_back,
    spread,
    trans,
    a1r,
    a2s,
    a2r,
    b1s,
    b1r,
    b2s,
    b2r,
    c1s,
    c1r,
    c2s,
    c2r,
    d1s,
    d1r,
    d2s,
    skip_part,
    kept,
    wsend,
    wrecv,
    gsend,
    grecv,
    send_sem,
    recv_sem,
    block_sem,
    pair_send,
    pair_recv,
    load_sem,
    store_sem,
):
    me = lax.axis_index("dom")
    core = lax.axis_index("dp")
    low, wide = jnp.bfloat16, jnp.float32
    members = n // HALVES
    half, member = me // members, lax.rem(me, members)
    block = dens.shape[0] // members
    width = dens.shape[1] // STREAMS
    channels = weight.shape[0]

    loads = [
        pltpu.make_async_copy(source, target, load_sem.at[index])
        for index, (source, target) in enumerate(
            (
                (dens_hbm, dens),
                (weight_hbm, weight),
                (skip_hbm, skip),
                (spread_hbm, spread),
                (bias_hbm, bias),
                (order_hbm, order),
                (order_back_hbm, order_back),
                *(
                    (trans_back_hbm.at[half, tile], trans_back.at[:, pl.ds(tile * LANES, LANES)])
                    for tile in range(trans_back_hbm.shape[1])
                ),
                (upst_hbm, upst),
            )
        )
    ]
    for load in loads:
        load.start()

    barrier = pltpu.get_barrier_semaphore()

    def greet(shift, carry):
        pl.semaphore_signal(
            barrier, inc=1, device_id=(core, lax.rem(me + shift, n)), device_id_type=MESH
        )
        return carry

    lax.fori_loop(1, n, greet, 0, unroll=True)
    pl.semaphore_signal(barrier, inc=1, device_id=(1 - core, me), device_id_type=MESH)
    pl.semaphore_wait(barrier, n)
    loads[0].wait()

    def remote(stage, stream, peer, source, target, arrival=None):
        return pltpu.make_async_remote_copy(
            src_ref=source,
            dst_ref=target,
            send_sem=send_sem.at[stage, stream],
            recv_sem=recv_sem.at[stage, stream] if arrival is None else arrival,
            device_id=(core, peer),
            device_id_type=MESH,
        )

    def send_modes(stage, stream, source, target, slots):
        def one(shift, carry):
            peer = lax.rem(me + shift, n)
            remote(
                stage,
                stream,
                peer,
                source.at[stream, lax.rem(peer, slots)],
                target.at[stream, me],
            ).start()
            return carry

        lax.fori_loop(1, n, one, 0, unroll=True)
        target[stream, me] = source[stream, lax.rem(me, slots)]

    def near(step):
        return lax.rem(member + step, members)

    def send_blocks(stage, stream, source, target):
        def one(shift, carry):
            peer = near(shift)
            remote(
                stage,
                stream,
                half * members + peer,
                source.at[stream, peer],
                target.at[stream, member],
                block_sem.at[stream, shift],
            ).start()
            return carry

        lax.fori_loop(1, members, one, 0, unroll=True)

    def all_of(stage, stream, ref):
        blocks = ref.at[stream, pl.ds(0, ref.shape[1] - 1)]
        return remote(stage, stream, me, blocks, blocks)

    def lanes(stream):
        return pl.ds(stream * width, width)

    def rows(device):
        return pl.ds(pl.multiple_of(device * block, block), block)

    for stream in range(STREAMS):

        def start_one(shift, carry):
            peer = near(shift)
            remote(
                0,
                stream,
                half * members + peer,
                dens.at[rows(peer), lanes(stream)],
                a1r.at[stream, member],
            ).start()
            return carry

        lax.fori_loop(1, members, start_one, 0, unroll=True)
        a1r[stream, member] = dens[rows(member), lanes(stream)]

    loads[1].wait()
    own_low = weight[...].astype(low)
    wsend[...] = jnp.concatenate([own_low, own_low], axis=1)
    swap = pltpu.make_async_remote_copy(
        src_ref=wsend,
        dst_ref=wrecv,
        send_sem=pair_send.at[0],
        recv_sem=pair_recv.at[0],
        device_id=(1 - core, me),
        device_id_type=MESH,
    )
    swap.start()
    for load in loads[2:]:
        load.wait()

    size = dens.shape[0]

    def wide_map(dims):
        same_row = lax.rem(lax.broadcasted_iota(jnp.int32, (size, size), 0), ROWS) == lax.rem(
            lax.broadcasted_iota(jnp.int32, (size, size), 1), ROWS
        )
        tall = dot(spread[...], skip[...], dims).astype(low)
        full = dot(tall, spread[...], ((1,), (1,)))
        return jnp.where(same_row, full, 0.0).astype(low)

    trans[...] = trans_back[...].astype(wide).T.astype(low)
    forward_map = wide_map(((1,), (0,)))
    swap.wait_recv()
    mine = weight[...].astype(low).astype(wide)
    other = wrecv[...].astype(wide)[:, :channels]
    is_first = core == 0
    weight_real = jnp.where(is_first, mine, other)
    weight_imag = jnp.where(is_first, other, mine)
    mixer = jnp.concatenate(
        [
            jnp.concatenate([weight_real, weight_imag], axis=1),
            jnp.concatenate([-weight_imag, weight_real], axis=1),
        ],
        axis=0,
    )
    mixer = dot(dot(order_back[...], mixer.astype(low)).astype(low), order[...])
    mixer_back = mixer.T.astype(low)
    mixer = mixer.astype(low)
    keep = jnp.where(me < counts[core], 1.0, 0.0)
    scale = keep * jnp.where(me == 0, 1.0, 2.0)

    def blocks_of(values, count):
        return values.astype(low).reshape(count, values.shape[0] // count, values.shape[1])

    def flat(ref, stream):
        values = ref[stream]
        return values.reshape(values.shape[0] * values.shape[1], values.shape[2])

    def added(ref, stream):
        values = ref[stream].astype(wide)
        total = values[:members]
        for other in range(1, HALVES):
            total += values[other * members : (other + 1) * members]
        return total.reshape(members * values.shape[1], values.shape[2])

    for stream in range(STREAMS):
        all_of(0, stream, a1r).wait_recv()
        a2s[stream] = blocks_of(dot(trans[...], flat(a1r, stream)), n)
        send_modes(1, stream, a2s, a2r, n)
    bias_column = jnp.sum(spread[...].astype(wide) * bias[...], axis=1, keepdims=True)
    skip_part[...] = dot(forward_map, dens[...]) + bias_column
    for stream in range(STREAMS):
        all_of(1, stream, a2r).wait_recv()
        spectrum = added(a2r, stream).astype(low)
        kept[stream] = spectrum
        b1s[stream] = blocks_of(dot(mixer_back, spectrum) * scale, members)
        send_modes(2, stream, b1s, b1r, members)
    back_map = wide_map(((1,), (1,)))
    for stream in range(STREAMS):
        all_of(2, stream, b1r).wait_recv()
        b2s[stream] = blocks_of(dot(trans_back[...], flat(b1r, stream)), members)
        send_blocks(3, stream, b2s, b2r)
    for stream in range(STREAMS):

        def slope_block(device, cells):
            before = cells.astype(wide) + skip_part[rows(device), lanes(stream)]
            cotangent = upst[rows(device), lanes(stream)].astype(wide)
            c1s[stream, device] = (cotangent * gelu_slope(before)).astype(low)

        slope_block(member, b2s[stream, member])
        c1r[stream, member] = c1s[stream, member]

        def one_slope(step, carry):
            device = near(step)
            cells = b2r.at[stream, device]
            remote(
                3, stream, me, cells, cells, block_sem.at[stream, members - step]
            ).wait_recv()
            slope_block(device, cells[...])
            remote(
                4,
                stream,
                half * members + device,
                c1s.at[stream, device],
                c1r.at[stream, member],
            ).start()
            return carry

        lax.fori_loop(1, members, one_slope, 0)
    for stream in range(STREAMS):
        all_of(4, stream, c1r).wait_recv()
        c2s[stream] = blocks_of(dot(trans[...], flat(c1r, stream)), n)
        send_modes(5, stream, c2s, c2r, n)
    for stream in range(STREAMS):
        skip_part[:, lanes(stream)] = dot(back_map, flat(c1s, stream))
    skip_store = pltpu.make_async_copy(skip_part, out_skip, store_sem.at[0])
    skip_store.start()
    products = jnp.zeros((2 * channels, 2 * channels), wide)
    for stream in range(STREAMS):
        all_of(5, stream, c2r).wait_recv()
        gradient = (added(c2r, stream) * scale).astype(low)
        d1s[stream] = blocks_of(dot(mixer, gradient), members)
        send_modes(6, stream, d1s, d1r, members)
        products += dot(kept[stream], gradient, ((1,), (1,)))
    products = exact_dot(exact_dot(order[...].astype(wide), products), order_back[...].astype(wide))
    top, bottom = products[:channels], products[channels:]
    grad_real = top[:, :channels] + bottom[:, channels:]
    grad_imag = top[:, channels:] - bottom[:, :channels]
    theirs = jnp.where(is_first, grad_imag, grad_real)
    ours = jnp.where(is_first, grad_real, grad_imag)
    gsend[...] = jnp.concatenate([theirs, theirs], axis=1)
    swap_grad = pltpu.make_async_remote_copy(
        src_ref=gsend,
        dst_ref=grecv,
        send_sem=pair_send.at[1],
        recv_sem=pair_recv.at[1],
        device_id=(1 - core, me),
        device_id_type=MESH,
    )
    swap_grad.start()

    def own_store(stream):
        return pltpu.make_async_copy(
            d2s.at[stream, member],
            out_rows.at[rows(member), lanes(stream)],
            store_sem.at[1 + stream],
        )

    for stream in range(STREAMS):
        all_of(6, stream, d1r).wait_recv()
        d2s[stream] = blocks_of(dot(trans_back[...], flat(d1r, stream)), members)

        def send_last(shift, carry):
            peer = near(shift)
            remote(
                7,
                stream,
                half * members + peer,
                d2s.at[stream, peer],
                out_rows.at[rows(member), lanes(stream)],
            ).start()
            return carry

        lax.fori_loop(1, members, send_last, 0, unroll=True)
        own_store(stream).start()
    swap_grad.wait_recv()
    out_grad[...] = ours + grecv[...][:, :channels]
    swap.wait_send()
    swap_grad.wait_send()
    for stage, source in enumerate((a1r, a2r, b1r, b2r, c1r, c2r, d1r, d2s)):
        for stream in range(STREAMS):
            all_of(stage, stream, source).wait_send()
    skip_store.wait()
    for stream in range(STREAMS):
        own_store(stream).wait()
        all_of(7, stream, d2s).wait_recv()


def finish_kernel(
    rows_hbm,
    skip_hbm,
    grad_hbm,
    weight_hbm,
    first_hbm,
    second_hbm,
    out,
    new_weight,
    new_first,
    new_second,
    rows,
    skip,
    grad,
    weight,
    first,
    second,
    total,
    one,
    two,
    three,
    load_sem,
    store_sem,
):
    loads = [
        pltpu.make_async_copy(source, target, load_sem.at[index])
        for index, (source, target) in enumerate(
            (
                (grad_hbm, grad),
                (weight_hbm, weight),
                (first_hbm, first),
                (second_hbm, second),
                (rows_hbm, rows),
                (skip_hbm, skip),
            )
        )
    ]
    for load in loads:
        load.start()
    for load in loads[:4]:
        load.wait()
    one[...], two[...], three[...] = adam(grad[...], weight[...], first[...], second[...])
    stores = [
        pltpu.make_async_copy(source, target, store_sem.at[index])
        for index, (source, target) in enumerate(
            ((one, new_weight), (two, new_first), (three, new_second), (total, out))
        )
    ]
    for store in stores[:3]:
        store.start()
    for load in loads[4:]:
        load.wait()
    total[...] = (rows[...].astype(jnp.float32) + skip[...]).astype(total.dtype)
    stores[3].start()
    for store in stores:
        store.wait()


def one_frequency_each(
    n, density, upstream, spectral_weight, moment_one, moment_two, skip_weight, skip_bias, mode_counts
):
    samples, channels, slab_rows, line_count = density.shape
    members = n // HALVES
    own = channels // members
    width = line_count // STREAMS
    size = channels * slab_rows
    tables = fixed_tables(HALVES, members, own, slab_rows)
    low, wide = jnp.bfloat16, jnp.float32
    vmem = pl.BlockSpec(memory_space=pltpu.VMEM)
    hbm = pl.BlockSpec(memory_space=pltpu.HBM)
    cells = pltpu.VMEM((STREAMS, members, own * slab_rows, width), low)
    modes = pltpu.VMEM((STREAMS, n, 2 * own, width), low)
    mixed = pltpu.VMEM((STREAMS, members, 2 * own, width), low)
    arrays = (
        density.reshape(size, line_count),
        upstream.reshape(size, line_count),
        spectral_weight,
        skip_weight,
        skip_bias.reshape(1, channels),
    )
    input_rows, skip_back, weight_grad = pl.pallas_call(
        functools.partial(step_kernel, n),
        out_shape=(
            jax.ShapeDtypeStruct((size, line_count), low),
            jax.ShapeDtypeStruct((size, line_count), wide),
            jax.ShapeDtypeStruct((channels, channels), wide),
        ),
        in_specs=[hbm] * 5 + [pl.BlockSpec(memory_space=pltpu.SMEM)] + [hbm] * 4,
        out_specs=(hbm, hbm, vmem),
        scratch_shapes=[pltpu.VMEM(each.shape, each.dtype) for each in arrays]
        + [pltpu.VMEM((size, 2 * MODES * own), low)]
        + [pltpu.VMEM(each.shape, each.dtype) for each in tables[1:]]
        + [pltpu.VMEM((2 * MODES * own, size), low)]
        + [cells, modes, modes, mixed, modes, cells, cells]
        + [cells, cells, modes, modes, mixed, modes, cells]
        + [
            pltpu.VMEM((size, line_count), wide),
            pltpu.VMEM((STREAMS, 2 * channels, width), low),
            pltpu.VMEM((channels, 2 * channels), low),
            pltpu.VMEM((channels, 2 * channels), low),
            pltpu.VMEM((channels, 2 * channels), wide),
            pltpu.VMEM((channels, 2 * channels), wide),
            pltpu.SemaphoreType.DMA((8, STREAMS)),
            pltpu.SemaphoreType.DMA((8, STREAMS)),
            pltpu.SemaphoreType.DMA((STREAMS, members)),
            pltpu.SemaphoreType.DMA((2,)),
            pltpu.SemaphoreType.DMA((2,)),
            pltpu.SemaphoreType.DMA((8 + tables[0].shape[1],)),
            pltpu.SemaphoreType.DMA((1 + STREAMS,)),
        ],
        compiler_params=pltpu.CompilerParams(
            collective_id=0, has_side_effects=True, vmem_limit_bytes=60 * 1024 * 1024
        ),
        cost_estimate=pl.CostEstimate(
            flops=1_000_000_000, bytes_accessed=2_000_000, transcendentals=300_000
        ),
    )(*arrays, mode_counts, *tables)
    square = jax.ShapeDtypeStruct((channels, channels), wide)
    input_grad, *updated = pl.pallas_call(
        finish_kernel,
        out_shape=(jax.ShapeDtypeStruct((size, line_count), low), square, square, square),
        in_specs=[hbm] * 6,
        out_specs=(hbm,) * 4,
        scratch_shapes=[
            pltpu.VMEM((size, line_count), low),
            pltpu.VMEM((size, line_count), wide),
            *[pltpu.VMEM((channels, channels), wide)] * 4,
            pltpu.VMEM((size, line_count), low),
            *[pltpu.VMEM((channels, channels), wide)] * 3,
            pltpu.SemaphoreType.DMA((6,)),
            pltpu.SemaphoreType.DMA((4,)),
        ],
        compiler_params=pltpu.CompilerParams(vmem_limit_bytes=60 * 1024 * 1024),
        cost_estimate=pl.CostEstimate(flops=300_000, bytes_accessed=1_200_000, transcendentals=0),
    )(input_rows, skip_back, weight_grad, spectral_weight, moment_one, moment_two)
    return (input_grad.reshape(density.shape), *updated)


def adam(weight_grad, spectral_weight, moment_one, moment_two):
    new_moment_one = beta_first * moment_one + (1.0 - beta_first) * weight_grad
    new_moment_two = beta_second * moment_two + (1.0 - beta_second) * weight_grad * weight_grad
    first_hat = new_moment_one / (1.0 - beta_first**STEP)
    second_hat = new_moment_two / (1.0 - beta_second**STEP)
    new_weight = spectral_weight - learn_rate * (
        first_hat / (jnp.sqrt(second_hat) + epsilon) + decay_rate * spectral_weight
    )
    return (new_weight, new_moment_one, new_moment_two)


def on_mesh(density, *others):
    samples, channels, slab_rows, line_count = density.shape
    n, groups = lax.axis_size("dom"), lax.axis_size("dp")
    fits = (
        n == MODES
        and groups == 2
        and samples == 1
        and slab_rows == ROWS
        and n % HALVES == 0
        and 2 * (channels // (n // HALVES)) == 16
        and line_count % (128 * STREAMS) == 0
    )
    if fits:
        return one_frequency_each(n, density, *others)
    return on_device(density, *others)


def solution(mesh):
    placed = (
        P("dp", None, "dom", None),
        P("dp", None, "dom", None),
        P(("dp", "dom"), None),
        P(("dp", "dom"), None),
        P(("dp", "dom"), None),
        P(),
        P(),
        P(),
    )
    return jax.shard_map(
        on_mesh,
        mesh=mesh,
        in_specs=placed,
        out_specs=(
            P("dp", None, "dom", None),
            P(("dp", "dom"), None),
            P(("dp", "dom"), None),
            P(("dp", "dom"), None),
        ),
        check_vma=False,
    )
```

```python
import functools
import math

import jax
import jax.numpy as jnp
import numpy as np
from jax import lax
from jax.experimental import pallas as pl
from jax.experimental.pallas import tpu as pltpu
from jax.sharding import PartitionSpec as P

MODES = 16
STEP = 10


learn_rate = 0.01
beta_first = 0.9
beta_second = 0.95
decay_rate = 0.1
epsilon = 1e-08


def axis_parts(count_xdim):
    freq_list = jnp.arange(MODES, dtype=jnp.int32)
    cell_list = jnp.arange(count_xdim, dtype=jnp.int32)
    phases = (
        jnp.mod(freq_list[:, None] * cell_list[None, :], count_xdim).astype(jnp.float32)
        / count_xdim
    )
    angles = 2.0 * math.pi * phases
    scaling = 1.0 / math.sqrt(count_xdim)
    return (
        (jnp.cos(angles) * scaling).astype(jnp.bfloat16),
        (jnp.sin(angles) * scaling).astype(jnp.bfloat16),
    )


def doubling_table():
    return jnp.where(jnp.arange(MODES, dtype=jnp.int32) > 0, 2.0, 1.0).astype(jnp.float32)


def gelu_slope(values):
    cumulative = 0.5 * (1.0 + lax.erf(values * 0.7071067811865476))
    bell_curve = jnp.exp(-0.5 * values * values) * 0.3989422804014327
    return cumulative + values * bell_curve


def send_pencils(field):
    return lax.all_to_all(field, "dom", split_axis=3, concat_axis=2, tiled=True)


def send_slabs(field):
    return lax.all_to_all(field, "dom", split_axis=2, concat_axis=3, tiled=True)


def forward_parts(field, cosines, sines):
    real_part = jnp.einsum("scxl,fx->slcf", field, cosines, preferred_element_type=jnp.float32)
    imag_part = -jnp.einsum("scxl,fx->slcf", field, sines, preferred_element_type=jnp.float32)
    return (real_part, imag_part)


def inverse_cells(values_real, values_imag, cosines, sines):
    first = jnp.einsum("slcf,fx->scxl", values_real, cosines, preferred_element_type=jnp.float32)
    second = jnp.einsum("slcf,fx->scxl", values_imag, sines, preferred_element_type=jnp.float32)
    return (first - second).astype(jnp.bfloat16)


def on_device(
    density, upstream, spectral_weight, moment_one, moment_two, skip_weight, skip_bias, mode_counts
):
    samples, channels, slab_rows, line_count = density.shape
    count_xdim = slab_rows * lax.axis_size("dom")
    cosines, sines = axis_parts(count_xdim)
    doubling = doubling_table()
    doubling_low = doubling.astype(jnp.bfloat16)
    counts_here = lax.dynamic_slice_in_dim(mode_counts, lax.axis_index("dp") * samples, samples, 0)
    keep_modes = (jnp.arange(MODES, dtype=jnp.int32)[None, :] < counts_here[:, None]).astype(
        jnp.float32
    )
    keep_wide = keep_modes[:, None, None, :]
    weight_short = spectral_weight.astype(jnp.bfloat16)
    group_low = lax.all_gather(weight_short, "dom", axis=0, tiled=True)
    weight_low = lax.all_gather(group_low, "dp", axis=0, tiled=True)
    weight_low = weight_low.reshape(2, MODES, channels, channels)
    weight_real = weight_low[0]
    weight_imag = weight_low[1]
    density_lines = send_pencils(density)
    real_part, imag_part = forward_parts(density_lines, cosines, sines)
    spec_real = real_part.astype(jnp.bfloat16)
    spec_imag = imag_part.astype(jnp.bfloat16)
    form = "slcf,fco->slof"
    mixed_real = jnp.einsum(
        form, spec_real, weight_real, preferred_element_type=jnp.float32
    ) - jnp.einsum(form, spec_imag, weight_imag, preferred_element_type=jnp.float32)
    mixed_imag = jnp.einsum(
        form, spec_imag, weight_real, preferred_element_type=jnp.float32
    ) + jnp.einsum(form, spec_real, weight_imag, preferred_element_type=jnp.float32)
    mixed_real = (mixed_real * keep_wide).astype(jnp.bfloat16) * doubling_low
    mixed_imag = (mixed_imag * keep_wide).astype(jnp.bfloat16) * doubling_low
    back_lines = inverse_cells(mixed_real, mixed_imag, cosines, sines)
    back_rows = send_slabs(back_lines)
    skip_part = jnp.einsum(
        "oc,scxl->soxl", skip_weight, density, preferred_element_type=jnp.float32
    )
    before = back_rows.astype(jnp.float32) + skip_part + skip_bias[None, :, None, None]
    gate_grad = (upstream.astype(jnp.float32) * gelu_slope(before)).astype(jnp.bfloat16)
    gate_lines = send_pencils(gate_grad)
    grad_real, grad_imag = forward_parts(gate_lines, cosines, sines)
    scale = keep_wide * doubling
    grad_real = (grad_real * scale).astype(jnp.bfloat16)
    grad_imag = (grad_imag * scale).astype(jnp.bfloat16)
    outer = "slof,slcf->fco"
    part_real = jnp.einsum(
        outer, grad_real, spec_real, preferred_element_type=jnp.float32
    ) + jnp.einsum(outer, grad_imag, spec_imag, preferred_element_type=jnp.float32)
    part_imag = jnp.einsum(
        outer, grad_imag, spec_real, preferred_element_type=jnp.float32
    ) - jnp.einsum(outer, grad_real, spec_imag, preferred_element_type=jnp.float32)
    grad_local = jnp.stack([part_real, part_imag], 0).reshape(2 * MODES * channels, channels)
    group_grad = lax.psum_scatter(
        grad_local.astype(jnp.bfloat16), "dp", scatter_dimension=0, tiled=True
    ).astype(jnp.float32)
    weight_grad = lax.psum_scatter(group_grad, "dom", scatter_dimension=0, tiled=True)
    inner = "fco,slof->slcf"
    input_real = jnp.einsum(
        inner, weight_real, grad_real, preferred_element_type=jnp.float32
    ) + jnp.einsum(inner, weight_imag, grad_imag, preferred_element_type=jnp.float32)
    input_imag = jnp.einsum(
        inner, weight_real, grad_imag, preferred_element_type=jnp.float32
    ) - jnp.einsum(inner, weight_imag, grad_real, preferred_element_type=jnp.float32)
    input_lines = inverse_cells(
        input_real.astype(jnp.bfloat16), input_imag.astype(jnp.bfloat16), cosines, sines
    )
    input_rows = send_slabs(input_lines)
    skip_back = jnp.einsum(
        "oc,soxl->scxl", skip_weight, gate_grad, preferred_element_type=jnp.float32
    )
    input_grad = (input_rows.astype(jnp.float32) + skip_back).astype(jnp.bfloat16)
    new_moment_one = beta_first * moment_one + (1.0 - beta_first) * weight_grad
    new_moment_two = beta_second * moment_two + (1.0 - beta_second) * weight_grad * weight_grad
    first_hat = new_moment_one / (1.0 - beta_first**STEP)
    second_hat = new_moment_two / (1.0 - beta_second**STEP)
    new_weight = spectral_weight - learn_rate * (
        first_hat / (jnp.sqrt(second_hat) + epsilon) + decay_rate * spectral_weight
    )
    return (input_grad, new_weight, new_moment_one, new_moment_two)


MESH = pl.DeviceIdType.MESH
ROWS = 8
STREAMS = 2
HALVES = 2
LANES = 128


def fixed_tables(halves, members, own, rows):
    cells = halves * members * rows
    freq = np.arange(MODES)[:, None]
    angles = 2.0 * np.pi * ((freq * np.arange(cells)[None, :]) % cells) / cells
    scaling = 1.0 / math.sqrt(cells)
    parts = np.stack([np.cos(angles) * scaling, -np.sin(angles) * scaling], 1)
    parts = parts.reshape(MODES, 2, halves, members, rows).transpose(2, 3, 4, 0, 1)
    parts = parts.reshape(halves, members, 1, rows, MODES, 2, 1)
    same = np.eye(own).reshape(1, 1, own, 1, 1, 1, own)
    transform = (parts * same).reshape(halves, members * own * rows, -1, LANES)
    turned = transform.transpose(0, 2, 3, 1).reshape(halves, MODES * 2 * own, -1, LANES)
    transform, turned = transform.transpose(0, 2, 1, 3), turned.transpose(0, 2, 1, 3)
    channels = members * own
    order = np.zeros((2, members, own, members, 2, own))
    for part in range(2):
        for device in range(members):
            for one in range(own):
                order[part, device, one, device, part, one] = 1.0
    order = order.reshape(2 * channels, 2 * channels)
    spread = np.repeat(np.eye(channels), rows, axis=0)
    low = lambda table: jnp.asarray(table.astype(np.float32), jnp.bfloat16)
    return low(transform), low(turned), low(order), low(order.T), low(spread)


def dot(left, right, dims=((1,), (0,))):
    return lax.dot_general(left, right, (dims, ((), ())), preferred_element_type=jnp.float32)


def exact_dot(left, right):
    return jnp.dot(
        left, right, precision=lax.Precision.HIGHEST, preferred_element_type=jnp.float32
    )


def step_kernel(
    n,
    dens_hbm,
    upst_hbm,
    weight_hbm,
    skip_hbm,
    bias_hbm,
    counts,
    trans_back_hbm,
    trans_hbm,
    order_hbm,
    order_back_hbm,
    spread_hbm,
    out_rows,
    out_skip,
    out_grad,
    dens,
    upst,
    weight,
    skip,
    bias,
    trans_back,
    trans,
    order,
    order_back,
    spread,
    a1r,
    a2s,
    a2r,
    b1s,
    b1r,
    b2s,
    b2r,
    c1s,
    c1r,
    c2s,
    c2r,
    d1s,
    d1r,
    d2s,
    skip_part,
    kept,
    wsend,
    wrecv,
    gsend,
    grecv,
    send_sem,
    recv_sem,
    block_sem,
    pair_send,
    pair_recv,
    load_sem,
    store_sem,
):
    me = lax.axis_index("dom")
    core = lax.axis_index("dp")
    low, wide = jnp.bfloat16, jnp.float32
    members = n // HALVES
    half, member = me // members, lax.rem(me, members)
    block = dens.shape[0] // members
    width = dens.shape[1] // STREAMS
    channels = weight.shape[0]

    loads = [
        pltpu.make_async_copy(source, target, load_sem.at[index])
        for index, (source, target) in enumerate(
            (
                (dens_hbm, dens),
                (weight_hbm, weight),
                (skip_hbm, skip),
                (spread_hbm, spread),
                (bias_hbm, bias),
                (order_hbm, order),
                (order_back_hbm, order_back),
                *(
                    (trans_hbm.at[half, tile], trans.at[:, pl.ds(tile * LANES, LANES)])
                    for tile in range(trans_hbm.shape[1])
                ),
                *(
                    (trans_back_hbm.at[half, tile], trans_back.at[:, pl.ds(tile * LANES, LANES)])
                    for tile in range(trans_back_hbm.shape[1])
                ),
                (upst_hbm, upst),
            )
        )
    ]
    for load in loads:
        load.start()

    barrier = pltpu.get_barrier_semaphore()

    def greet(shift, carry):
        pl.semaphore_signal(
            barrier, inc=1, device_id=(core, lax.rem(me + shift, n)), device_id_type=MESH
        )
        return carry

    lax.fori_loop(1, n, greet, 0, unroll=True)
    pl.semaphore_signal(barrier, inc=1, device_id=(1 - core, me), device_id_type=MESH)
    pl.semaphore_wait(barrier, n)
    loads[0].wait()

    def remote(stage, stream, peer, source, target, arrival=None):
        return pltpu.make_async_remote_copy(
            src_ref=source,
            dst_ref=target,
            send_sem=send_sem.at[stage, stream],
            recv_sem=recv_sem.at[stage, stream] if arrival is None else arrival,
            device_id=(core, peer),
            device_id_type=MESH,
        )

    def send_modes(stage, stream, source, target, slots):
        def one(shift, carry):
            peer = lax.rem(me + shift, n)
            remote(
                stage,
                stream,
                peer,
                source.at[stream, lax.rem(peer, slots)],
                target.at[stream, me],
            ).start()
            return carry

        lax.fori_loop(1, n, one, 0, unroll=True)
        target[stream, me] = source[stream, lax.rem(me, slots)]

    def near(step):
        return lax.rem(member + step, members)

    def send_blocks(stage, stream, source, target):
        def one(shift, carry):
            peer = near(shift)
            remote(
                stage,
                stream,
                half * members + peer,
                source.at[stream, peer],
                target.at[stream, member],
                block_sem.at[stream, shift],
            ).start()
            return carry

        lax.fori_loop(1, members, one, 0, unroll=True)

    def all_of(stage, stream, ref):
        blocks = ref.at[stream, pl.ds(0, ref.shape[1] - 1)]
        return remote(stage, stream, me, blocks, blocks)

    def lanes(stream):
        return pl.ds(stream * width, width)

    def rows(device):
        return pl.ds(pl.multiple_of(device * block, block), block)

    for stream in range(STREAMS):

        def start_one(shift, carry):
            peer = near(shift)
            remote(
                0,
                stream,
                half * members + peer,
                dens.at[rows(peer), lanes(stream)],
                a1r.at[stream, member],
            ).start()
            return carry

        lax.fori_loop(1, members, start_one, 0, unroll=True)
        a1r[stream, member] = dens[rows(member), lanes(stream)]

    loads[1].wait()
    own_low = weight[...].astype(low)
    wsend[...] = jnp.concatenate([own_low, own_low], axis=1)
    swap = pltpu.make_async_remote_copy(
        src_ref=wsend,
        dst_ref=wrecv,
        send_sem=pair_send.at[0],
        recv_sem=pair_recv.at[0],
        device_id=(1 - core, me),
        device_id_type=MESH,
    )
    swap.start()
    for load in loads[2:]:
        load.wait()

    size = dens.shape[0]

    def wide_map(dims):
        same_row = lax.rem(lax.broadcasted_iota(jnp.int32, (size, size), 0), ROWS) == lax.rem(
            lax.broadcasted_iota(jnp.int32, (size, size), 1), ROWS
        )
        tall = dot(spread[...], skip[...], dims).astype(low)
        full = dot(tall, spread[...], ((1,), (1,)))
        return jnp.where(same_row, full, 0.0).astype(low)

    forward_map = wide_map(((1,), (0,)))
    swap.wait_recv()
    mine = weight[...].astype(low).astype(wide)
    other = wrecv[...].astype(wide)[:, :channels]
    is_first = core == 0
    weight_real = jnp.where(is_first, mine, other)
    weight_imag = jnp.where(is_first, other, mine)
    mixer = jnp.concatenate(
        [
            jnp.concatenate([weight_real, weight_imag], axis=1),
            jnp.concatenate([-weight_imag, weight_real], axis=1),
        ],
        axis=0,
    )
    mixer = dot(dot(order_back[...], mixer.astype(low)).astype(low), order[...])
    mixer_back = mixer.T.astype(low)
    mixer = mixer.astype(low)
    keep = jnp.where(me < counts[core], 1.0, 0.0)
    scale = keep * jnp.where(me == 0, 1.0, 2.0)

    def blocks_of(values, count):
        return values.astype(low).reshape(count, values.shape[0] // count, values.shape[1])

    def flat(ref, stream):
        values = ref[stream]
        return values.reshape(values.shape[0] * values.shape[1], values.shape[2])

    def added(ref, stream):
        values = ref[stream].astype(wide)
        total = values[:members]
        for other in range(1, HALVES):
            total += values[other * members : (other + 1) * members]
        return total.reshape(members * values.shape[1], values.shape[2])

    for stream in range(STREAMS):
        all_of(0, stream, a1r).wait_recv()
        a2s[stream] = blocks_of(dot(trans[...], flat(a1r, stream)), n)
        send_modes(1, stream, a2s, a2r, n)
    bias_column = jnp.sum(spread[...].astype(wide) * bias[...], axis=1, keepdims=True)
    skip_part[...] = dot(forward_map, dens[...]) + bias_column
    for stream in range(STREAMS):
        all_of(1, stream, a2r).wait_recv()
        spectrum = added(a2r, stream).astype(low)
        kept[stream] = spectrum
        b1s[stream] = blocks_of(dot(mixer_back, spectrum) * scale, members)
        send_modes(2, stream, b1s, b1r, members)
    back_map = wide_map(((1,), (1,)))
    for stream in range(STREAMS):
        all_of(2, stream, b1r).wait_recv()
        b2s[stream] = blocks_of(dot(trans_back[...], flat(b1r, stream)), members)
        send_blocks(3, stream, b2s, b2r)
    for stream in range(STREAMS):

        def slope_block(device, cells):
            before = cells.astype(wide) + skip_part[rows(device), lanes(stream)]
            cotangent = upst[rows(device), lanes(stream)].astype(wide)
            c1s[stream, device] = (cotangent * gelu_slope(before)).astype(low)

        slope_block(member, b2s[stream, member])
        c1r[stream, member] = c1s[stream, member]

        def one_slope(shift, carry):
            device = near(members - shift)
            cells = b2r.at[stream, device]
            remote(3, stream, me, cells, cells, block_sem.at[stream, shift]).wait_recv()
            slope_block(device, cells[...])
            remote(
                4,
                stream,
                half * members + device,
                c1s.at[stream, device],
                c1r.at[stream, member],
            ).start()
            return carry

        lax.fori_loop(1, members, one_slope, 0, unroll=True)
    for stream in range(STREAMS):
        all_of(4, stream, c1r).wait_recv()
        c2s[stream] = blocks_of(dot(trans[...], flat(c1r, stream)), n)
        send_modes(5, stream, c2s, c2r, n)
    for stream in range(STREAMS):
        skip_part[:, lanes(stream)] = dot(back_map, flat(c1s, stream))
    skip_store = pltpu.make_async_copy(skip_part, out_skip, store_sem.at[0])
    skip_store.start()
    products = jnp.zeros((2 * channels, 2 * channels), wide)
    for stream in range(STREAMS):
        all_of(5, stream, c2r).wait_recv()
        gradient = (added(c2r, stream) * scale).astype(low)
        d1s[stream] = blocks_of(dot(mixer, gradient), members)
        send_modes(6, stream, d1s, d1r, members)
        products += dot(kept[stream], gradient, ((1,), (1,)))
    products = exact_dot(exact_dot(order[...].astype(wide), products), order_back[...].astype(wide))
    top, bottom = products[:channels], products[channels:]
    grad_real = top[:, :channels] + bottom[:, channels:]
    grad_imag = top[:, channels:] - bottom[:, :channels]
    theirs = jnp.where(is_first, grad_imag, grad_real)
    ours = jnp.where(is_first, grad_real, grad_imag)
    gsend[...] = jnp.concatenate([theirs, theirs], axis=1)
    swap_grad = pltpu.make_async_remote_copy(
        src_ref=gsend,
        dst_ref=grecv,
        send_sem=pair_send.at[1],
        recv_sem=pair_recv.at[1],
        device_id=(1 - core, me),
        device_id_type=MESH,
    )
    swap_grad.start()

    def own_store(stream):
        return pltpu.make_async_copy(
            d2s.at[stream, member],
            out_rows.at[rows(member), lanes(stream)],
            store_sem.at[1 + stream],
        )

    for stream in range(STREAMS):
        all_of(6, stream, d1r).wait_recv()
        d2s[stream] = blocks_of(dot(trans_back[...], flat(d1r, stream)), members)

        def send_last(shift, carry):
            peer = near(shift)
            remote(
                7,
                stream,
                half * members + peer,
                d2s.at[stream, peer],
                out_rows.at[rows(member), lanes(stream)],
            ).start()
            return carry

        lax.fori_loop(1, members, send_last, 0, unroll=True)
        own_store(stream).start()
    swap_grad.wait_recv()
    out_grad[...] = ours + grecv[...][:, :channels]
    swap.wait_send()
    swap_grad.wait_send()
    for stage, source in enumerate((a1r, a2r, b1r, b2r, c1r, c2r, d1r, d2s)):
        for stream in range(STREAMS):
            all_of(stage, stream, source).wait_send()
    skip_store.wait()
    for stream in range(STREAMS):
        own_store(stream).wait()
        all_of(7, stream, d2s).wait_recv()


def finish_kernel(
    rows_hbm,
    skip_hbm,
    grad_hbm,
    weight_hbm,
    first_hbm,
    second_hbm,
    out,
    new_weight,
    new_first,
    new_second,
    rows,
    skip,
    grad,
    weight,
    first,
    second,
    total,
    one,
    two,
    three,
    load_sem,
    store_sem,
):
    loads = [
        pltpu.make_async_copy(source, target, load_sem.at[index])
        for index, (source, target) in enumerate(
            (
                (grad_hbm, grad),
                (weight_hbm, weight),
                (first_hbm, first),
                (second_hbm, second),
                (rows_hbm, rows),
                (skip_hbm, skip),
            )
        )
    ]
    for load in loads:
        load.start()
    for load in loads[:4]:
        load.wait()
    one[...], two[...], three[...] = adam(grad[...], weight[...], first[...], second[...])
    stores = [
        pltpu.make_async_copy(source, target, store_sem.at[index])
        for index, (source, target) in enumerate(
            ((one, new_weight), (two, new_first), (three, new_second), (total, out))
        )
    ]
    for store in stores[:3]:
        store.start()
    for load in loads[4:]:
        load.wait()
    total[...] = (rows[...].astype(jnp.float32) + skip[...]).astype(total.dtype)
    stores[3].start()
    for store in stores:
        store.wait()


def one_frequency_each(
    n, density, upstream, spectral_weight, moment_one, moment_two, skip_weight, skip_bias, mode_counts
):
    samples, channels, slab_rows, line_count = density.shape
    members = n // HALVES
    own = channels // members
    width = line_count // STREAMS
    size = channels * slab_rows
    tables = fixed_tables(HALVES, members, own, slab_rows)
    low, wide = jnp.bfloat16, jnp.float32
    vmem = pl.BlockSpec(memory_space=pltpu.VMEM)
    hbm = pl.BlockSpec(memory_space=pltpu.HBM)
    cells = pltpu.VMEM((STREAMS, members, own * slab_rows, width), low)
    modes = pltpu.VMEM((STREAMS, n, 2 * own, width), low)
    mixed = pltpu.VMEM((STREAMS, members, 2 * own, width), low)
    arrays = (
        density.reshape(size, line_count),
        upstream.reshape(size, line_count),
        spectral_weight,
        skip_weight,
        skip_bias.reshape(1, channels),
    )
    input_rows, skip_back, weight_grad = pl.pallas_call(
        functools.partial(step_kernel, n),
        out_shape=(
            jax.ShapeDtypeStruct((size, line_count), low),
            jax.ShapeDtypeStruct((size, line_count), wide),
            jax.ShapeDtypeStruct((channels, channels), wide),
        ),
        in_specs=[hbm] * 5 + [pl.BlockSpec(memory_space=pltpu.SMEM)] + [hbm] * 5,
        out_specs=(hbm, hbm, vmem),
        scratch_shapes=[pltpu.VMEM(each.shape, each.dtype) for each in arrays]
        + [pltpu.VMEM((size, 2 * MODES * own), low)]
        + [pltpu.VMEM((2 * MODES * own, size), low)]
        + [pltpu.VMEM(each.shape, each.dtype) for each in tables[2:]]
        + [cells, modes, modes, mixed, modes, cells, cells]
        + [cells, cells, modes, modes, mixed, modes, cells]
        + [
            pltpu.VMEM((size, line_count), wide),
            pltpu.VMEM((STREAMS, 2 * channels, width), low),
            pltpu.VMEM((channels, 2 * channels), low),
            pltpu.VMEM((channels, 2 * channels), low),
            pltpu.VMEM((channels, 2 * channels), wide),
            pltpu.VMEM((channels, 2 * channels), wide),
            pltpu.SemaphoreType.DMA((8, STREAMS)),
            pltpu.SemaphoreType.DMA((8, STREAMS)),
            pltpu.SemaphoreType.DMA((STREAMS, members)),
            pltpu.SemaphoreType.DMA((2,)),
            pltpu.SemaphoreType.DMA((2,)),
            pltpu.SemaphoreType.DMA((8 + tables[0].shape[1] + tables[1].shape[1],)),
            pltpu.SemaphoreType.DMA((1 + STREAMS,)),
        ],
        compiler_params=pltpu.CompilerParams(
            collective_id=0, has_side_effects=True, vmem_limit_bytes=60 * 1024 * 1024
        ),
        cost_estimate=pl.CostEstimate(
            flops=1_000_000_000, bytes_accessed=2_000_000, transcendentals=300_000
        ),
    )(*arrays, mode_counts, *tables)
    square = jax.ShapeDtypeStruct((channels, channels), wide)
    input_grad, *updated = pl.pallas_call(
        finish_kernel,
        out_shape=(jax.ShapeDtypeStruct((size, line_count), low), square, square, square),
        in_specs=[hbm] * 6,
        out_specs=(hbm,) * 4,
        scratch_shapes=[
            pltpu.VMEM((size, line_count), low),
            pltpu.VMEM((size, line_count), wide),
            *[pltpu.VMEM((channels, channels), wide)] * 4,
            pltpu.VMEM((size, line_count), low),
            *[pltpu.VMEM((channels, channels), wide)] * 3,
            pltpu.SemaphoreType.DMA((6,)),
            pltpu.SemaphoreType.DMA((4,)),
        ],
        compiler_params=pltpu.CompilerParams(vmem_limit_bytes=60 * 1024 * 1024),
        cost_estimate=pl.CostEstimate(flops=300_000, bytes_accessed=1_200_000, transcendentals=0),
    )(input_rows, skip_back, weight_grad, spectral_weight, moment_one, moment_two)
    return (input_grad.reshape(density.shape), *updated)


def adam(weight_grad, spectral_weight, moment_one, moment_two):
    new_moment_one = beta_first * moment_one + (1.0 - beta_first) * weight_grad
    new_moment_two = beta_second * moment_two + (1.0 - beta_second) * weight_grad * weight_grad
    first_hat = new_moment_one / (1.0 - beta_first**STEP)
    second_hat = new_moment_two / (1.0 - beta_second**STEP)
    new_weight = spectral_weight - learn_rate * (
        first_hat / (jnp.sqrt(second_hat) + epsilon) + decay_rate * spectral_weight
    )
    return (new_weight, new_moment_one, new_moment_two)


def on_mesh(density, *others):
    samples, channels, slab_rows, line_count = density.shape
    n, groups = lax.axis_size("dom"), lax.axis_size("dp")
    fits = (
        n == MODES
        and groups == 2
        and samples == 1
        and slab_rows == ROWS
        and n % HALVES == 0
        and 2 * (channels // (n // HALVES)) == 16
        and line_count % (128 * STREAMS) == 0
    )
    if fits:
        return one_frequency_each(n, density, *others)
    return on_device(density, *others)


def solution(mesh):
    placed = (
        P("dp", None, "dom", None),
        P("dp", None, "dom", None),
        P(("dp", "dom"), None),
        P(("dp", "dom"), None),
        P(("dp", "dom"), None),
        P(),
        P(),
        P(),
    )
    return jax.shard_map(
        on_mesh,
        mesh=mesh,
        in_specs=placed,
        out_specs=(
            P("dp", None, "dom", None),
            P(("dp", "dom"), None),
            P(("dp", "dom"), None),
            P(("dp", "dom"), None),
        ),
        check_vma=False,
    )
```

```python
import functools
import math

import jax
import jax.numpy as jnp
import numpy as np
from jax import lax
from jax.experimental import pallas as pl
from jax.experimental.pallas import tpu as pltpu
from jax.sharding import PartitionSpec as P

MODES = 16
STEP = 10


learn_rate = 0.01
beta_first = 0.9
beta_second = 0.95
decay_rate = 0.1
epsilon = 1e-08


def axis_parts(count_xdim):
    freq_list = jnp.arange(MODES, dtype=jnp.int32)
    cell_list = jnp.arange(count_xdim, dtype=jnp.int32)
    phases = (
        jnp.mod(freq_list[:, None] * cell_list[None, :], count_xdim).astype(jnp.float32)
        / count_xdim
    )
    angles = 2.0 * math.pi * phases
    scaling = 1.0 / math.sqrt(count_xdim)
    return (
        (jnp.cos(angles) * scaling).astype(jnp.bfloat16),
        (jnp.sin(angles) * scaling).astype(jnp.bfloat16),
    )


def doubling_table():
    return jnp.where(jnp.arange(MODES, dtype=jnp.int32) > 0, 2.0, 1.0).astype(jnp.float32)


def gelu_slope(values):
    cumulative = 0.5 * (1.0 + lax.erf(values * 0.7071067811865476))
    bell_curve = jnp.exp(-0.5 * values * values) * 0.3989422804014327
    return cumulative + values * bell_curve


def send_pencils(field):
    return lax.all_to_all(field, "dom", split_axis=3, concat_axis=2, tiled=True)


def send_slabs(field):
    return lax.all_to_all(field, "dom", split_axis=2, concat_axis=3, tiled=True)


def forward_parts(field, cosines, sines):
    real_part = jnp.einsum("scxl,fx->slcf", field, cosines, preferred_element_type=jnp.float32)
    imag_part = -jnp.einsum("scxl,fx->slcf", field, sines, preferred_element_type=jnp.float32)
    return (real_part, imag_part)


def inverse_cells(values_real, values_imag, cosines, sines):
    first = jnp.einsum("slcf,fx->scxl", values_real, cosines, preferred_element_type=jnp.float32)
    second = jnp.einsum("slcf,fx->scxl", values_imag, sines, preferred_element_type=jnp.float32)
    return (first - second).astype(jnp.bfloat16)


def on_device(
    density, upstream, spectral_weight, moment_one, moment_two, skip_weight, skip_bias, mode_counts
):
    samples, channels, slab_rows, line_count = density.shape
    count_xdim = slab_rows * lax.axis_size("dom")
    cosines, sines = axis_parts(count_xdim)
    doubling = doubling_table()
    doubling_low = doubling.astype(jnp.bfloat16)
    counts_here = lax.dynamic_slice_in_dim(mode_counts, lax.axis_index("dp") * samples, samples, 0)
    keep_modes = (jnp.arange(MODES, dtype=jnp.int32)[None, :] < counts_here[:, None]).astype(
        jnp.float32
    )
    keep_wide = keep_modes[:, None, None, :]
    weight_short = spectral_weight.astype(jnp.bfloat16)
    group_low = lax.all_gather(weight_short, "dom", axis=0, tiled=True)
    weight_low = lax.all_gather(group_low, "dp", axis=0, tiled=True)
    weight_low = weight_low.reshape(2, MODES, channels, channels)
    weight_real = weight_low[0]
    weight_imag = weight_low[1]
    density_lines = send_pencils(density)
    real_part, imag_part = forward_parts(density_lines, cosines, sines)
    spec_real = real_part.astype(jnp.bfloat16)
    spec_imag = imag_part.astype(jnp.bfloat16)
    form = "slcf,fco->slof"
    mixed_real = jnp.einsum(
        form, spec_real, weight_real, preferred_element_type=jnp.float32
    ) - jnp.einsum(form, spec_imag, weight_imag, preferred_element_type=jnp.float32)
    mixed_imag = jnp.einsum(
        form, spec_imag, weight_real, preferred_element_type=jnp.float32
    ) + jnp.einsum(form, spec_real, weight_imag, preferred_element_type=jnp.float32)
    mixed_real = (mixed_real * keep_wide).astype(jnp.bfloat16) * doubling_low
    mixed_imag = (mixed_imag * keep_wide).astype(jnp.bfloat16) * doubling_low
    back_lines = inverse_cells(mixed_real, mixed_imag, cosines, sines)
    back_rows = send_slabs(back_lines)
    skip_part = jnp.einsum(
        "oc,scxl->soxl", skip_weight, density, preferred_element_type=jnp.float32
    )
    before = back_rows.astype(jnp.float32) + skip_part + skip_bias[None, :, None, None]
    gate_grad = (upstream.astype(jnp.float32) * gelu_slope(before)).astype(jnp.bfloat16)
    gate_lines = send_pencils(gate_grad)
    grad_real, grad_imag = forward_parts(gate_lines, cosines, sines)
    scale = keep_wide * doubling
    grad_real = (grad_real * scale).astype(jnp.bfloat16)
    grad_imag = (grad_imag * scale).astype(jnp.bfloat16)
    outer = "slof,slcf->fco"
    part_real = jnp.einsum(
        outer, grad_real, spec_real, preferred_element_type=jnp.float32
    ) + jnp.einsum(outer, grad_imag, spec_imag, preferred_element_type=jnp.float32)
    part_imag = jnp.einsum(
        outer, grad_imag, spec_real, preferred_element_type=jnp.float32
    ) - jnp.einsum(outer, grad_real, spec_imag, preferred_element_type=jnp.float32)
    grad_local = jnp.stack([part_real, part_imag], 0).reshape(2 * MODES * channels, channels)
    group_grad = lax.psum_scatter(
        grad_local.astype(jnp.bfloat16), "dp", scatter_dimension=0, tiled=True
    ).astype(jnp.float32)
    weight_grad = lax.psum_scatter(group_grad, "dom", scatter_dimension=0, tiled=True)
    inner = "fco,slof->slcf"
    input_real = jnp.einsum(
        inner, weight_real, grad_real, preferred_element_type=jnp.float32
    ) + jnp.einsum(inner, weight_imag, grad_imag, preferred_element_type=jnp.float32)
    input_imag = jnp.einsum(
        inner, weight_real, grad_imag, preferred_element_type=jnp.float32
    ) - jnp.einsum(inner, weight_imag, grad_real, preferred_element_type=jnp.float32)
    input_lines = inverse_cells(
        input_real.astype(jnp.bfloat16), input_imag.astype(jnp.bfloat16), cosines, sines
    )
    input_rows = send_slabs(input_lines)
    skip_back = jnp.einsum(
        "oc,soxl->scxl", skip_weight, gate_grad, preferred_element_type=jnp.float32
    )
    input_grad = (input_rows.astype(jnp.float32) + skip_back).astype(jnp.bfloat16)
    new_moment_one = beta_first * moment_one + (1.0 - beta_first) * weight_grad
    new_moment_two = beta_second * moment_two + (1.0 - beta_second) * weight_grad * weight_grad
    first_hat = new_moment_one / (1.0 - beta_first**STEP)
    second_hat = new_moment_two / (1.0 - beta_second**STEP)
    new_weight = spectral_weight - learn_rate * (
        first_hat / (jnp.sqrt(second_hat) + epsilon) + decay_rate * spectral_weight
    )
    return (input_grad, new_weight, new_moment_one, new_moment_two)


MESH = pl.DeviceIdType.MESH
ROWS = 8
STREAMS = 2
HALVES = 2
LANES = 128
CHUNKS = 4


def fixed_tables(halves, members, own, rows):
    cells = halves * members * rows
    freq = np.arange(MODES)[:, None]
    angles = 2.0 * np.pi * ((freq * np.arange(cells)[None, :]) % cells) / cells
    scaling = 1.0 / math.sqrt(cells)
    parts = np.stack([np.cos(angles) * scaling, -np.sin(angles) * scaling], 1)
    parts = parts.reshape(MODES, 2, halves, members, rows).transpose(2, 3, 4, 0, 1)
    parts = parts.reshape(halves, members, 1, rows, MODES, 2, 1)
    same = np.eye(own).reshape(1, 1, own, 1, 1, 1, own)
    transform = (parts * same).reshape(halves, members * own * rows, -1, LANES)
    transform = transform.transpose(0, 2, 1, 3)
    channels = members * own
    order = np.zeros((2, members, own, members, 2, own))
    for part in range(2):
        for device in range(members):
            for one in range(own):
                order[part, device, one, device, part, one] = 1.0
    order = order.reshape(2 * channels, 2 * channels)
    spread = np.repeat(np.eye(channels), rows, axis=0)
    low = lambda table: jnp.asarray(table.astype(np.float32), jnp.bfloat16)
    return low(transform), low(order), low(order.T), low(spread)


def dot(left, right, dims=((1,), (0,))):
    return lax.dot_general(left, right, (dims, ((), ())), preferred_element_type=jnp.float32)


def exact_dot(left, right):
    return jnp.dot(
        left, right, precision=lax.Precision.HIGHEST, preferred_element_type=jnp.float32
    )


def step_kernel(
    n,
    dens_hbm,
    upst_hbm,
    weight_hbm,
    skip_hbm,
    bias_hbm,
    counts,
    trans_back_hbm,
    order_hbm,
    order_back_hbm,
    spread_hbm,
    out_rows,
    out_skip,
    out_grad,
    dens,
    upst,
    weight,
    skip,
    bias,
    trans_back,
    order,
    order_back,
    spread,
    trans,
    a1r,
    a2s,
    a2r,
    b1s,
    b1r,
    b2s,
    b2r,
    c1s,
    c1r,
    c2s,
    c2r,
    d1s,
    d1r,
    d2s,
    skip_part,
    kept,
    wsend,
    wrecv,
    gsend,
    grecv,
    send_sem,
    recv_sem,
    block_sem,
    pair_send,
    pair_recv,
    load_sem,
    store_sem,
):
    me = lax.axis_index("dom")
    core = lax.axis_index("dp")
    low, wide = jnp.bfloat16, jnp.float32
    members = n // HALVES
    half, member = me // members, lax.rem(me, members)
    block = dens.shape[0] // members
    width = dens.shape[1] // STREAMS
    channels = weight.shape[0]

    loads = [
        pltpu.make_async_copy(source, target, load_sem.at[index])
        for index, (source, target) in enumerate(
            (
                (dens_hbm, dens),
                (weight_hbm, weight),
                (skip_hbm, skip),
                (spread_hbm, spread),
                (bias_hbm, bias),
                (order_hbm, order),
                (order_back_hbm, order_back),
                *(
                    (trans_back_hbm.at[half, tile], trans_back.at[:, pl.ds(tile * LANES, LANES)])
                    for tile in range(trans_back_hbm.shape[1])
                ),
                (upst_hbm, upst),
            )
        )
    ]
    for load in loads:
        load.start()

    barrier = pltpu.get_barrier_semaphore()

    def greet(shift, carry):
        pl.semaphore_signal(
            barrier, inc=1, device_id=(core, lax.rem(me + shift, n)), device_id_type=MESH
        )
        return carry

    lax.fori_loop(1, n, greet, 0, unroll=True)
    pl.semaphore_signal(barrier, inc=1, device_id=(1 - core, me), device_id_type=MESH)
    pl.semaphore_wait(barrier, n)
    loads[0].wait()

    def remote(stage, stream, peer, source, target, arrival=None):
        return pltpu.make_async_remote_copy(
            src_ref=source,
            dst_ref=target,
            send_sem=send_sem.at[stage, stream],
            recv_sem=recv_sem.at[stage, stream] if arrival is None else arrival,
            device_id=(core, peer),
            device_id_type=MESH,
        )

    def send_modes(stage, stream, source, target, slots):
        def one(shift, carry):
            peer = lax.rem(me + shift, n)
            remote(
                stage,
                stream,
                peer,
                source.at[stream, lax.rem(peer, slots)],
                target.at[stream, me],
            ).start()
            return carry

        lax.fori_loop(1, n, one, 0, unroll=True)
        target[stream, me] = source[stream, lax.rem(me, slots)]

    def near(step):
        return lax.rem(member + step, members)

    def send_blocks(stage, stream, source, target):
        def one(shift, carry):
            peer = near(shift)
            remote(
                stage,
                stream,
                half * members + peer,
                source.at[stream, peer],
                target.at[stream, member],
                block_sem.at[stream, shift],
            ).start()
            return carry

        lax.fori_loop(1, members, one, 0, unroll=True)

    def all_of(stage, stream, ref):
        blocks = ref.at[stream, pl.ds(0, ref.shape[1] - 1)]
        return remote(stage, stream, me, blocks, blocks)

    def lanes(stream):
        return pl.ds(stream * width, width)

    def rows(device):
        return pl.ds(pl.multiple_of(device * block, block), block)

    for stream in range(STREAMS):

        def start_one(shift, carry):
            peer = near(shift)
            remote(
                0,
                stream,
                half * members + peer,
                dens.at[rows(peer), lanes(stream)],
                a1r.at[stream, member],
            ).start()
            return carry

        lax.fori_loop(1, members, start_one, 0, unroll=True)
        a1r[stream, member] = dens[rows(member), lanes(stream)]

    loads[1].wait()
    own_low = weight[...].astype(low)
    wsend[...] = jnp.concatenate([own_low, own_low], axis=1)
    swap = pltpu.make_async_remote_copy(
        src_ref=wsend,
        dst_ref=wrecv,
        send_sem=pair_send.at[0],
        recv_sem=pair_recv.at[0],
        device_id=(1 - core, me),
        device_id_type=MESH,
    )
    swap.start()
    for load in loads[2:]:
        load.wait()

    size = dens.shape[0]

    def wide_map(dims):
        same_row = lax.rem(lax.broadcasted_iota(jnp.int32, (size, size), 0), ROWS) == lax.rem(
            lax.broadcasted_iota(jnp.int32, (size, size), 1), ROWS
        )
        tall = dot(spread[...], skip[...], dims).astype(low)
        full = dot(tall, spread[...], ((1,), (1,)))
        return jnp.where(same_row, full, 0.0).astype(low)

    trans[...] = trans_back[...].astype(wide).T.astype(low)
    forward_map = wide_map(((1,), (0,)))
    swap.wait_recv()
    mine = weight[...].astype(low).astype(wide)
    other = wrecv[...].astype(wide)[:, :channels]
    is_first = core == 0
    weight_real = jnp.where(is_first, mine, other)
    weight_imag = jnp.where(is_first, other, mine)
    mixer = jnp.concatenate(
        [
            jnp.concatenate([weight_real, weight_imag], axis=1),
            jnp.concatenate([-weight_imag, weight_real], axis=1),
        ],
        axis=0,
    )
    mixer = dot(dot(order_back[...], mixer.astype(low)).astype(low), order[...])
    mixer_back = mixer.T.astype(low)
    mixer = mixer.astype(low)
    keep = jnp.where(me < counts[core], 1.0, 0.0)
    scale = keep * jnp.where(me == 0, 1.0, 2.0)

    def blocks_of(values, count):
        return values.astype(low).reshape(count, values.shape[0] // count, values.shape[1])

    def flat(ref, stream):
        values = ref[stream]
        return values.reshape(values.shape[0] * values.shape[1], values.shape[2])

    def added(ref, stream):
        values = ref[stream].astype(wide)
        total = values[:members]
        for other in range(1, HALVES):
            total += values[other * members : (other + 1) * members]
        return total.reshape(members * values.shape[1], values.shape[2])

    for stream in range(STREAMS):
        all_of(0, stream, a1r).wait_recv()
        a2s[stream] = blocks_of(dot(trans[...], flat(a1r, stream)), n)
        send_modes(1, stream, a2s, a2r, n)
    bias_column = jnp.sum(spread[...].astype(wide) * bias[...], axis=1, keepdims=True)
    skip_part[...] = dot(forward_map, dens[...]) + bias_column
    for stream in range(STREAMS):
        all_of(1, stream, a2r).wait_recv()
        spectrum = added(a2r, stream).astype(low)
        kept[stream] = spectrum
        b1s[stream] = blocks_of(dot(mixer_back, spectrum) * scale, members)
        send_modes(2, stream, b1s, b1r, members)
    back_map = wide_map(((1,), (1,)))
    for stream in range(STREAMS):
        all_of(2, stream, b1r).wait_recv()
        b2s[stream] = blocks_of(dot(trans_back[...], flat(b1r, stream)), members)
        send_blocks(3, stream, b2s, b2r)
    for stream in range(STREAMS):

        def slope_block(device, cells):
            before = cells.astype(wide) + skip_part[rows(device), lanes(stream)]
            cotangent = upst[rows(device), lanes(stream)].astype(wide)
            c1s[stream, device] = (cotangent * gelu_slope(before)).astype(low)

        slope_block(member, b2s[stream, member])
        c1r[stream, member] = c1s[stream, member]

        def one_slope(shift, carry):
            device = near(members - shift)
            cells = b2r.at[stream, device]
            remote(3, stream, me, cells, cells, block_sem.at[stream, shift]).wait_recv()
            slope_block(device, cells[...])
            remote(
                4,
                stream,
                half * members + device,
                c1s.at[stream, device],
                c1r.at[stream, member],
            ).start()
            return carry

        lax.fori_loop(1, members, one_slope, 0)
    for stream in range(STREAMS):
        all_of(4, stream, c1r).wait_recv()
        c2s[stream] = blocks_of(dot(trans[...], flat(c1r, stream)), n)
        send_modes(5, stream, c2s, c2r, n)
    for stream in range(STREAMS):
        skip_part[:, lanes(stream)] = dot(back_map, flat(c1s, stream))
    skip_store = pltpu.make_async_copy(skip_part, out_skip, store_sem.at[0])
    skip_store.start()
    products = jnp.zeros((2 * channels, 2 * channels), wide)
    for stream in range(STREAMS):
        all_of(5, stream, c2r).wait_recv()
        gradient = (added(c2r, stream) * scale).astype(low)
        d1s[stream] = blocks_of(dot(mixer, gradient), members)
        send_modes(6, stream, d1s, d1r, members)
        products += dot(kept[stream], gradient, ((1,), (1,)))
    products = exact_dot(exact_dot(order[...].astype(wide), products), order_back[...].astype(wide))
    top, bottom = products[:channels], products[channels:]
    grad_real = top[:, :channels] + bottom[:, channels:]
    grad_imag = top[:, channels:] - bottom[:, :channels]
    theirs = jnp.where(is_first, grad_imag, grad_real)
    ours = jnp.where(is_first, grad_real, grad_imag)
    gsend[...] = jnp.concatenate([theirs, theirs], axis=1)
    swap_grad = pltpu.make_async_remote_copy(
        src_ref=gsend,
        dst_ref=grecv,
        send_sem=pair_send.at[1],
        recv_sem=pair_recv.at[1],
        device_id=(1 - core, me),
        device_id_type=MESH,
    )
    swap_grad.start()

    def own_store(stream):
        return pltpu.make_async_copy(
            d2s.at[stream, member],
            out_rows.at[rows(member), lanes(stream)],
            store_sem.at[1 + stream],
        )

    for stream in range(STREAMS):
        all_of(6, stream, d1r).wait_recv()
        d2s[stream] = blocks_of(dot(trans_back[...], flat(d1r, stream)), members)

        def send_last(shift, carry):
            peer = near(shift)
            remote(
                7,
                stream,
                half * members + peer,
                d2s.at[stream, peer],
                out_rows.at[rows(member), lanes(stream)],
            ).start()
            return carry

        lax.fori_loop(1, members, send_last, 0, unroll=True)
        own_store(stream).start()
    swap_grad.wait_recv()
    out_grad[...] = ours + grecv[...][:, :channels]
    swap.wait_send()
    swap_grad.wait_send()
    for stage, source in enumerate((a1r, a2r, b1r, b2r, c1r, c2r, d1r, d2s)):
        for stream in range(STREAMS):
            all_of(stage, stream, source).wait_send()
    skip_store.wait()
    for stream in range(STREAMS):
        own_store(stream).wait()
        all_of(7, stream, d2s).wait_recv()


def finish_kernel(
    rows_hbm,
    skip_hbm,
    grad_hbm,
    weight_hbm,
    first_hbm,
    second_hbm,
    out,
    new_weight,
    new_first,
    new_second,
    rows,
    skip,
    grad,
    weight,
    first,
    second,
    total,
    one,
    two,
    three,
    load_sem,
    store_sem,
):
    loads = [
        pltpu.make_async_copy(source, target, load_sem.at[index])
        for index, (source, target) in enumerate(
            (
                (grad_hbm, grad),
                (weight_hbm, weight),
                (first_hbm, first),
                (second_hbm, second),
            )
        )
    ]
    step = rows.shape[0] // CHUNKS
    parts = [pl.ds(chunk * step, step) for chunk in range(CHUNKS)]
    row_loads = [
        [
            pltpu.make_async_copy(source.at[part], target.at[part], load_sem.at[4 + 2 * chunk + k])
            for k, (source, target) in enumerate(((rows_hbm, rows), (skip_hbm, skip)))
        ]
        for chunk, part in enumerate(parts)
    ]
    row_stores = [
        pltpu.make_async_copy(total.at[part], out.at[part], store_sem.at[3 + chunk])
        for chunk, part in enumerate(parts)
    ]
    for load in loads + [each for pair in row_loads for each in pair]:
        load.start()
    for part, pair, store in zip(parts, row_loads, row_stores):
        for load in pair:
            load.wait()
        total[part] = (rows[part].astype(jnp.float32) + skip[part]).astype(total.dtype)
        store.start()
    for load in loads:
        load.wait()
    one[...], two[...], three[...] = adam(grad[...], weight[...], first[...], second[...])
    stores = [
        pltpu.make_async_copy(source, target, store_sem.at[index])
        for index, (source, target) in enumerate(
            ((one, new_weight), (two, new_first), (three, new_second))
        )
    ]
    for store in stores:
        store.start()
    for store in row_stores + stores:
        store.wait()


def one_frequency_each(
    n, density, upstream, spectral_weight, moment_one, moment_two, skip_weight, skip_bias, mode_counts
):
    samples, channels, slab_rows, line_count = density.shape
    members = n // HALVES
    own = channels // members
    width = line_count // STREAMS
    size = channels * slab_rows
    tables = fixed_tables(HALVES, members, own, slab_rows)
    low, wide = jnp.bfloat16, jnp.float32
    vmem = pl.BlockSpec(memory_space=pltpu.VMEM)
    hbm = pl.BlockSpec(memory_space=pltpu.HBM)
    cells = pltpu.VMEM((STREAMS, members, own * slab_rows, width), low)
    modes = pltpu.VMEM((STREAMS, n, 2 * own, width), low)
    mixed = pltpu.VMEM((STREAMS, members, 2 * own, width), low)
    arrays = (
        density.reshape(size, line_count),
        upstream.reshape(size, line_count),
        spectral_weight,
        skip_weight,
        skip_bias.reshape(1, channels),
    )
    input_rows, skip_back, weight_grad = pl.pallas_call(
        functools.partial(step_kernel, n),
        out_shape=(
            jax.ShapeDtypeStruct((size, line_count), low),
            jax.ShapeDtypeStruct((size, line_count), wide),
            jax.ShapeDtypeStruct((channels, channels), wide),
        ),
        in_specs=[hbm] * 5 + [pl.BlockSpec(memory_space=pltpu.SMEM)] + [hbm] * 4,
        out_specs=(hbm, hbm, vmem),
        scratch_shapes=[pltpu.VMEM(each.shape, each.dtype) for each in arrays]
        + [pltpu.VMEM((size, 2 * MODES * own), low)]
        + [pltpu.VMEM(each.shape, each.dtype) for each in tables[1:]]
        + [pltpu.VMEM((2 * MODES * own, size), low)]
        + [cells, modes, modes, mixed, modes, cells, cells]
        + [cells, cells, modes, modes, mixed, modes, cells]
        + [
            pltpu.VMEM((size, line_count), wide),
            pltpu.VMEM((STREAMS, 2 * channels, width), low),
            pltpu.VMEM((channels, 2 * channels), low),
            pltpu.VMEM((channels, 2 * channels), low),
            pltpu.VMEM((channels, 2 * channels), wide),
            pltpu.VMEM((channels, 2 * channels), wide),
            pltpu.SemaphoreType.DMA((8, STREAMS)),
            pltpu.SemaphoreType.DMA((8, STREAMS)),
            pltpu.SemaphoreType.DMA((STREAMS, members)),
            pltpu.SemaphoreType.DMA((2,)),
            pltpu.SemaphoreType.DMA((2,)),
            pltpu.SemaphoreType.DMA((8 + tables[0].shape[1],)),
            pltpu.SemaphoreType.DMA((1 + STREAMS,)),
        ],
        compiler_params=pltpu.CompilerParams(
            collective_id=0, has_side_effects=True, vmem_limit_bytes=60 * 1024 * 1024
        ),
        cost_estimate=pl.CostEstimate(
            flops=1_000_000_000, bytes_accessed=2_000_000, transcendentals=300_000
        ),
    )(*arrays, mode_counts, *tables)
    square = jax.ShapeDtypeStruct((channels, channels), wide)
    input_grad, *updated = pl.pallas_call(
        finish_kernel,
        out_shape=(jax.ShapeDtypeStruct((size, line_count), low), square, square, square),
        in_specs=[hbm] * 6,
        out_specs=(hbm,) * 4,
        scratch_shapes=[
            pltpu.VMEM((size, line_count), low),
            pltpu.VMEM((size, line_count), wide),
            *[pltpu.VMEM((channels, channels), wide)] * 4,
            pltpu.VMEM((size, line_count), low),
            *[pltpu.VMEM((channels, channels), wide)] * 3,
            pltpu.SemaphoreType.DMA((4 + 2 * CHUNKS,)),
            pltpu.SemaphoreType.DMA((3 + CHUNKS,)),
        ],
        compiler_params=pltpu.CompilerParams(vmem_limit_bytes=60 * 1024 * 1024),
        cost_estimate=pl.CostEstimate(flops=300_000, bytes_accessed=1_200_000, transcendentals=0),
    )(input_rows, skip_back, weight_grad, spectral_weight, moment_one, moment_two)
    return (input_grad.reshape(density.shape), *updated)


def adam(weight_grad, spectral_weight, moment_one, moment_two):
    new_moment_one = beta_first * moment_one + (1.0 - beta_first) * weight_grad
    new_moment_two = beta_second * moment_two + (1.0 - beta_second) * weight_grad * weight_grad
    first_hat = new_moment_one / (1.0 - beta_first**STEP)
    second_hat = new_moment_two / (1.0 - beta_second**STEP)
    new_weight = spectral_weight - learn_rate * (
        first_hat / (jnp.sqrt(second_hat) + epsilon) + decay_rate * spectral_weight
    )
    return (new_weight, new_moment_one, new_moment_two)


def on_mesh(density, *others):
    samples, channels, slab_rows, line_count = density.shape
    n, groups = lax.axis_size("dom"), lax.axis_size("dp")
    fits = (
        n == MODES
        and groups == 2
        and samples == 1
        and slab_rows == ROWS
        and n % HALVES == 0
        and 2 * (channels // (n // HALVES)) == 16
        and line_count % (128 * STREAMS) == 0
    )
    if fits:
        return one_frequency_each(n, density, *others)
    return on_device(density, *others)


def solution(mesh):
    placed = (
        P("dp", None, "dom", None),
        P("dp", None, "dom", None),
        P(("dp", "dom"), None),
        P(("dp", "dom"), None),
        P(("dp", "dom"), None),
        P(),
        P(),
        P(),
    )
    return jax.shard_map(
        on_mesh,
        mesh=mesh,
        in_specs=placed,
        out_specs=(
            P("dp", None, "dom", None),
            P(("dp", "dom"), None),
            P(("dp", "dom"), None),
            P(("dp", "dom"), None),
        ),
        check_vma=False,
    )
```

```python
import functools
import math

import jax
import jax.numpy as jnp
import numpy as np
from jax import lax
from jax.experimental import pallas as pl
from jax.experimental.pallas import tpu as pltpu
from jax.sharding import PartitionSpec as P

MODES = 16
STEP = 10


learn_rate = 0.01
beta_first = 0.9
beta_second = 0.95
decay_rate = 0.1
epsilon = 1e-08


def axis_parts(count_xdim):
    freq_list = jnp.arange(MODES, dtype=jnp.int32)
    cell_list = jnp.arange(count_xdim, dtype=jnp.int32)
    phases = (
        jnp.mod(freq_list[:, None] * cell_list[None, :], count_xdim).astype(jnp.float32)
        / count_xdim
    )
    angles = 2.0 * math.pi * phases
    scaling = 1.0 / math.sqrt(count_xdim)
    return (
        (jnp.cos(angles) * scaling).astype(jnp.bfloat16),
        (jnp.sin(angles) * scaling).astype(jnp.bfloat16),
    )


def doubling_table():
    return jnp.where(jnp.arange(MODES, dtype=jnp.int32) > 0, 2.0, 1.0).astype(jnp.float32)


def gelu_slope(values):
    cumulative = 0.5 * (1.0 + lax.erf(values * 0.7071067811865476))
    bell_curve = jnp.exp(-0.5 * values * values) * 0.3989422804014327
    return cumulative + values * bell_curve


def send_pencils(field):
    return lax.all_to_all(field, "dom", split_axis=3, concat_axis=2, tiled=True)


def send_slabs(field):
    return lax.all_to_all(field, "dom", split_axis=2, concat_axis=3, tiled=True)


def forward_parts(field, cosines, sines):
    real_part = jnp.einsum("scxl,fx->slcf", field, cosines, preferred_element_type=jnp.float32)
    imag_part = -jnp.einsum("scxl,fx->slcf", field, sines, preferred_element_type=jnp.float32)
    return (real_part, imag_part)


def inverse_cells(values_real, values_imag, cosines, sines):
    first = jnp.einsum("slcf,fx->scxl", values_real, cosines, preferred_element_type=jnp.float32)
    second = jnp.einsum("slcf,fx->scxl", values_imag, sines, preferred_element_type=jnp.float32)
    return (first - second).astype(jnp.bfloat16)


def on_device(
    density, upstream, spectral_weight, moment_one, moment_two, skip_weight, skip_bias, mode_counts
):
    samples, channels, slab_rows, line_count = density.shape
    count_xdim = slab_rows * lax.axis_size("dom")
    cosines, sines = axis_parts(count_xdim)
    doubling = doubling_table()
    doubling_low = doubling.astype(jnp.bfloat16)
    counts_here = lax.dynamic_slice_in_dim(mode_counts, lax.axis_index("dp") * samples, samples, 0)
    keep_modes = (jnp.arange(MODES, dtype=jnp.int32)[None, :] < counts_here[:, None]).astype(
        jnp.float32
    )
    keep_wide = keep_modes[:, None, None, :]
    weight_short = spectral_weight.astype(jnp.bfloat16)
    group_low = lax.all_gather(weight_short, "dom", axis=0, tiled=True)
    weight_low = lax.all_gather(group_low, "dp", axis=0, tiled=True)
    weight_low = weight_low.reshape(2, MODES, channels, channels)
    weight_real = weight_low[0]
    weight_imag = weight_low[1]
    density_lines = send_pencils(density)
    real_part, imag_part = forward_parts(density_lines, cosines, sines)
    spec_real = real_part.astype(jnp.bfloat16)
    spec_imag = imag_part.astype(jnp.bfloat16)
    form = "slcf,fco->slof"
    mixed_real = jnp.einsum(
        form, spec_real, weight_real, preferred_element_type=jnp.float32
    ) - jnp.einsum(form, spec_imag, weight_imag, preferred_element_type=jnp.float32)
    mixed_imag = jnp.einsum(
        form, spec_imag, weight_real, preferred_element_type=jnp.float32
    ) + jnp.einsum(form, spec_real, weight_imag, preferred_element_type=jnp.float32)
    mixed_real = (mixed_real * keep_wide).astype(jnp.bfloat16) * doubling_low
    mixed_imag = (mixed_imag * keep_wide).astype(jnp.bfloat16) * doubling_low
    back_lines = inverse_cells(mixed_real, mixed_imag, cosines, sines)
    back_rows = send_slabs(back_lines)
    skip_part = jnp.einsum(
        "oc,scxl->soxl", skip_weight, density, preferred_element_type=jnp.float32
    )
    before = back_rows.astype(jnp.float32) + skip_part + skip_bias[None, :, None, None]
    gate_grad = (upstream.astype(jnp.float32) * gelu_slope(before)).astype(jnp.bfloat16)
    gate_lines = send_pencils(gate_grad)
    grad_real, grad_imag = forward_parts(gate_lines, cosines, sines)
    scale = keep_wide * doubling
    grad_real = (grad_real * scale).astype(jnp.bfloat16)
    grad_imag = (grad_imag * scale).astype(jnp.bfloat16)
    outer = "slof,slcf->fco"
    part_real = jnp.einsum(
        outer, grad_real, spec_real, preferred_element_type=jnp.float32
    ) + jnp.einsum(outer, grad_imag, spec_imag, preferred_element_type=jnp.float32)
    part_imag = jnp.einsum(
        outer, grad_imag, spec_real, preferred_element_type=jnp.float32
    ) - jnp.einsum(outer, grad_real, spec_imag, preferred_element_type=jnp.float32)
    grad_local = jnp.stack([part_real, part_imag], 0).reshape(2 * MODES * channels, channels)
    group_grad = lax.psum_scatter(
        grad_local.astype(jnp.bfloat16), "dp", scatter_dimension=0, tiled=True
    ).astype(jnp.float32)
    weight_grad = lax.psum_scatter(group_grad, "dom", scatter_dimension=0, tiled=True)
    inner = "fco,slof->slcf"
    input_real = jnp.einsum(
        inner, weight_real, grad_real, preferred_element_type=jnp.float32
    ) + jnp.einsum(inner, weight_imag, grad_imag, preferred_element_type=jnp.float32)
    input_imag = jnp.einsum(
        inner, weight_real, grad_imag, preferred_element_type=jnp.float32
    ) - jnp.einsum(inner, weight_imag, grad_real, preferred_element_type=jnp.float32)
    input_lines = inverse_cells(
        input_real.astype(jnp.bfloat16), input_imag.astype(jnp.bfloat16), cosines, sines
    )
    input_rows = send_slabs(input_lines)
    skip_back = jnp.einsum(
        "oc,soxl->scxl", skip_weight, gate_grad, preferred_element_type=jnp.float32
    )
    input_grad = (input_rows.astype(jnp.float32) + skip_back).astype(jnp.bfloat16)
    new_moment_one = beta_first * moment_one + (1.0 - beta_first) * weight_grad
    new_moment_two = beta_second * moment_two + (1.0 - beta_second) * weight_grad * weight_grad
    first_hat = new_moment_one / (1.0 - beta_first**STEP)
    second_hat = new_moment_two / (1.0 - beta_second**STEP)
    new_weight = spectral_weight - learn_rate * (
        first_hat / (jnp.sqrt(second_hat) + epsilon) + decay_rate * spectral_weight
    )
    return (input_grad, new_weight, new_moment_one, new_moment_two)


MESH = pl.DeviceIdType.MESH
ROWS = 8
STREAMS = 2
HALVES = 2
LANES = 128


def fixed_tables(halves, members, own, rows):
    cells = halves * members * rows
    freq = np.arange(MODES)[:, None]
    angles = 2.0 * np.pi * ((freq * np.arange(cells)[None, :]) % cells) / cells
    scaling = 1.0 / math.sqrt(cells)
    parts = np.stack([np.cos(angles) * scaling, -np.sin(angles) * scaling], 1)
    parts = parts.reshape(MODES, 2, halves, members, rows).transpose(2, 3, 4, 0, 1)
    parts = parts.reshape(halves, members, 1, rows, MODES, 2, 1)
    same = np.eye(own).reshape(1, 1, own, 1, 1, 1, own)
    transform = (parts * same).reshape(halves, members * own * rows, -1, LANES)
    transform = transform.transpose(0, 2, 1, 3)
    channels = members * own
    order = np.zeros((2, members, own, members, 2, own))
    for part in range(2):
        for device in range(members):
            for one in range(own):
                order[part, device, one, device, part, one] = 1.0
    order = order.reshape(2 * channels, 2 * channels)
    spread = np.repeat(np.eye(channels), rows, axis=0)
    low = lambda table: jnp.asarray(table.astype(np.float32), jnp.bfloat16)
    return low(transform), low(order), low(order.T), low(spread)


def dot(left, right, dims=((1,), (0,))):
    return lax.dot_general(left, right, (dims, ((), ())), preferred_element_type=jnp.float32)


def exact_dot(left, right):
    return jnp.dot(
        left, right, precision=lax.Precision.HIGHEST, preferred_element_type=jnp.float32
    )


def step_kernel(
    n,
    dens_hbm,
    upst_hbm,
    weight_hbm,
    skip_hbm,
    bias_hbm,
    counts,
    trans_back_hbm,
    order_hbm,
    order_back_hbm,
    spread_hbm,
    out_rows,
    out_skip,
    out_grad,
    dens,
    upst,
    weight,
    skip,
    bias,
    trans_back,
    order,
    order_back,
    spread,
    trans,
    a1r,
    a2s,
    a2r,
    b1s,
    b1r,
    b2s,
    b2r,
    c1s,
    c1r,
    c2s,
    c2r,
    d1s,
    d1r,
    d2s,
    skip_part,
    kept,
    wsend,
    wrecv,
    gsend,
    grecv,
    send_sem,
    recv_sem,
    block_sem,
    pair_send,
    pair_recv,
    load_sem,
    store_sem,
):
    me = lax.axis_index("dom")
    core = lax.axis_index("dp")
    low, wide = jnp.bfloat16, jnp.float32
    members = n // HALVES
    half, member = me // members, lax.rem(me, members)
    block = dens.shape[0] // members
    width = dens.shape[1] // STREAMS
    channels = weight.shape[0]

    loads = [
        pltpu.make_async_copy(source, target, load_sem.at[index])
        for index, (source, target) in enumerate(
            (
                (dens_hbm, dens),
                (weight_hbm, weight),
                (skip_hbm, skip),
                (spread_hbm, spread),
                (bias_hbm, bias),
                (order_hbm, order),
                (order_back_hbm, order_back),
                *(
                    (trans_back_hbm.at[half, tile], trans_back.at[:, pl.ds(tile * LANES, LANES)])
                    for tile in range(trans_back_hbm.shape[1])
                ),
                (upst_hbm, upst),
            )
        )
    ]
    for load in loads:
        load.start()

    barrier = pltpu.get_barrier_semaphore()

    def greet(shift, carry):
        pl.semaphore_signal(
            barrier, inc=1, device_id=(core, lax.rem(me + shift, n)), device_id_type=MESH
        )
        return carry

    lax.fori_loop(1, n, greet, 0)
    pl.semaphore_signal(barrier, inc=1, device_id=(1 - core, me), device_id_type=MESH)
    pl.semaphore_wait(barrier, n)
    loads[0].wait()

    def remote(stage, stream, peer, source, target, arrival=None):
        return pltpu.make_async_remote_copy(
            src_ref=source,
            dst_ref=target,
            send_sem=send_sem.at[stage, stream],
            recv_sem=recv_sem.at[stage, stream] if arrival is None else arrival,
            device_id=(core, peer),
            device_id_type=MESH,
        )

    def send_modes(stage, stream, source, target, slots):
        def one(shift, carry):
            peer = lax.rem(me + shift, n)
            remote(
                stage,
                stream,
                peer,
                source.at[stream, lax.rem(peer, slots)],
                target.at[stream, me],
            ).start()
            return carry

        lax.fori_loop(1, n, one, 0)
        target[stream, me] = source[stream, lax.rem(me, slots)]

    def near(step):
        return lax.rem(member + step, members)

    def send_blocks(stage, stream, source, target):
        def one(shift, carry):
            peer = near(shift)
            remote(
                stage,
                stream,
                half * members + peer,
                source.at[stream, peer],
                target.at[stream, member],
                block_sem.at[stream, shift],
            ).start()
            return carry

        lax.fori_loop(1, members, one, 0)

    def all_of(stage, stream, ref):
        blocks = ref.at[stream, pl.ds(0, ref.shape[1] - 1)]
        return remote(stage, stream, me, blocks, blocks)

    def lanes(stream):
        return pl.ds(stream * width, width)

    def rows(device):
        return pl.ds(pl.multiple_of(device * block, block), block)

    for stream in range(STREAMS):

        def start_one(shift, carry):
            peer = near(shift)
            remote(
                0,
                stream,
                half * members + peer,
                dens.at[rows(peer), lanes(stream)],
                a1r.at[stream, member],
            ).start()
            return carry

        lax.fori_loop(1, members, start_one, 0)
        a1r[stream, member] = dens[rows(member), lanes(stream)]

    loads[1].wait()
    own_low = weight[...].astype(low)
    wsend[...] = jnp.concatenate([own_low, own_low], axis=1)
    swap = pltpu.make_async_remote_copy(
        src_ref=wsend,
        dst_ref=wrecv,
        send_sem=pair_send.at[0],
        recv_sem=pair_recv.at[0],
        device_id=(1 - core, me),
        device_id_type=MESH,
    )
    swap.start()
    for load in loads[2:]:
        load.wait()

    size = dens.shape[0]

    def wide_map(dims):
        same_row = lax.rem(lax.broadcasted_iota(jnp.int32, (size, size), 0), ROWS) == lax.rem(
            lax.broadcasted_iota(jnp.int32, (size, size), 1), ROWS
        )
        tall = dot(spread[...], skip[...], dims).astype(low)
        full = dot(tall, spread[...], ((1,), (1,)))
        return jnp.where(same_row, full, 0.0).astype(low)

    trans[...] = trans_back[...].astype(wide).T.astype(low)
    forward_map = wide_map(((1,), (0,)))
    swap.wait_recv()
    mine = weight[...].astype(low).astype(wide)
    other = wrecv[...].astype(wide)[:, :channels]
    is_first = core == 0
    weight_real = jnp.where(is_first, mine, other)
    weight_imag = jnp.where(is_first, other, mine)
    mixer = jnp.concatenate(
        [
            jnp.concatenate([weight_real, weight_imag], axis=1),
            jnp.concatenate([-weight_imag, weight_real], axis=1),
        ],
        axis=0,
    )
    mixer = dot(dot(order_back[...], mixer.astype(low)).astype(low), order[...])
    mixer_back = mixer.T.astype(low)
    mixer = mixer.astype(low)
    keep = jnp.where(me < counts[core], 1.0, 0.0)
    scale = keep * jnp.where(me == 0, 1.0, 2.0)

    def blocks_of(values, count):
        return values.astype(low).reshape(count, values.shape[0] // count, values.shape[1])

    def flat(ref, stream):
        values = ref[stream]
        return values.reshape(values.shape[0] * values.shape[1], values.shape[2])

    def added(ref, stream):
        values = ref[stream].astype(wide)
        total = values[:members]
        for other in range(1, HALVES):
            total += values[other * members : (other + 1) * members]
        return total.reshape(members * values.shape[1], values.shape[2])

    for stream in range(STREAMS):
        all_of(0, stream, a1r).wait_recv()
        a2s[stream] = blocks_of(dot(trans[...], flat(a1r, stream)), n)
        send_modes(1, stream, a2s, a2r, n)
    bias_column = jnp.sum(spread[...].astype(wide) * bias[...], axis=1, keepdims=True)
    skip_part[...] = dot(forward_map, dens[...]) + bias_column
    for stream in range(STREAMS):
        all_of(1, stream, a2r).wait_recv()
        spectrum = added(a2r, stream).astype(low)
        kept[stream] = spectrum
        b1s[stream] = blocks_of(dot(mixer_back, spectrum) * scale, members)
        send_modes(2, stream, b1s, b1r, members)
    back_map = wide_map(((1,), (1,)))
    for stream in range(STREAMS):
        all_of(2, stream, b1r).wait_recv()
        b2s[stream] = blocks_of(dot(trans_back[...], flat(b1r, stream)), members)
        send_blocks(3, stream, b2s, b2r)
    for stream in range(STREAMS):

        def slope_block(device, cells):
            before = cells.astype(wide) + skip_part[rows(device), lanes(stream)]
            cotangent = upst[rows(device), lanes(stream)].astype(wide)
            c1s[stream, device] = (cotangent * gelu_slope(before)).astype(low)

        slope_block(member, b2s[stream, member])
        c1r[stream, member] = c1s[stream, member]

        def one_slope(step, carry):
            device = near(step)
            cells = b2r.at[stream, device]
            remote(
                3, stream, me, cells, cells, block_sem.at[stream, members - step]
            ).wait_recv()
            slope_block(device, cells[...])
            remote(
                4,
                stream,
                half * members + device,
                c1s.at[stream, device],
                c1r.at[stream, member],
            ).start()
            return carry

        lax.fori_loop(1, members, one_slope, 0)
    for stream in range(STREAMS):
        all_of(4, stream, c1r).wait_recv()
        c2s[stream] = blocks_of(dot(trans[...], flat(c1r, stream)), n)
        send_modes(5, stream, c2s, c2r, n)
    for stream in range(STREAMS):
        skip_part[:, lanes(stream)] = dot(back_map, flat(c1s, stream))
    skip_store = pltpu.make_async_copy(skip_part, out_skip, store_sem.at[0])
    skip_store.start()
    products = jnp.zeros((2 * channels, 2 * channels), wide)
    for stream in range(STREAMS):
        all_of(5, stream, c2r).wait_recv()
        gradient = (added(c2r, stream) * scale).astype(low)
        d1s[stream] = blocks_of(dot(mixer, gradient), members)
        send_modes(6, stream, d1s, d1r, members)
        products += dot(kept[stream], gradient, ((1,), (1,)))
    products = exact_dot(exact_dot(order[...].astype(wide), products), order_back[...].astype(wide))
    top, bottom = products[:channels], products[channels:]
    grad_real = top[:, :channels] + bottom[:, channels:]
    grad_imag = top[:, channels:] - bottom[:, :channels]
    theirs = jnp.where(is_first, grad_imag, grad_real)
    ours = jnp.where(is_first, grad_real, grad_imag)
    gsend[...] = jnp.concatenate([theirs, theirs], axis=1)
    swap_grad = pltpu.make_async_remote_copy(
        src_ref=gsend,
        dst_ref=grecv,
        send_sem=pair_send.at[1],
        recv_sem=pair_recv.at[1],
        device_id=(1 - core, me),
        device_id_type=MESH,
    )
    swap_grad.start()

    def own_store(stream):
        return pltpu.make_async_copy(
            d2s.at[stream, member],
            out_rows.at[rows(member), lanes(stream)],
            store_sem.at[1 + stream],
        )

    for stream in range(STREAMS):
        all_of(6, stream, d1r).wait_recv()
        d2s[stream] = blocks_of(dot(trans_back[...], flat(d1r, stream)), members)

        def send_last(shift, carry):
            peer = near(shift)
            remote(
                7,
                stream,
                half * members + peer,
                d2s.at[stream, peer],
                out_rows.at[rows(member), lanes(stream)],
            ).start()
            return carry

        lax.fori_loop(1, members, send_last, 0)
        own_store(stream).start()
    swap_grad.wait_recv()
    out_grad[...] = ours + grecv[...][:, :channels]
    swap.wait_send()
    swap_grad.wait_send()
    for stage, source in enumerate((a1r, a2r, b1r, b2r, c1r, c2r, d1r, d2s)):
        for stream in range(STREAMS):
            all_of(stage, stream, source).wait_send()
    skip_store.wait()
    for stream in range(STREAMS):
        own_store(stream).wait()
        all_of(7, stream, d2s).wait_recv()


def finish_kernel(
    rows_hbm,
    skip_hbm,
    grad_hbm,
    weight_hbm,
    first_hbm,
    second_hbm,
    out,
    new_weight,
    new_first,
    new_second,
    rows,
    skip,
    grad,
    weight,
    first,
    second,
    total,
    one,
    two,
    three,
    load_sem,
    store_sem,
):
    loads = [
        pltpu.make_async_copy(source, target, load_sem.at[index])
        for index, (source, target) in enumerate(
            (
                (grad_hbm, grad),
                (weight_hbm, weight),
                (first_hbm, first),
                (second_hbm, second),
                (rows_hbm, rows),
                (skip_hbm, skip),
            )
        )
    ]
    for load in loads:
        load.start()
    for load in loads[:4]:
        load.wait()
    one[...], two[...], three[...] = adam(grad[...], weight[...], first[...], second[...])
    stores = [
        pltpu.make_async_copy(source, target, store_sem.at[index])
        for index, (source, target) in enumerate(
            ((one, new_weight), (two, new_first), (three, new_second), (total, out))
        )
    ]
    for store in stores[:3]:
        store.start()
    for load in loads[4:]:
        load.wait()
    total[...] = (rows[...].astype(jnp.float32) + skip[...]).astype(total.dtype)
    stores[3].start()
    for store in stores:
        store.wait()


def one_frequency_each(
    n, density, upstream, spectral_weight, moment_one, moment_two, skip_weight, skip_bias, mode_counts
):
    samples, channels, slab_rows, line_count = density.shape
    members = n // HALVES
    own = channels // members
    width = line_count // STREAMS
    size = channels * slab_rows
    tables = fixed_tables(HALVES, members, own, slab_rows)
    low, wide = jnp.bfloat16, jnp.float32
    vmem = pl.BlockSpec(memory_space=pltpu.VMEM)
    hbm = pl.BlockSpec(memory_space=pltpu.HBM)
    cells = pltpu.VMEM((STREAMS, members, own * slab_rows, width), low)
    modes = pltpu.VMEM((STREAMS, n, 2 * own, width), low)
    mixed = pltpu.VMEM((STREAMS, members, 2 * own, width), low)
    arrays = (
        density.reshape(size, line_count),
        upstream.reshape(size, line_count),
        spectral_weight,
        skip_weight,
        skip_bias.reshape(1, channels),
    )
    input_rows, skip_back, weight_grad = pl.pallas_call(
        functools.partial(step_kernel, n),
        out_shape=(
            jax.ShapeDtypeStruct((size, line_count), low),
            jax.ShapeDtypeStruct((size, line_count), wide),
            jax.ShapeDtypeStruct((channels, channels), wide),
        ),
        in_specs=[hbm] * 5 + [pl.BlockSpec(memory_space=pltpu.SMEM)] + [hbm] * 4,
        out_specs=(hbm, hbm, vmem),
        scratch_shapes=[pltpu.VMEM(each.shape, each.dtype) for each in arrays]
        + [pltpu.VMEM((size, 2 * MODES * own), low)]
        + [pltpu.VMEM(each.shape, each.dtype) for each in tables[1:]]
        + [pltpu.VMEM((2 * MODES * own, size), low)]
        + [cells, modes, modes, mixed, modes, cells, cells]
        + [cells, cells, modes, modes, mixed, modes, cells]
        + [
            pltpu.VMEM((size, line_count), wide),
            pltpu.VMEM((STREAMS, 2 * channels, width), low),
            pltpu.VMEM((channels, 2 * channels), low),
            pltpu.VMEM((channels, 2 * channels), low),
            pltpu.VMEM((channels, 2 * channels), wide),
            pltpu.VMEM((channels, 2 * channels), wide),
            pltpu.SemaphoreType.DMA((8, STREAMS)),
            pltpu.SemaphoreType.DMA((8, STREAMS)),
            pltpu.SemaphoreType.DMA((STREAMS, members)),
            pltpu.SemaphoreType.DMA((2,)),
            pltpu.SemaphoreType.DMA((2,)),
            pltpu.SemaphoreType.DMA((8 + tables[0].shape[1],)),
            pltpu.SemaphoreType.DMA((1 + STREAMS,)),
        ],
        compiler_params=pltpu.CompilerParams(
            collective_id=0, has_side_effects=True, vmem_limit_bytes=60 * 1024 * 1024
        ),
        cost_estimate=pl.CostEstimate(
            flops=1_000_000_000, bytes_accessed=2_000_000, transcendentals=300_000
        ),
    )(*arrays, mode_counts, *tables)
    square = jax.ShapeDtypeStruct((channels, channels), wide)
    input_grad, *updated = pl.pallas_call(
        finish_kernel,
        out_shape=(jax.ShapeDtypeStruct((size, line_count), low), square, square, square),
        in_specs=[hbm] * 6,
        out_specs=(hbm,) * 4,
        scratch_shapes=[
            pltpu.VMEM((size, line_count), low),
            pltpu.VMEM((size, line_count), wide),
            *[pltpu.VMEM((channels, channels), wide)] * 4,
            pltpu.VMEM((size, line_count), low),
            *[pltpu.VMEM((channels, channels), wide)] * 3,
            pltpu.SemaphoreType.DMA((6,)),
            pltpu.SemaphoreType.DMA((4,)),
        ],
        compiler_params=pltpu.CompilerParams(vmem_limit_bytes=60 * 1024 * 1024),
        cost_estimate=pl.CostEstimate(flops=300_000, bytes_accessed=1_200_000, transcendentals=0),
    )(input_rows, skip_back, weight_grad, spectral_weight, moment_one, moment_two)
    return (input_grad.reshape(density.shape), *updated)


def adam(weight_grad, spectral_weight, moment_one, moment_two):
    new_moment_one = beta_first * moment_one + (1.0 - beta_first) * weight_grad
    new_moment_two = beta_second * moment_two + (1.0 - beta_second) * weight_grad * weight_grad
    first_hat = new_moment_one / (1.0 - beta_first**STEP)
    second_hat = new_moment_two / (1.0 - beta_second**STEP)
    new_weight = spectral_weight - learn_rate * (
        first_hat / (jnp.sqrt(second_hat) + epsilon) + decay_rate * spectral_weight
    )
    return (new_weight, new_moment_one, new_moment_two)


def on_mesh(density, *others):
    samples, channels, slab_rows, line_count = density.shape
    n, groups = lax.axis_size("dom"), lax.axis_size("dp")
    fits = (
        n == MODES
        and groups == 2
        and samples == 1
        and slab_rows == ROWS
        and n % HALVES == 0
        and 2 * (channels // (n // HALVES)) == 16
        and line_count % (128 * STREAMS) == 0
    )
    if fits:
        return one_frequency_each(n, density, *others)
    return on_device(density, *others)


def solution(mesh):
    placed = (
        P("dp", None, "dom", None),
        P("dp", None, "dom", None),
        P(("dp", "dom"), None),
        P(("dp", "dom"), None),
        P(("dp", "dom"), None),
        P(),
        P(),
        P(),
    )
    return jax.shard_map(
        on_mesh,
        mesh=mesh,
        in_specs=placed,
        out_specs=(
            P("dp", None, "dom", None),
            P(("dp", "dom"), None),
            P(("dp", "dom"), None),
            P(("dp", "dom"), None),
        ),
        check_vma=False,
    )
```
